32 devices in a mesh: dp: 8 (over z, x), mp: 4 (over y, core).
Axes of the slice: x: 2, y: 2, z: 4, core: 2. Of those that a mesh axis runs over, the one named last changes fastest.
Arguments:
- text_tokens: bfloat16 [32, 64, 768], P('dp'), may hold values from -6 to 6
- image_tokens: bfloat16 [32, 576, 768], P('dp'), may hold values from -6 to 6
- text_lengths: int32 [32], P('dp'), may hold values from 8 to 64, as said below
- patch_counts: int32 [32], P('dp'), may hold values from 196 to 576, as said below
- self_qkv: bfloat16 [3, 768, 768], P(None, 'dp', 'mp'), may hold values from -0.21875 to 0.21875
- self_out: bfloat16 [768, 768], P('mp', 'dp'), may hold values from -0.625 to 0.625
- cross_query: bfloat16 [768, 768], P('dp', 'mp'), may hold values from -0.21875 to 0.21875
- cross_keyval: bfloat16 [2, 768, 768], P(None, 'dp', 'mp'), may hold values from -0.21875 to 0.21875
- cross_out: bfloat16 [768, 768], P('mp', 'dp'), may hold values from -0.875 to 0.875
- mlp_up: bfloat16 [768, 3072], P('dp', 'mp'), may hold values from -0.21875 to 0.21875
- mlp_down: bfloat16 [3072, 768], P('mp', 'dp'), may hold values from -0.15625 to 0.15625
- norm_gain: float32 [3, 768], replicated, may hold values from 0.25 to 1.75
- norm_bias: float32 [3, 768], replicated, may hold values from -4 to 4
- out_bias: float32 [3, 768], replicated, may hold values from -4 to 4
- up_bias: float32 [3072], P('mp'), may hold values from -4 to 4
- out_grad: bfloat16 [32, 64, 768], P('dp'), may hold values from -6 to 6
Outputs:
- layer_out: bfloat16 [32, 64, 768], P('dp')
- text_grad: float32 [32, 64, 768], P('dp')
- image_grad: float32 [32, 576, 768], P('dp', None, 'mp')
- self_qkv_grad: float32 [3, 768, 768], P(None, 'dp', 'mp')
- self_out_grad: float32 [768, 768], P('mp', 'dp')
- cross_query_grad: float32 [768, 768], P('dp', 'mp')
- cross_keyval_grad: float32 [2, 768, 768], P(None, 'dp', 'mp')
- cross_out_grad: float32 [768, 768], P('mp', 'dp')
- mlp_up_grad: float32 [768, 3072], P('dp', 'mp')
- mlp_down_grad: float32 [3072, 768], P('mp', 'dp')
- norm_gain_grad: float32 [3, 768], replicated
- norm_bias_grad: float32 [3, 768], replicated
- out_bias_grad: float32 [3, 768], replicated
- up_bias_grad: float32 [3072], P('mp')
The draws below stay inside these ranges and needn't reach their ends.
Inputs may be any that keep to these rules, and one draw needn't show every extreme that they name: Caption b holds text_lengths[b] real tokens at its first positions; keys past them are padding. Image b has patch_counts[b] valid tokens at its first positions, either 196 or 576.
All inputs are finite; a program needn't handle non-finite values.
Results may differ from the reference program's by a relative error of at most 0.018.
Values may be sent and summed in bfloat16 or wider, within the bound.
No kernel may reach another device: no remote copies, remote signals or barrier semaphores. Data moves between devices by JAX's collectives and lax.ppermute only.
A program may use at most 128 MiB of HBM per device.

```python
from functools import partial
import jax
import jax.numpy as jnp
from jax import lax

D = 768
HEADS = 12
HEAD_DIM = 64
FF = 3072
CAP_LEN = 64
PATCHES = 576
PATCHES_FEW = 196
SEQ_DEV = 4
CAPTIONS = 32


def draw_text_lengths(key, part):
    lengths_drawn = jax.random.randint(key, (CAPTIONS,), CAP_LEN // 8, CAP_LEN + 1, dtype=jnp.int32)
    return lengths_drawn.at[0].set(CAP_LEN).at[1].set(CAP_LEN // 8)


def draw_patch_counts(key, part):
    chosen = jax.random.randint(key, (CAPTIONS,), 0, 2, dtype=jnp.int32)
    counts = PATCHES_FEW + (PATCHES - PATCHES_FEW) * chosen
    return counts.at[0].set(PATCHES).at[1].set(PATCHES_FEW)


def steps_of(key, dims, shards, least, high):
    loudness = 1.0
    for dim, parts in shards:
        heights = jax.random.uniform(jax.random.fold_in(jax.random.fold_in(key, 6), dim), (parts,), jnp.float32, least / len(shards), high / len(shards))
        loudness = loudness * jnp.repeat(jnp.exp(heights), dims[dim] // parts).reshape((-1,) + (1,) * (len(dims) - 1 - dim))
    return loudness


def bell_draw(stream_key, extent, deviation, limit, split=(), kind=jnp.bfloat16):
    level = steps_of(stream_key, extent, split, -0.22, 0.18) if split else 1.0
    values = jax.random.normal(stream_key, extent, jnp.float32) * deviation * level
    return jnp.minimum(jnp.maximum(values, -limit), limit).astype(kind)


def setup_inputs(seed: int = 0) -> dict:
    splits = jax.random.split(jax.random.key(seed), 17)
    text_tokens = bell_draw(splits[0], (CAPTIONS, CAP_LEN, D), 1.0, 6.0, ((0, 8),))
    image_tokens = bell_draw(splits[1], (CAPTIONS, PATCHES, D), 1.0, 6.0, ((0, 8),))
    text_lengths = draw_text_lengths(jax.random.fold_in(splits[16], 71), 0)
    patch_counts = draw_patch_counts(jax.random.fold_in(splits[16], 71), 0)
    self_qkv = bell_draw(splits[4], (3, D, D), D ** -0.5, 0.21875, ((1, 8), (2, 4)))
    self_out = bell_draw(splits[5], (D, D), (D // 8) ** -0.5, 0.625, ((0, 4), (1, 8)))
    cross_query = bell_draw(splits[6], (D, D), D ** -0.5, 0.21875, ((0, 8), (1, 4)))
    cross_keyval = bell_draw(splits[7], (2, D, D), D ** -0.5, 0.21875, ((1, 8), (2, 4)))
    cross_out = bell_draw(splits[8], (D, D), (D // 16) ** -0.5, 0.875, ((0, 4), (1, 8)))
    mlp_up = bell_draw(splits[9], (D, FF), D ** -0.5, 0.21875, ((0, 8), (1, 4)))
    mlp_down = bell_draw(splits[10], (FF, D), (FF // 2) ** -0.5, 0.15625, ((0, 4), (1, 8)))
    norm_gain = jnp.clip(1.0 + 0.15 * jax.random.normal(splits[11], (3, D), jnp.float32), 0.25, 1.75)
    norm_bias = bell_draw(splits[12], (3, D), 0.3, 4.0, (), jnp.float32)
    out_bias = bell_draw(splits[13], (3, D), 0.3, 4.0, (), jnp.float32)
    up_bias = bell_draw(splits[14], (FF,), 0.3, 4.0, ((0, 4),), jnp.float32)
    out_grad = bell_draw(splits[15], (CAPTIONS, CAP_LEN, D), 1.0, 6.0, ((0, 8),))
    return dict(text_tokens=text_tokens, image_tokens=image_tokens, text_lengths=text_lengths, patch_counts=patch_counts, self_qkv=self_qkv, self_out=self_out, cross_query=cross_query, cross_keyval=cross_keyval, cross_out=cross_out, mlp_up=mlp_up, mlp_down=mlp_down, norm_gain=norm_gain, norm_bias=norm_bias, out_bias=out_bias, up_bias=up_bias, out_grad=out_grad)


@jax.custom_vjp
def low(v):
    return lax.optimization_barrier(v.astype(jnp.bfloat16)).astype(jnp.float32)

@jax.custom_vjp
def low_back(v):
    return v

def low_keep(v):
    return (low(v), None)

def low_pass(kept, grad):
    return (grad,)

def back_keep(v):
    return (v, None)

def back_low(kept, grad):
    return (low(grad),)
low.defvjp(low_keep, low_pass)
low_back.defvjp(back_keep, back_low)
PRECISE = lax.Precision.HIGHEST

def layer_norm(values, gain_row, shift_row):
    center = lax.optimization_barrier(jnp.mean(values, axis=-1, keepdims=True))
    centered = values - center
    variance = lax.optimization_barrier(jnp.mean(centered * centered, axis=-1, keepdims=True))
    return centered * lax.rsqrt(variance + 1e-05) * gain_row + shift_row

def matmul_high(left, right):
    return jnp.matmul(left, right, precision=PRECISE)

def attention(queries, key_heads, value_heads, allowed):
    score_scale = HEAD_DIM ** (-0.5)
    raw_scores = jnp.einsum('bqhe,bkhe->bhqk', queries, key_heads, precision=PRECISE) * score_scale
    scores = jnp.where(allowed[:, None], low_back(raw_scores), -1e+30)
    probability = jax.nn.softmax(scores, axis=-1)
    context = jnp.einsum('bhqk,bkhe->bqhe', low(probability), value_heads, precision=PRECISE)
    return low(low_back(context))

def forward(self_allowed, cross_allowed, stream_in, image_in, self_qkv, self_out, cross_query, cross_keyval, cross_out, mlp_up, mlp_down, norm_gain, norm_bias, out_bias, up_bias):
    seq_count = stream_in.shape[0]
    row_count = seq_count * CAP_LEN
    flat_text = stream_in.reshape(row_count, D)
    normed_text = low(layer_norm(flat_text, norm_gain[0], norm_bias[0]))
    projected = low(low_back(jnp.einsum('td,jdc->jtc', normed_text, self_qkv, precision=PRECISE)))
    heads_text = projected.reshape(3, seq_count, CAP_LEN, HEADS, HEAD_DIM)
    self_ctx = attention(heads_text[0], heads_text[1], heads_text[2], self_allowed).reshape(row_count, D)
    hidden_one = flat_text + low_back(matmul_high(self_ctx, self_out)) + out_bias[0]
    normed_mid = low(layer_norm(hidden_one, norm_gain[1], norm_bias[1]))
    cross_q = low(low_back(matmul_high(normed_mid, cross_query))).reshape(seq_count, CAP_LEN, HEADS, HEAD_DIM)
    image_flat = image_in.reshape(seq_count * PATCHES, D)
    keyval = low(low_back(jnp.einsum('td,jdc->jtc', image_flat, cross_keyval, precision=PRECISE)))
    keyval = keyval.reshape(2, seq_count, PATCHES, HEADS, HEAD_DIM)
    cross_ctx = attention(cross_q, keyval[0], keyval[1], cross_allowed).reshape(row_count, D)
    hidden_two = hidden_one + low_back(matmul_high(cross_ctx, cross_out)) + out_bias[1]
    normed_ffn = low(layer_norm(hidden_two, norm_gain[2], norm_bias[2]))
    pre_act = low_back(matmul_high(normed_ffn, mlp_up)) + up_bias
    activation = low(jax.nn.gelu(pre_act, approximate=False))
    result = hidden_two + low_back(matmul_high(activation, mlp_down)) + out_bias[2]
    return result.reshape(seq_count, CAP_LEN, D)

def reference(text_tokens, image_tokens, text_lengths, patch_counts, self_qkv, self_out, cross_query, cross_keyval, cross_out, mlp_up, mlp_down, norm_gain, norm_bias, out_bias, up_bias, out_grad):
    group_count = CAPTIONS // SEQ_DEV
    params = tuple((weight.astype(jnp.float32) for weight in (self_qkv, self_out, cross_query, cross_keyval, cross_out, mlp_up, mlp_down, norm_gain, norm_bias, out_bias, up_bias)))
    position = jnp.arange(CAP_LEN)
    patch_index = jnp.arange(PATCHES)

    def regroup(array):
        return array.reshape((group_count, SEQ_DEV) + array.shape[1:])

    def one_group(totals, batch_part):
        text_part, image_part, length_part, count_part, cot_part = batch_part
        key_live = position[None, :] < length_part[:, None]
        self_allowed = (position[:, None] >= position[None, :])[None] & key_live[:, None, :]
        cross_allowed = (patch_index[None, :] < count_part[:, None])[:, None, :]
        fixed = partial(forward, self_allowed, cross_allowed)
        primal, pullback = jax.vjp(fixed, text_part.astype(jnp.float32), image_part.astype(jnp.float32), *params)
        grads = pullback(cot_part.astype(jnp.float32))
        new_totals = tuple((total_part + new_part for total_part, new_part in zip(totals, grads[2:])))
        return (new_totals, (primal.astype(jnp.bfloat16), grads[0], grads[1]))
    start_totals = tuple((jnp.zeros(param.shape, jnp.float32) for param in params))
    totals, stacked = lax.scan(one_group, start_totals, (regroup(text_tokens), regroup(image_tokens), regroup(text_lengths), regroup(patch_counts), regroup(out_grad)))
    layer_out = stacked[0].reshape(CAPTIONS, CAP_LEN, D)
    text_grad = stacked[1].reshape(CAPTIONS, CAP_LEN, D)
    image_grad = stacked[2].reshape(CAPTIONS, PATCHES, D)
    return (layer_out, text_grad, image_grad, totals[0], totals[1], totals[2], totals[3], totals[4], totals[5], totals[6], totals[7], totals[8], totals[9], totals[10])
```

```python
import functools
import math

import jax
import jax.numpy as jnp
from jax import lax
from jax.experimental import pallas as pl
from jax.experimental.pallas import tpu as pltpu
from jax.sharding import PartitionSpec as P

BF = jnp.bfloat16
F32 = jnp.float32
HEAD_DIM = 64
SCALE = HEAD_DIM ** (-0.5)
NORM_EPS = 1e-05
NEG_FILL = -1e30
INV_ROOT_TWO = 1.0 / math.sqrt(2.0)
INV_ROOT_TAU = 1.0 / math.sqrt(2.0 * math.pi)
VMEM_LIMIT = 40 * 1024 * 1024


def nn(a, b):
    return lax.dot_general(a, b, (((1,), (0,)), ((), ())), preferred_element_type=F32)


def nt(a, b):
    return lax.dot_general(a, b, (((1,), (1,)), ((), ())), preferred_element_type=F32)


def tn(a, b):
    return lax.dot_general(a, b, (((0,), (0,)), ((), ())), preferred_element_type=F32)


def norm_parts(values):
    centered = values - jnp.mean(values, axis=-1, keepdims=True)
    inv_std = lax.rsqrt(jnp.mean(centered * centered, axis=-1, keepdims=True) + NORM_EPS)
    return centered * inv_std, inv_std


def norm_back(grad, normed, inv_std, gain_row):
    scaled = grad * gain_row
    first = jnp.mean(scaled, axis=-1, keepdims=True)
    second = jnp.mean(scaled * normed, axis=-1, keepdims=True)
    return inv_std * (scaled - first - normed * second)


def head_masks(width, kind):
    column = lax.broadcasted_iota(jnp.int32, (1, width), 1) // HEAD_DIM
    return [(column == h).astype(F32).astype(kind) for h in range(width // HEAD_DIM)]


def stack_heads(rows, masks):
    return jnp.concatenate([rows * m for m in masks], axis=0)


def unstack_heads(stacked, masks):
    count = stacked.shape[0] // len(masks)
    total = stacked[:count] * masks[0]
    for h in range(1, len(masks)):
        total = total + stacked[h * count : (h + 1) * count] * masks[h]
    return total


def call(body, name, outs, scalars, arrays, scratch=(), flops=0):
    nbytes = sum(a.size * a.dtype.itemsize for a in arrays)
    nbytes += sum(math.prod(s) * jnp.dtype(d).itemsize for s, d in outs)
    return pl.pallas_call(
        body,
        out_shape=[jax.ShapeDtypeStruct(s, d) for s, d in outs],
        in_specs=[pl.BlockSpec(memory_space=pltpu.SMEM)] * len(scalars)
        + [pl.BlockSpec(memory_space=pltpu.VMEM)] * len(arrays),
        out_specs=[pl.BlockSpec(memory_space=pltpu.VMEM)] * len(outs),
        scratch_shapes=list(scratch),
        compiler_params=pltpu.CompilerParams(vmem_limit_bytes=VMEM_LIMIT),
        cost_estimate=pl.CostEstimate(flops=flops, bytes_accessed=nbytes, transcendentals=0),
        name=name,
    )(*scalars, *arrays)


def block_rows(tab, k, height):
    return pl.ds(pl.multiple_of(tab[k], 32), height)


def place_pieces(tab, pieces, targets):
    height = pieces[0].shape[0]
    for k, piece in enumerate(pieces):
        rows = block_rows(tab, k, height) if len(pieces) > 1 else slice(None)
        start = 0
        for target in targets:
            width = target.shape[1]
            target[rows, :] = piece[:, start : start + width]
            start += width


def join_halves(tab, own, other, target):
    half = own.shape[0]
    target[pl.ds(pl.multiple_of(tab[8], 32), half), :] = own[...]
    target[pl.ds(pl.multiple_of(tab[9], 32), half), :] = other[...]


def split_halves(tab, full, send, keep):
    half = send.shape[0]
    keep[...] = full[pl.ds(pl.multiple_of(tab[8], 32), half), :].astype(keep.dtype)
    send[...] = full[pl.ds(pl.multiple_of(tab[9], 32), half), :].astype(send.dtype)


def pack_self_kernel(qkv, out, packed):
    width = qkv.shape[2]
    for j in range(3):
        packed[:, j * width : (j + 1) * width] = qkv[j]
    packed[:, 3 * width :] = out[...].astype(F32).T.astype(BF)


def pack_rest_kernel(query, keyval, out, up, down, cross, ffn):
    width = query.shape[1]
    cross[:, :width] = query[...]
    cross[:, width : 2 * width] = keyval[0]
    cross[:, 2 * width : 3 * width] = keyval[1]
    cross[:, 3 * width :] = out[...].astype(F32).T.astype(BF)
    hidden = up.shape[1]
    ffn[:, :hidden] = up[...]
    ffn[:, hidden:] = down[...].astype(F32).T.astype(BF)


def self_forward_kernel(count, seqs, tab, lens, text, gain, bias, *refs):
    pieces, (wq, wk, wv, wo, normed, q, k, v, prob, ctx, send, keep, full) = (
        refs[:count],
        refs[count:],
    )
    place_pieces(tab, pieces, (wq, wk, wv, wo))
    n, _ = norm_parts(text[...].astype(F32))
    low = (n * gain[0:1] + bias[0:1]).astype(BF)
    normed[...] = low
    for w, target in ((wq, q), (wk, k), (wv, v)):
        target[...] = nn(low, w[...]).astype(BF)
    width = q.shape[1]
    low_masks, masks = head_masks(width, BF), head_masks(width, F32)
    rows = text.shape[0] // seqs
    stacked = rows * len(masks)
    query_at = lax.broadcasted_iota(jnp.int32, (stacked, rows), 0) % rows
    key_at = lax.broadcasted_iota(jnp.int32, (stacked, rows), 1)
    for b in range(seqs):
        at = slice(b * rows, (b + 1) * rows)
        scores = nt(stack_heads(q[at], low_masks), k[at]) * SCALE
        allowed = (key_at <= query_at) & (key_at < lens[b])
        scores = jnp.where(allowed, scores, NEG_FILL)
        raised = jnp.exp(scores - jnp.max(scores, axis=-1, keepdims=True))
        p = raised / jnp.sum(raised, axis=-1, keepdims=True)
        prob[b] = p
        ctx[at] = unstack_heads(nn(p.astype(BF), v[at]), masks).astype(BF)
    full[...] = nt(ctx[...], wo[...])
    split_halves(tab, full, send, keep)


def keyval_kernel(count, tab, image, *refs):
    pieces, (wq, wk, wv, wo, keys, values) = refs[:count], refs[count:]

    @pl.when(pl.program_id(0) == 0)
    def _():
        place_pieces(tab, pieces, (wq, wk, wv, wo))

    keys[...] = nn(image[...], wk[...]).astype(BF)
    values[...] = nn(image[...], wv[...]).astype(BF)


def norm_kernel(index, sliced, tab, chip, other, resid, out_bias, gain, bias, hidden, normed):
    half = chip.shape[0]
    if sliced:
        base = resid[pl.ds(pl.multiple_of(tab[8], 32), half), :].astype(F32)
    else:
        base = resid[...]
    value = (
        base
        + (chip[...].astype(F32) + other[...].astype(F32))
        + out_bias[index : index + 1]
    )
    hidden[...] = value
    n, _ = norm_parts(value)
    normed[...] = (n * gain[index + 1 : index + 2] + bias[index + 1 : index + 2]).astype(BF)


def cross_forward_kernel(
    seqs, tab, counts, own, other, wq, wo, keys, values, normed, q, prob, ctx, send, keep, full
):
    join_halves(tab, own, other, normed)
    q[...] = nn(normed[...], wq[...]).astype(BF)
    width = q.shape[1]
    low_masks, masks = head_masks(width, BF), head_masks(width, F32)
    rows = normed.shape[0] // seqs
    patches = keys.shape[0] // seqs
    patch_at = lax.broadcasted_iota(jnp.int32, (rows * len(masks), patches), 1)
    for b in range(seqs):
        at = slice(b * rows, (b + 1) * rows)
        ks = slice(b * patches, (b + 1) * patches)
        scores = nt(stack_heads(q[at], low_masks), keys[ks]) * SCALE
        scores = jnp.where(patch_at < counts[b], scores, NEG_FILL)
        raised = jnp.exp(scores - jnp.max(scores, axis=-1, keepdims=True))
        p = raised / jnp.sum(raised, axis=-1, keepdims=True)
        prob[b] = p
        ctx[at] = unstack_heads(nn(p.astype(BF), values[ks]), masks).astype(BF)
    full[...] = nt(ctx[...], wo[...])
    split_halves(tab, full, send, keep)


def ffn_ready_kernel(count, tab, grad, *refs):
    pieces, (up, down, grad_act) = refs[:count], refs[count:]
    place_pieces(tab, pieces, (up, down))
    grad_act[...] = nn(grad[...], down[...])


def ffn_kernel(
    tab, own, other, up, down, grad_act, up_bias,
    normed, act, grad_low, bias_sum, send, keep, out_send, out_keep, full,
):
    join_halves(tab, own, other, normed)
    pre = nn(normed[...], up[...]) + up_bias[...]
    cdf = 0.5 * (1.0 + lax.erf(pre * INV_ROOT_TWO))
    density = jnp.exp(-0.5 * pre * pre) * INV_ROOT_TAU
    grad_pre = grad_act[...] * (cdf + pre * density)
    grad_low[...] = grad_pre.astype(BF)
    act[...] = (pre * cdf).astype(BF)
    bias_sum[...] = jnp.sum(grad_pre, axis=0, keepdims=True)
    full[...] = nt(grad_low[...], up[...])
    split_halves(tab, full, send, keep)
    full[...] = nt(act[...], down[...])
    split_halves(tab, full, out_send, out_keep)


def scatter_blocks(tab, matrix, column, outs):
    blocks = sum(o.shape[0] for o in outs)
    height = outs[0].shape[1]
    width = matrix.shape[1]
    for k in range(blocks):
        rows = block_rows(tab, k, height) if blocks > 1 else slice(None)
        target = outs[k // outs[0].shape[0]]
        target[k % outs[0].shape[0], :, column : column + width] = matrix[rows, :].astype(BF)


def ffn_weight_kernel(parts, tab, normed, grad_low, grad, act, *refs):
    outs, full = refs[:parts], refs[parts]
    full[...] = tn(normed[...], grad_low[...])
    scatter_blocks(tab, full, 0, outs)
    full[...] = tn(grad[...], act[...])
    scatter_blocks(tab, full, full.shape[1], outs)


def norm_back_kernel(index, sliced, tab, chip, other, hidden, resid, gain, total, low, vec):
    half = chip.shape[0]
    if sliced:
        base = resid[pl.ds(pl.multiple_of(tab[8], 32), half), :].astype(F32)
    else:
        base = resid[...]
    grad = chip[...].astype(F32) + other[...].astype(F32)
    n, inv_std = norm_parts(hidden[...])
    value = base + norm_back(grad, n, inv_std, gain[index : index + 1])
    total[...] = value
    low[...] = value.astype(BF)
    vec[...] = jnp.zeros_like(vec)
    vec[0:1] = 0.5 * jnp.sum(grad * n, axis=0, keepdims=True)
    vec[1:2] = 0.5 * jnp.sum(grad, axis=0, keepdims=True)
    vec[2:3] = 0.5 * jnp.sum(value, axis=0, keepdims=True)
    if sliced:
        vec[3:4] = 0.5 * jnp.sum(base, axis=0, keepdims=True)


def attention_back(p, q_stack, keys, values, grad_stack):
    grad_p = nt(grad_stack, values)
    inner = jnp.sum(p * grad_p, axis=-1, keepdims=True)
    ds = (p * (grad_p - inner)).astype(BF)
    return (
        nn(ds, keys) * SCALE,
        (tn(ds, q_stack) * SCALE).astype(BF),
        tn(p.astype(BF), grad_stack).astype(BF),
    )


def cross_back_kernel(
    seqs, tab, own, other, wq, wo, keys, values, q, prob, grad_two, dq, dk, dv, send, keep, full
):
    join_halves(tab, own, other, grad_two)
    grad_ctx = nn(grad_two[...], wo[...]).astype(BF)
    width = q.shape[1]
    low_masks, masks = head_masks(width, BF), head_masks(width, F32)
    rows = q.shape[0] // seqs
    patches = keys.shape[0] // seqs
    for b in range(seqs):
        at = slice(b * rows, (b + 1) * rows)
        ks = slice(b * patches, (b + 1) * patches)
        gq, gk, gv = attention_back(
            prob[b],
            stack_heads(q[at], low_masks),
            keys[ks],
            values[ks],
            stack_heads(grad_ctx[at], low_masks),
        )
        dq[at] = unstack_heads(gq, masks).astype(BF)
        dk[ks] = gk
        dv[ks] = gv
    full[...] = nt(dq[...], wq[...])
    split_halves(tab, full, send, keep)


def cross_weight_kernel(parts, tab, image, dk, dv, normed, dq, grad_two, ctx, *refs):
    outs, (acc_k, acc_v) = refs[:parts], refs[parts:]
    step = pl.program_id(0)

    @pl.when(step == 0)
    def _():
        acc_k[...] = tn(normed[...], dq[...])
        acc_v[...] = tn(grad_two[...], ctx[...])
        width = acc_k.shape[1]
        scatter_blocks(tab, acc_k, 0, outs)
        scatter_blocks(tab, acc_v, 3 * width, outs)
        acc_k[...] = jnp.zeros_like(acc_k)
        acc_v[...] = jnp.zeros_like(acc_v)

    acc_k[...] += tn(image[...], dk[...])
    acc_v[...] += tn(image[...], dv[...])

    @pl.when(step == pl.num_programs(0) - 1)
    def _():
        width = acc_k.shape[1]
        scatter_blocks(tab, acc_k, width, outs)
        scatter_blocks(tab, acc_v, 2 * width, outs)


def image_part_kernel(tab, dk, dv, wk, wv, send, keep):
    width = wk.shape[1]
    for target, first in ((keep, 10), (send, 12)):
        for j in range(2):
            rows = pl.ds(pl.multiple_of(tab[first + j], 64), width)
            part = nt(dk[...], wk[rows, :]) + nt(dv[...], wv[rows, :])
            target[:, j * width : (j + 1) * width] = part.astype(BF)


def image_chip_kernel(keep, other, own, send):
    total = keep[...].astype(F32) + other[...].astype(F32)
    width = own.shape[1]
    half = send.shape[0]
    own[...] = total[:, :width].astype(BF)
    away = total[:, width:]
    send[:, :width] = away[:half].astype(BF)
    send[:, width:] = away[half:].astype(BF)


def image_sum_kernel(own, other, out):
    half = other.shape[0]
    width = own.shape[1]
    out[:half] = own[:half].astype(F32) + other[:, :width].astype(F32)
    out[half:] = own[half:].astype(F32) + other[:, width:].astype(F32)


def self_back_kernel(
    seqs, parts, tab, own, other, text, gain, normed, wq, wk, wv, wo, q, k, v, prob, ctx, *refs
):
    outs = refs[:parts]
    send, keep, vec, low, dq, dk, dv, full, narrow = refs[parts:]
    join_halves(tab, own, other, low)
    grad_ctx = nn(low[...], wo[...]).astype(BF)
    width = q.shape[1]
    low_masks, masks = head_masks(width, BF), head_masks(width, F32)
    rows = q.shape[0] // seqs
    for b in range(seqs):
        at = slice(b * rows, (b + 1) * rows)
        gq, gk, gv = attention_back(
            prob[b],
            stack_heads(q[at], low_masks),
            k[at],
            v[at],
            stack_heads(grad_ctx[at], low_masks),
        )
        dq[at] = unstack_heads(gq, masks).astype(BF)
        dk[at] = gk
        dv[at] = gv
    for j, (left, right) in enumerate(((normed, dq), (normed, dk), (normed, dv), (low, ctx))):
        narrow[...] = tn(left[...], right[...])
        scatter_blocks(tab, narrow, j * width, outs)
    full[...] = nt(dq[...], wq[...]) + nt(dk[...], wk[...]) + nt(dv[...], wv[...])
    split_halves(tab, full, send, keep)
    n, _ = norm_parts(text[...].astype(F32))
    part = full[...]
    vec[...] = jnp.zeros_like(vec)
    vec[0:1] = jnp.sum(part * n, axis=0, keepdims=True)
    vec[1:2] = jnp.sum(part, axis=0, keepdims=True)


def text_grad_kernel(tab, chip, other, text, resid, gain, out):
    half = chip.shape[0]
    grad = chip[...].astype(F32) + other[...].astype(F32)
    base = text[pl.ds(pl.multiple_of(tab[8], 32), half), :].astype(F32)
    n, inv_std = norm_parts(base)
    out[...] = resid[...] + norm_back(grad, n, inv_std, gain[0:1])


def layer_out_kernel(chip, other, hidden, out_bias, out):
    out[...] = (
        hidden[...] + (chip[...].astype(F32) + other[...].astype(F32)) + out_bias[2:3]
    ).astype(BF)


def join_kernel(tab, own, other, out):
    join_halves(tab, own, other, out)


def add_kernel(keep, other, *outs):
    for k, out in enumerate(outs):
        out[...] = (keep[k].astype(F32) + other[k].astype(F32)).astype(BF)


def sum_pieces(refs):
    total = refs[0][...].astype(F32)
    for ref in refs[1:]:
        total = total + ref[...].astype(F32)
    return total


def close_self_kernel(count, *refs):
    pieces, (qkv, out) = refs[:count], refs[count:]
    total = sum_pieces(pieces)
    width = qkv.shape[2]
    for j in range(3):
        qkv[j] = total[:, j * width : (j + 1) * width]
    out[...] = total[:, 3 * width :].T


def close_cross_kernel(count, *refs):
    pieces, (query, keyval, out) = refs[:count], refs[count:]
    total = sum_pieces(pieces)
    width = query.shape[1]
    query[...] = total[:, :width]
    keyval[0] = total[:, width : 2 * width]
    keyval[1] = total[:, 2 * width : 3 * width]
    out[...] = total[:, 3 * width :].T


def close_ffn_kernel(count, *refs):
    pieces, (up, down) = refs[:count], refs[count:]
    total = sum_pieces(pieces)
    hidden = up.shape[1]
    up[...] = total[:, :hidden]
    down[...] = total[:, hidden:].T


def swap(value, axis, size, bits):
    return lax.ppermute(value, axis, [(i, i ^ bits) for i in range(size)])


def per_device(
    dp_size,
    mp_size,
    text_tokens,
    image_tokens,
    text_lengths,
    patch_counts,
    self_qkv,
    self_out,
    cross_query,
    cross_keyval,
    cross_out,
    mlp_up,
    mlp_down,
    norm_gain,
    norm_bias,
    out_bias,
    up_bias,
    out_grad,
):
    seqs, positions, model = text_tokens.shape
    patches = image_tokens.shape[1]
    rows = seqs * positions
    half = rows // 2
    width = cross_query.shape[1]
    hidden = mlp_up.shape[1]
    image_rows = seqs * patches
    quick = dp_size == 8
    height = model // dp_size
    place = lax.axis_index("dp")
    lane = lax.axis_index("mp")
    core, level = lane % 2, lane // 2
    if quick:
        offsets = [(place ^ (((k & 3) << 1) | (k >> 2))) * height for k in range(8)]
        count, parts, out_blocks = 8, 2, [(4, height)] * 2
    else:
        offsets = [place * 0] * 8
        count, parts, out_blocks = 1, 1, [(1, model)]
    blocks = [(2 * (level ^ j) + (core ^ side)) * width for side in range(2) for j in range(2)]
    tab = jnp.stack(offsets + [core * half, (1 - core) * half] + blocks + [core, level]).astype(
        jnp.int32
    )

    def gather(shard):
        if not quick:
            return [lax.all_gather(shard, "dp", axis=0, tiled=True)]
        near = [shard] + [swap(shard, "dp", 8, k << 1) for k in (1, 2, 3)]
        return near + [swap(piece, "dp", 8, 1) for piece in near]

    def reduce_scatter(outs):
        if not quick:
            total = lax.psum_scatter(outs[0][0], "dp", scatter_dimension=0, tiled=True)
            return [total]
        keep, send = outs
        other = swap(send, "dp", 8, 1)
        near = call(
            add_kernel, "add_blocks", [(keep.shape[1:], BF)] * 4, (), (keep, other)
        )
        return [near[0]] + [swap(near[k], "dp", 8, k << 1) for k in (1, 2, 3)]

    def mp_sum(send, keep):
        other = swap(send, "mp", mp_size, 1)
        chip = (keep.astype(F32) + other.astype(F32)).astype(BF)
        return chip, swap(chip, "mp", mp_size, 2)

    def core_swap(value):
        return swap(value, "mp", mp_size, 1)

    text = text_tokens.reshape(rows, model)
    image = image_tokens.reshape(image_rows, model)
    grad = out_grad.reshape(rows, model)

    if quick:
        (self_shard,) = call(
            pack_self_kernel, "pack_self", [((height, 4 * width), BF)], (), (self_qkv, self_out)
        )
        cross_shard, ffn_shard = call(
            pack_rest_kernel,
            "pack_rest",
            [((height, 4 * width), BF), ((height, 2 * hidden), BF)],
            (),
            (cross_query, cross_keyval, cross_out, mlp_up, mlp_down),
        )
    else:
        self_shard = jnp.concatenate([self_qkv[0], self_qkv[1], self_qkv[2], self_out.T], 1)
        cross_shard = jnp.concatenate(
            [cross_query, cross_keyval[0], cross_keyval[1], cross_out.T], 1
        )
        ffn_shard = jnp.concatenate([mlp_up, mlp_down.T], 1)
    self_pieces = gather(self_shard)
    cross_pieces = gather(cross_shard)
    ffn_pieces = gather(ffn_shard)

    square = ((model, width), BF)
    narrow = ((rows, width), BF)
    wide = ((rows, model), BF)
    halves = [((half, model), BF)] * 2
    half_f32 = ((half, model), F32)
    half_low = ((half, model), BF)
    heads = width // HEAD_DIM
    full = pltpu.VMEM((rows, model), F32)

    (wq, wk, wv, wo, normed_text, q, k, v, self_prob, self_ctx, send, keep) = call(
        functools.partial(self_forward_kernel, count, seqs),
        "self_forward",
        [square] * 4
        + [wide]
        + [narrow] * 3
        + [((seqs, heads * positions, positions), F32), narrow]
        + halves,
        (tab, text_lengths),
        (text, norm_gain, norm_bias, *self_pieces),
        [full],
        flops=2 * rows * model * width * 4,
    )
    chip, other = mp_sum(send, keep)

    constant = lambda b: (0, 0)
    per_seq = lambda b: (b, 0)
    cq, ck, cv, co, keys, values = pl.pallas_call(
        functools.partial(keyval_kernel, count),
        grid=(seqs,),
        out_shape=[jax.ShapeDtypeStruct((model, width), BF)] * 4
        + [jax.ShapeDtypeStruct((image_rows, width), BF)] * 2,
        in_specs=[
            pl.BlockSpec(memory_space=pltpu.SMEM),
            pl.BlockSpec((patches, model), per_seq),
        ]
        + [pl.BlockSpec(cross_pieces[0].shape, constant)] * count,
        out_specs=[pl.BlockSpec((model, width), constant)] * 4
        + [pl.BlockSpec((patches, width), per_seq)] * 2,
        compiler_params=pltpu.CompilerParams(vmem_limit_bytes=VMEM_LIMIT),
        cost_estimate=pl.CostEstimate(
            flops=2 * image_rows * model * width * 2,
            bytes_accessed=image.size * 2,
            transcendentals=0,
        ),
        name="keyval",
    )(tab, image, *cross_pieces)

    hidden_one, normed_half = call(
        functools.partial(norm_kernel, 0, True),
        "norm_mid",
        [half_f32, half_low],
        (tab,),
        (chip, other, text, out_bias, norm_gain, norm_bias),
    )
    normed_mid, xq, cross_prob, cross_ctx, send, keep = call(
        functools.partial(cross_forward_kernel, seqs),
        "cross_forward",
        [wide, narrow, ((seqs, heads * positions, patches), F32), narrow] + halves,
        (tab, patch_counts),
        (normed_half, core_swap(normed_half), cq, co, keys, values),
        [full],
        flops=2 * rows * model * width * 2,
    )
    chip, other = mp_sum(send, keep)
    w_up, w_down, grad_act = call(
        functools.partial(ffn_ready_kernel, count),
        "ffn_ready",
        [((model, hidden), BF)] * 2 + [((rows, hidden), F32)],
        (tab,),
        (grad, *ffn_pieces),
        flops=2 * rows * model * hidden,
    )
    hidden_two, normed_half = call(
        functools.partial(norm_kernel, 1, False),
        "norm_ffn",
        [half_f32, half_low],
        (tab,),
        (chip, other, hidden_one, out_bias, norm_gain, norm_bias),
    )
    (normed_ffn, act, grad_low, up_sum, send, keep, out_send, out_keep) = call(
        ffn_kernel,
        "ffn",
        [wide, ((rows, hidden), BF), ((rows, hidden), BF), ((1, hidden), F32)] + halves + halves,
        (tab,),
        (
            normed_half,
            core_swap(normed_half),
            w_up,
            w_down,
            grad_act,
            up_bias.reshape(1, hidden),
        ),
        [full],
        flops=2 * rows * model * hidden * 3,
    )
    chip, other = mp_sum(send, keep)
    out_chip, out_other = mp_sum(out_send, out_keep)

    ffn_blocks = call(
        functools.partial(ffn_weight_kernel, parts),
        "ffn_weights",
        [(b + (2 * hidden,), BF) for b in out_blocks],
        (tab,),
        (normed_ffn, grad_low, grad, act),
        [pltpu.VMEM((model, hidden), F32)],
        flops=2 * rows * model * hidden * 2,
    )
    ffn_sums = reduce_scatter(ffn_blocks)
    vec_shape = ((8, model), F32)
    grad_two, low_half, vec_two = call(
        functools.partial(norm_back_kernel, 2, True),
        "norm_back_ffn",
        [half_f32, half_low, vec_shape],
        (tab,),
        (chip, other, hidden_two, grad, norm_gain),
    )
    grad_two_low, dq, dk, dv, send, keep = call(
        functools.partial(cross_back_kernel, seqs),
        "cross_back",
        [wide, narrow, ((image_rows, width), BF), ((image_rows, width), BF)] + halves,
        (tab,),
        (low_half, core_swap(low_half), cq, co, keys, values, xq, cross_prob),
        [full],
        flops=2 * rows * model * width * 2,
    )
    chip, other = mp_sum(send, keep)
    whole = lambda shape: pl.BlockSpec(shape, lambda b: (0,) * len(shape))
    cross_blocks = pl.pallas_call(
        functools.partial(cross_weight_kernel, parts),
        grid=(seqs,),
        out_shape=[jax.ShapeDtypeStruct(b + (4 * width,), BF) for b in out_blocks],
        in_specs=[
            pl.BlockSpec(memory_space=pltpu.SMEM),
            pl.BlockSpec((patches, model), per_seq),
            pl.BlockSpec((patches, width), per_seq),
            pl.BlockSpec((patches, width), per_seq),
            whole((rows, model)),
            whole((rows, width)),
            whole((rows, model)),
            whole((rows, width)),
        ],
        out_specs=[whole(b + (4 * width,)) for b in out_blocks],
        scratch_shapes=[pltpu.VMEM((model, width), F32)] * 2,
        compiler_params=pltpu.CompilerParams(vmem_limit_bytes=VMEM_LIMIT),
        cost_estimate=pl.CostEstimate(
            flops=2 * image_rows * model * width * 2,
            bytes_accessed=image.size * 2,
            transcendentals=0,
        ),
        name="cross_weights",
    )(tab, image, dk, dv, normed_mid, dq, grad_two_low, cross_ctx)
    cross_sums = reduce_scatter(cross_blocks)
    image_send, image_keep = pl.pallas_call(
        image_part_kernel,
        grid=(seqs,),
        out_shape=[jax.ShapeDtypeStruct((image_rows, 2 * width), BF)] * 2,
        in_specs=[
            pl.BlockSpec(memory_space=pltpu.SMEM),
            pl.BlockSpec((patches, width), per_seq),
            pl.BlockSpec((patches, width), per_seq),
            whole((model, width)),
            whole((model, width)),
        ],
        out_specs=[pl.BlockSpec((patches, 2 * width), per_seq)] * 2,
        compiler_params=pltpu.CompilerParams(vmem_limit_bytes=VMEM_LIMIT),
        cost_estimate=pl.CostEstimate(
            flops=2 * image_rows * model * width * 2,
            bytes_accessed=image.size * 2,
            transcendentals=0,
        ),
        name="image_part",
    )(tab, dk, dv, ck, cv)
    image_own, image_away = call(
        image_chip_kernel,
        "image_chip",
        [((image_rows, width), BF), ((image_rows // 2, 2 * width), BF)],
        (),
        (image_keep, core_swap(image_send)),
    )
    (image_grad,) = call(
        image_sum_kernel,
        "image_sum",
        [((image_rows, width), F32)],
        (),
        (image_own, swap(image_away, "mp", mp_size, 2)),
    )
    grad_one, low_half, vec_one = call(
        functools.partial(norm_back_kernel, 1, False),
        "norm_back_mid",
        [half_f32, half_low, vec_shape],
        (tab,),
        (chip, other, hidden_one, grad_two, norm_gain),
    )
    self_back = call(
        functools.partial(self_back_kernel, seqs, parts),
        "self_back",
        [(b + (4 * width,), BF) for b in out_blocks] + halves + [vec_shape],
        (tab,),
        (
            low_half,
            core_swap(low_half),
            text,
            norm_gain,
            normed_text,
            wq,
            wk,
            wv,
            wo,
            q,
            k,
            v,
            self_prob,
            self_ctx,
        ),
        [
            pltpu.VMEM((rows, model), BF),
            pltpu.VMEM((rows, width), BF),
            pltpu.VMEM((rows, width), BF),
            pltpu.VMEM((rows, width), BF),
            full,
            pltpu.VMEM((model, width), F32),
        ],
        flops=2 * rows * model * width * 8,
    )
    self_blocks, (send, keep, vec_zero) = self_back[:parts], self_back[parts:]
    self_sums = reduce_scatter(self_blocks)
    chip, other = mp_sum(send, keep)
    (text_half,) = call(
        text_grad_kernel,
        "text_grad",
        [half_f32],
        (tab,),
        (chip, other, text, grad_one, norm_gain),
    )
    (text_grad,) = call(
        join_kernel, "text_join", [((rows, model), F32)], (tab,), (text_half, core_swap(text_half))
    )
    (out_half,) = call(
        layer_out_kernel,
        "layer_out",
        [half_low],
        (),
        (out_chip, out_other, hidden_two, out_bias),
    )
    (layer_out,) = call(join_kernel, "out_join", [wide], (tab,), (out_half, core_swap(out_half)))

    vector = jnp.concatenate(
        [
            vec_zero[0:1],
            vec_one[0:1],
            vec_two[0:1],
            vec_zero[1:2],
            vec_one[1:2],
            vec_two[1:2],
            vec_one[2:3],
            vec_two[2:3],
            vec_two[3:4],
        ],
        axis=0,
    )
    if quick:
        for bits in (1, 2):
            vector = vector + swap(vector, "mp", mp_size, bits)
        vector = jnp.concatenate([vector, up_sum], axis=0)
        for bits in (1, 2, 4):
            vector = vector + swap(vector, "dp", dp_size, bits)
        gains, shifts, biases, ups = vector[0:3], vector[3:6], vector[6:9], vector[9]
    else:
        vector = lax.psum(vector, ("dp", "mp"))
        ups = lax.psum(up_sum, "dp")[0]
        gains, shifts, biases = vector[0:3], vector[3:6], vector[6:9]

    if quick:
        qkv_grad, self_out_grad = call(
            functools.partial(close_self_kernel, 4),
            "close_self",
            [((3, height, width), F32), ((width, height), F32)],
            (),
            self_sums,
        )
        query_grad, keyval_grad, cross_out_grad = call(
            functools.partial(close_cross_kernel, 4),
            "close_cross",
            [((height, width), F32), ((2, height, width), F32), ((width, height), F32)],
            (),
            cross_sums,
        )
        up_grad, down_grad = call(
            functools.partial(close_ffn_kernel, 4),
            "close_ffn",
            [((height, hidden), F32), ((hidden, height), F32)],
            (),
            ffn_sums,
        )
    else:
        total = self_sums[0].astype(F32)
        qkv_grad = jnp.stack([total[:, j * width : (j + 1) * width] for j in range(3)])
        self_out_grad = total[:, 3 * width :].T
        total = cross_sums[0].astype(F32)
        query_grad = total[:, :width]
        keyval_grad = jnp.stack([total[:, j * width : (j + 1) * width] for j in (1, 2)])
        cross_out_grad = total[:, 3 * width :].T
        total = ffn_sums[0].astype(F32)
        up_grad, down_grad = total[:, :hidden], total[:, hidden:].T
    return (
        layer_out.reshape(seqs, positions, model),
        text_grad.reshape(seqs, positions, model),
        image_grad.reshape(seqs, patches, width),
        qkv_grad,
        self_out_grad,
        query_grad,
        keyval_grad,
        cross_out_grad,
        up_grad,
        down_grad,
        gains,
        shifts,
        biases,
        ups,
    )


def solution(mesh):
    placed = (
        P("dp", None, None),
        P("dp", None, None),
        P("dp"),
        P("dp"),
        P(None, "dp", "mp"),
        P("mp", "dp"),
        P("dp", "mp"),
        P(None, "dp", "mp"),
        P("mp", "dp"),
        P("dp", "mp"),
        P("mp", "dp"),
        P(),
        P(),
        P(),
        P("mp"),
        P("dp", None, None),
    )
    return jax.shard_map(
        functools.partial(per_device, mesh.shape["dp"], mesh.shape["mp"]),
        mesh=mesh,
        in_specs=placed,
        out_specs=(
            P("dp", None, None),
            P("dp", None, None),
            P("dp", None, "mp"),
            P(None, "dp", "mp"),
            P("mp", "dp"),
            P("dp", "mp"),
            P(None, "dp", "mp"),
            P("mp", "dp"),
            P("dp", "mp"),
            P("mp", "dp"),
            P(),
            P(),
            P(),
            P("mp"),
        ),
        check_vma=False,
    )
```

```python
import functools
import math

import jax
import jax.numpy as jnp
from jax import lax
from jax.experimental import pallas as pl
from jax.experimental.pallas import tpu as pltpu
from jax.sharding import PartitionSpec as P

BF = jnp.bfloat16
F32 = jnp.float32
HEAD_DIM = 64
SCALE = HEAD_DIM ** (-0.5)
NORM_EPS = 1e-05
NEG_FILL = -1e30
INV_ROOT_TWO = 1.0 / math.sqrt(2.0)
INV_ROOT_TAU = 1.0 / math.sqrt(2.0 * math.pi)
VMEM_LIMIT = 24 * 1024 * 1024
COST_PER_BYTE = 1
COST = pl.CostEstimate(flops=1, bytes_accessed=10**7, transcendentals=0)


def nn(a, b):
    return lax.dot_general(a, b, (((1,), (0,)), ((), ())), preferred_element_type=F32)


def nt(a, b):
    return lax.dot_general(a, b, (((1,), (1,)), ((), ())), preferred_element_type=F32)


def tn(a, b):
    return lax.dot_general(a, b, (((0,), (0,)), ((), ())), preferred_element_type=F32)


def norm_parts(values):
    centered = values - jnp.mean(values, axis=-1, keepdims=True)
    inv_std = lax.rsqrt(jnp.mean(centered * centered, axis=-1, keepdims=True) + NORM_EPS)
    return centered * inv_std, inv_std


def norm_back(grad, normed, inv_std, gain_row):
    scaled = grad * gain_row
    first = jnp.mean(scaled, axis=-1, keepdims=True)
    second = jnp.mean(scaled * normed, axis=-1, keepdims=True)
    return inv_std * (scaled - first - normed * second)


def head_masks(width, kind):
    column = lax.broadcasted_iota(jnp.int32, (1, width), 1) // HEAD_DIM
    return [(column == h).astype(F32).astype(kind) for h in range(width // HEAD_DIM)]


def stack_heads(rows, masks):
    return jnp.concatenate([rows * m for m in masks], axis=0)


def unstack_heads(stacked, masks):
    count = stacked.shape[0] // len(masks)
    total = stacked[:count] * masks[0]
    for h in range(1, len(masks)):
        total = total + stacked[h * count : (h + 1) * count] * masks[h]
    return total


def call(body, name, outs, scalars, arrays, scratch=(), flops=0):
    nbytes = sum(a.size * a.dtype.itemsize for a in arrays)
    nbytes += sum(math.prod(s) * jnp.dtype(d).itemsize for s, d in outs)
    return pl.pallas_call(
        body,
        out_shape=[jax.ShapeDtypeStruct(s, d) for s, d in outs],
        in_specs=[pl.BlockSpec(memory_space=pltpu.SMEM)] * len(scalars)
        + [pl.BlockSpec(memory_space=pltpu.VMEM)] * len(arrays),
        out_specs=[pl.BlockSpec(memory_space=pltpu.VMEM)] * len(outs),
        scratch_shapes=list(scratch),
        compiler_params=pltpu.CompilerParams(vmem_limit_bytes=VMEM_LIMIT),
        cost_estimate=pl.CostEstimate(
            flops=1, bytes_accessed=int(nbytes * COST_PER_BYTE) + 1, transcendentals=0
        ),
        name=name,
    )(*scalars, *arrays)


def turns_of(one, two, three):
    return [a ^ b ^ c for a in (0, one) for c in (0, three) for b in (0, two)]


X_FIRST = (1, 2, 4)
Z_FIRST = (2, 4, 1)


def block_rows(turn, height):
    at = (lax.axis_index("dp") ^ turn) * height
    return pl.ds(pl.multiple_of(at, 32), height)


def half_rows(height, away=False):
    core = lax.axis_index("mp") & 1
    at = (1 - core if away else core) * height
    return pl.ds(pl.multiple_of(at, 128), height)


def ring_rows(hops, height):
    index = lax.axis_index("dp")
    spot = jnp.where((index & 1) == 0, index >> 1, 7 - (index >> 1))
    spot = (spot + hops + 8) & 7
    at = jnp.where(spot < 4, 2 * spot, 15 - 2 * spot) * height
    return pl.ds(pl.multiple_of(at, 32), height)


def place_pieces(pieces, targets):
    if len(pieces) == 1:
        blocks = [(slice(None), pieces[0])]
    else:
        height = pieces[0].shape[0]
        side = 2 * (lax.axis_index("mp") & 1) - 1
        blocks = [(ring_rows(0, height), pieces[0]), (ring_rows(4, height), pieces[7])]
        for k in (1, 2, 3):
            blocks.append((ring_rows(side * k, height), pieces[k].at[0]))
            blocks.append((ring_rows(-side * k, height), pieces[3 + k].at[1]))
    for rows, piece in blocks:
        start = 0
        for target in targets:
            width = target.shape[1]
            target[rows, :] = piece[:, start : start + width]
            start += width


def join_halves(own, other, target):
    half = own.shape[0]
    target[half_rows(half), :] = own[...]
    target[half_rows(half, True), :] = other[...]


def split_halves(full, send, keep):
    half = full.shape[0] // 2
    keep[:half] = full[half_rows(half), :].astype(keep.dtype)
    send[:half] = full[half_rows(half, True), :].astype(send.dtype)


def pack_self_kernel(qkv, out, packed):
    width = qkv.shape[2]
    for j in range(3):
        packed[:, j * width : (j + 1) * width] = qkv[j]
    packed[:, 3 * width :] = out[...].astype(F32).T.astype(BF)


def pack_cross_kernel(query, keyval, out, cross):
    width = query.shape[1]
    cross[:, :width] = query[...]
    cross[:, width : 2 * width] = keyval[0]
    cross[:, 2 * width : 3 * width] = keyval[1]
    cross[:, 3 * width :] = out[...].astype(F32).T.astype(BF)


def pack_ffn_kernel(up, down, ffn):
    hidden = up.shape[1]
    ffn[:, :hidden] = up[...]
    ffn[:, hidden:] = down[...]


def pair_kernel(own, other, out):
    out[0] = own[...]
    out[1] = other[...]


def take_kernel(pair, out):
    out[...] = pair[0]


def self_forward_kernel(
    count, seqs, lens, text, gain, bias, *refs
):
    pieces, (weights, saved, send, keep, w, qkv, full, sems) = refs[:count], refs[count:]
    place_pieces(pieces, (w,))
    save_w = pltpu.make_async_copy(w, weights, sems.at[0])
    save_w.start()
    n, _ = norm_parts(text[...].astype(F32))
    low = (n * gain[0:1] + bias[0:1]).astype(BF)
    width = w.shape[1] // 4
    qkv[:, : 3 * width] = nn(low, w[:, : 3 * width]).astype(BF)
    low_masks, masks = head_masks(width, BF), head_masks(width, F32)
    rows = text.shape[0] // seqs
    for b in range(seqs):
        at = slice(b * rows, (b + 1) * rows)
        q_stack = stack_heads(qkv[at, :width], low_masks)
        p = self_softmax(q_stack, qkv[at, width : 2 * width], lens[b], rows)
        qkv[at, 3 * width :] = unstack_heads(
            nn(p.astype(BF), qkv[at, 2 * width : 3 * width]), masks
        ).astype(BF)
    save_q = pltpu.make_async_copy(qkv, saved, sems.at[1])
    save_q.start()
    full[...] = nt(qkv[:, 3 * width :], w[:, 3 * width :])
    split_halves(full, send, keep)
    save_w.wait()
    save_q.wait()


def self_softmax(q_stack, keys, length, rows):
    shape = (q_stack.shape[0], rows)
    query_at = lax.broadcasted_iota(jnp.int32, shape, 0) % rows
    key_at = lax.broadcasted_iota(jnp.int32, shape, 1)
    allowed = (key_at <= query_at) & (key_at < length)
    scores = jnp.where(allowed, nt(q_stack, keys) * SCALE, NEG_FILL)
    raised = jnp.exp(scores - jnp.max(scores, axis=-1, keepdims=True))
    return raised / jnp.sum(raised, axis=-1, keepdims=True)


def keyval_kernel(count, image, *refs):
    pieces, (wq, wk, wv, wo, keys, values) = refs[:count], refs[count:]

    @pl.when(pl.program_id(0) == 0)
    def _():
        place_pieces(pieces, (wq, wk, wv, wo))

    keys[...] = nn(image[...], wk[...]).astype(BF)
    values[...] = nn(image[...], wv[...]).astype(BF)


def norm_kernel(index, sliced, chip, other, resid, out_bias, gain, bias, hidden, normed):
    half = chip.shape[0]
    if sliced:
        base = resid[half_rows(half), :].astype(F32)
    else:
        base = resid[...]
    value = (
        base
        + (chip[...].astype(F32) + other[...].astype(F32))
        + out_bias[index : index + 1]
    )
    hidden[...] = value
    n, _ = norm_parts(value)
    normed[...] = (n * gain[index + 1 : index + 2] + bias[index + 1 : index + 2]).astype(BF)


def cross_forward_kernel(
    seqs, counts, own, other, wq, wo, keys, values, normed, q, prob, ctx, send, keep, full
):
    join_halves(own, other, normed)
    q[...] = nn(normed[...], wq[...]).astype(BF)
    width = q.shape[1]
    low_masks, masks = head_masks(width, BF), head_masks(width, F32)
    rows = normed.shape[0] // seqs
    patches = keys.shape[0] // seqs
    patch_at = lax.broadcasted_iota(jnp.int32, (rows * len(masks), patches), 1)
    for b in range(seqs):
        at = slice(b * rows, (b + 1) * rows)
        ks = slice(b * patches, (b + 1) * patches)
        scores = nt(stack_heads(q[at], low_masks), keys[ks]) * SCALE
        scores = jnp.where(patch_at < counts[b], scores, NEG_FILL)
        raised = jnp.exp(scores - jnp.max(scores, axis=-1, keepdims=True))
        p = raised / jnp.sum(raised, axis=-1, keepdims=True)
        prob[b] = p
        ctx[at] = unstack_heads(nn(p.astype(BF), values[ks]), masks).astype(BF)
    full[...] = nt(ctx[...], wo[...])
    split_halves(full, send, keep)


def ffn_ready_kernel(count, grad, *refs):
    pieces, (up, down, grad_act) = refs[:count], refs[count:]
    place_pieces(pieces, (up, down))
    grad_act[...] = nn(grad[...], down[...])


def ffn_kernel(
    own, other, up, down, grad_act, up_bias,
    normed, act, grad_low, bias_sum, send, keep, out_send, out_keep, full,
):
    join_halves(own, other, normed)
    pre = nn(normed[...], up[...]) + up_bias[...]
    cdf = 0.5 * (1.0 + lax.erf(pre * INV_ROOT_TWO))
    density = jnp.exp(-0.5 * pre * pre) * INV_ROOT_TAU
    grad_pre = grad_act[...] * (cdf + pre * density)
    grad_low[...] = grad_pre.astype(BF)
    act[...] = (pre * cdf).astype(BF)
    bias_sum[...] = jnp.sum(grad_pre, axis=0, keepdims=True)
    full[...] = nt(grad_low[...], up[...])
    split_halves(full, send, keep)
    full[...] = nt(act[...], down[...])
    split_halves(full, out_send, out_keep)


def scatter_blocks(matrix, column, outs, order=X_FIRST):
    blocks = sum(o.shape[0] for o in outs)
    height = outs[0].shape[1]
    width = matrix.shape[1]
    turns = turns_of(*order)
    for k in range(blocks):
        rows = block_rows(turns[k], height) if blocks > 1 else slice(None)
        target = outs[k // outs[0].shape[0]]
        target[k % outs[0].shape[0], :, column : column + width] = matrix[rows, :].astype(BF)


def ffn_weight_kernel(parts, normed, grad_low, grad, act, *refs):
    ups, downs, full = refs[:parts], refs[parts : 2 * parts], refs[2 * parts]
    full[...] = tn(normed[...], grad_low[...])
    scatter_blocks(full, 0, ups, Z_FIRST)
    full[...] = tn(grad[...], act[...])
    scatter_blocks(full, 0, downs)


def norm_back_kernel(index, sliced, chip, other, hidden, resid, gain, total, low, vec):
    half = chip.shape[0]
    if sliced:
        base = resid[half_rows(half), :].astype(F32)
    else:
        base = resid[...]
    grad = chip[...].astype(F32) + other[...].astype(F32)
    n, inv_std = norm_parts(hidden[...])
    value = base + norm_back(grad, n, inv_std, gain[index : index + 1])
    total[...] = value
    low[...] = value.astype(BF)
    vec[...] = jnp.zeros_like(vec)
    vec[0:1] = 0.5 * jnp.sum(grad * n, axis=0, keepdims=True)
    vec[1:2] = 0.5 * jnp.sum(grad, axis=0, keepdims=True)
    vec[2:3] = 0.5 * jnp.sum(value, axis=0, keepdims=True)
    if sliced:
        vec[3:4] = 0.5 * jnp.sum(base, axis=0, keepdims=True)


def score_grad(p, values, grad_stack):
    grad_p = nt(grad_stack, values)
    inner = jnp.sum(p * grad_p, axis=-1, keepdims=True)
    return (p * (grad_p - inner)).astype(BF)


def cross_back_kernel(
    seqs, own, other, wq, wo, keys, values, q, prob, grad_two, dq, dkt, dvt, send, keep, full
):
    join_halves(own, other, grad_two)
    grad_ctx = nn(grad_two[...], wo[...]).astype(BF)
    width = q.shape[1]
    low_masks, masks = head_masks(width, BF), head_masks(width, F32)
    rows = q.shape[0] // seqs
    patches = keys.shape[0] // seqs
    for b in range(seqs):
        at = slice(b * rows, (b + 1) * rows)
        ks = slice(b * patches, (b + 1) * patches)
        p = prob[b]
        q_stack = stack_heads(q[at], low_masks)
        grad_stack = stack_heads(grad_ctx[at], low_masks)
        ds = score_grad(p, values[ks], grad_stack)
        dq[at] = unstack_heads(nn(ds, keys[ks]) * SCALE, masks).astype(BF)
        dkt[:, ks] = (tn(q_stack, ds) * SCALE).astype(BF)
        dvt[:, ks] = tn(grad_stack, p.astype(BF)).astype(BF)
    full[...] = nt(dq[...], wq[...])
    split_halves(full, send, keep)


def cross_weight_kernel(parts, image, dkt, dvt, normed, dq, grad_two, ctx, *refs):
    outs, turned = refs[:parts], refs[parts]
    width = dq.shape[1]
    turned[...] = tn(normed[...], dq[...])
    scatter_blocks(turned, 0, outs)
    turned[...] = nn(dkt[...], image[...]).T
    scatter_blocks(turned, width, outs)
    turned[...] = nn(dvt[...], image[...]).T
    scatter_blocks(turned, 2 * width, outs)
    turned[...] = tn(grad_two[...], ctx[...])
    scatter_blocks(turned, 3 * width, outs)


def image_part_kernel(dkt, dvt, wk, wv, send_away, send_own, keep_away, keep_own):
    width = wk.shape[1]
    for k, target in enumerate((keep_own, keep_away, send_own, send_away)):
        core, level = lax.axis_index("mp") & 1, lax.axis_index("mp") >> 1
        at = (2 * (level ^ (k & 1)) + (core ^ (k >> 1))) * width
        rows = pl.ds(pl.multiple_of(at, 64), width)
        target[...] = (nn(wk[rows, :], dkt[...]) + nn(wv[rows, :], dvt[...])).astype(BF)


def add_pair_kernel(one, two, out):
    out[...] = (one[...].astype(F32) + two[...].astype(F32)).astype(BF)


def image_chip_kernel(keep_own, own, keep_away, away, out_own, out_away):
    out_own[...] = keep_own[...].astype(F32) + own[...].astype(F32)
    out_away[...] = (keep_away[...].astype(F32) + away[...].astype(F32)).astype(BF)


def image_sum_kernel(own, away, out):
    patches = out.shape[2]
    for b in range(out.shape[0]):
        ks = slice(b * patches, (b + 1) * patches)
        out[b] = own[:, ks] + away[:, ks].astype(F32)


def self_back_kernel(
    seqs, parts, lens, own, other, text, gain, bias, w, qkv,
    out_send, out_keep, one, two, ups, *refs
):
    outs = refs[:parts]
    send, keep, low, dqkv, full, narrow, vec = refs[parts:]
    join_halves(own, other, low)
    width = w.shape[1] // 4
    grad_ctx = nn(low[...], w[:, 3 * width :]).astype(BF)
    low_masks, masks = head_masks(width, BF), head_masks(width, F32)
    rows = text.shape[0] // seqs
    for b in range(seqs):
        at = slice(b * rows, (b + 1) * rows)
        q_stack = stack_heads(qkv[at, :width], low_masks)
        keys = qkv[at, width : 2 * width]
        p = self_softmax(q_stack, keys, lens[b], rows)
        grad_stack = stack_heads(grad_ctx[at], low_masks)
        ds = score_grad(p, qkv[at, 2 * width : 3 * width], grad_stack)
        dqkv[0, at] = unstack_heads(nn(ds, keys) * SCALE, masks).astype(BF)
        dqkv[1, at] = (tn(ds, q_stack) * SCALE).astype(BF)
        dqkv[2, at] = tn(p.astype(BF), grad_stack).astype(BF)
    n, _ = norm_parts(text[...].astype(F32))
    normed = (n * gain[0:1] + bias[0:1]).astype(BF)
    for j in range(3):
        narrow[...] = tn(normed, dqkv[j])
        scatter_blocks(narrow, j * width, outs)
    narrow[...] = tn(low[...], qkv[:, 3 * width :])
    scatter_blocks(narrow, 3 * width, outs)
    part = nt(dqkv[0], w[:, :width])
    for j in (1, 2):
        part = part + nt(dqkv[j], w[:, j * width : (j + 1) * width])
    full[...] = part
    split_halves(full, send, keep)
    half = own.shape[0]
    send[half : 2 * half] = out_send[...]
    keep[half : 2 * half] = out_keep[...]
    vec[...] = jnp.zeros_like(vec)
    vec[0:1] = jnp.sum(part * n, axis=0, keepdims=True)
    vec[1:2], vec[2:3] = one[0:1], two[0:1]
    vec[3:4] = jnp.sum(part, axis=0, keepdims=True)
    vec[4:5], vec[5:6] = one[1:2], two[1:2]
    vec[6:7], vec[7:8], vec[8:9] = one[2:3], two[2:3], two[3:4]
    vec[pl.ds(9 + lax.axis_index("mp"), 1), :] = ups[...]
    send[2 * half :] = vec[...].astype(BF)
    keep[2 * half :] = vec[...].astype(BF)


def finish_kernel(chip, other, text, resid, gain, hidden, out_bias, grad_out, layer_out, vec):
    half = resid.shape[0]
    grad = chip[:half].astype(F32) + other[:half].astype(F32)
    base = text[half_rows(half), :].astype(F32)
    n, inv_std = norm_parts(base)
    grad_out[...] = resid[...] + norm_back(grad, n, inv_std, gain[0:1])
    mid = slice(half, 2 * half)
    layer_out[...] = (
        hidden[...] + (chip[mid].astype(F32) + other[mid].astype(F32)) + out_bias[2:3]
    ).astype(BF)
    vec[...] = (chip[2 * half :].astype(F32) + other[2 * half :].astype(F32)).astype(BF)


def join_both_kernel(own, other, own_low, other_low, out, out_low):
    join_halves(own, other, out)
    join_halves(own_low, other_low, out_low)


def fold_kernel(keep, other, stay, send):
    for k in range(keep.shape[0]):
        target = send if k % 2 else stay
        value = (keep[k].astype(F32) + other[k].astype(F32)).astype(target.dtype)
        if len(target.shape) == 3:
            target[k // 2] = value
        else:
            target[...] = value


def fold_self_one_kernel(keep, other, vec, vec_other, stay, send, vec_sum):
    height = keep.shape[1]
    for k in range(4):
        value = (keep[k].astype(F32) + other[k].astype(F32)).astype(BF)
        at = (k // 2) * height
        (send if k % 2 else stay)[at : at + height] = value
    total = (vec[...].astype(F32) + vec_other[...].astype(F32)).astype(BF)
    vec_sum[...] = total
    send[2 * height :] = total


def fold_self_two_kernel(keep, other, vec, stay, send, vec_sum):
    height = stay.shape[0]
    stay[...] = keep[:height].astype(F32) + other[:height].astype(F32)
    rest = slice(height, 2 * height)
    send[:height] = (keep[rest].astype(F32) + other[rest].astype(F32)).astype(BF)
    total = (vec[...].astype(F32) + other[2 * height :].astype(F32)).astype(BF)
    vec_sum[...] = total
    send[height:] = total


def vector_parts(total, gains, shifts, biases, ups):
    gains[...] = total[0:3]
    shifts[...] = total[3:6]
    biases[...] = total[6:9]
    full = total[9]
    for k in range(1, 4):
        full = jnp.where(lax.axis_index("mp") == k, total[9 + k], full)
    ups[...] = full


def vector_kernel(vec, gains, shifts, biases, ups):
    vector_parts(vec[...], gains, shifts, biases, ups)


def close_cross_kernel(*refs):
    own, other, query, keyval, out = refs
    total = own[...] + other[...].astype(F32)
    width = out.shape[0]
    query[...] = total[:, :width]
    keyval[0] = total[:, width : 2 * width]
    keyval[1] = total[:, 2 * width : 3 * width]
    out[...] = total[:, 3 * width :].T


def close_ffn_kernel(own, other, out):
    out[...] = own[...] + other[...].astype(F32)


def close_self_kernel(own, other, vec, qkv, out, gains, shifts, biases, ups):
    height = own.shape[0]
    total = own[...] + other[:height].astype(F32)
    width = out.shape[0]
    for j in range(3):
        qkv[j] = total[:, j * width : (j + 1) * width]
    out[...] = total[:, 3 * width :].T
    vector_parts(vec[...].astype(F32) + other[height:].astype(F32), gains, shifts, biases, ups)


def swap(value, axis, size, bits):
    return lax.ppermute(value, axis, [(i, i ^ bits) for i in range(size)])


def gate_all(values, *first):
    return list(lax.optimization_barrier((*values, *first)))[: len(values)]


def gate(value, *first):
    return lax.optimization_barrier((value, *first))[0]


def per_device(
    dp_size,
    mp_size,
    text_tokens,
    image_tokens,
    text_lengths,
    patch_counts,
    self_qkv,
    self_out,
    cross_query,
    cross_keyval,
    cross_out,
    mlp_up,
    mlp_down,
    norm_gain,
    norm_bias,
    out_bias,
    up_bias,
    out_grad,
):
    seqs, positions, model = text_tokens.shape
    patches = image_tokens.shape[1]
    rows = seqs * positions
    half = rows // 2
    width = cross_query.shape[1]
    hidden = mlp_up.shape[1]
    image_rows = seqs * patches
    quick = dp_size == 8
    height = model // dp_size
    parts, blocks = (2, (4, height)) if quick else (1, (1, model))

    spots = [0, 2, 4, 6, 7, 5, 3, 1]
    turns = [
        (spots[p] * mp_size + m, spots[(p + (1 if m % 2 == 0 else -1)) % 8] * mp_size + m)
        for p in range(8)
        for m in range(mp_size)
    ]

    def around(value):
        return lax.ppermute(value, ("dp", "mp"), turns)

    def pair_up(shard, name):
        return call(
            pair_kernel, name, [((2,) + shard.shape, BF)], (), (shard, core_swap(shard))
        )[0]

    def last_hop(pair, name):
        (own,) = call(take_kernel, name, [(pair.shape[1:], BF)], (), (pair,))
        return around(own)

    def collect(shard, hops, swaps=None):
        swaps = swaps or [core_swap(hop) for hop in hops[:3]]
        return [shard] + hops[:3] + swaps + [hops[3]]

    def send_blocks(outs, bits):
        return (outs[0], swap(outs[1], "dp", 8, bits)) if quick else outs

    def fold(halves, bits, name, *first):
        if not quick:
            return halves
        keep, other = halves
        count, shape = keep.shape[0] // 2, keep.shape[1:]
        kinds = [((2,) + shape, BF)] * 2 if count == 2 else [(shape, F32), (shape, BF)]
        stay, send = call(fold_kernel, name, kinds, (), (gate(keep, *first), other))
        return stay, swap(send, "dp", 8, bits)

    def whole_sum(halves):
        return lax.psum_scatter(halves[0][0], "dp", scatter_dimension=0, tiled=True).astype(F32)

    def core_swap(value):
        return swap(value, "mp", mp_size, 1)

    def level_swap(value):
        return swap(value, "mp", mp_size, 2)

    def add_pair(one, two):
        return call(add_pair_kernel, "add_pair", [(one.shape, BF)], (), (one, two))[0]

    def mp_sum(send, keep):
        chip = add_pair(keep, core_swap(send))
        return chip, level_swap(chip)

    text = text_tokens.reshape(rows, model)
    image = image_tokens.reshape(image_rows, model)
    grad = out_grad.reshape(rows, model)

    if quick:
        (self_shard,) = call(
            pack_self_kernel, "pack_self", [((height, 4 * width), BF)], (), (self_qkv, self_out)
        )
        (cross_shard,) = call(
            pack_cross_kernel,
            "pack_cross",
            [((height, 4 * width), BF)],
            (),
            (cross_query, cross_keyval, cross_out),
        )
        (ffn_shard,) = call(
            pack_ffn_kernel, "pack_ffn", [((height, 2 * hidden), BF)], (), (mlp_up, mlp_down.T)
        )
        self_pair = pair_up(self_shard, "pairA")
        self_hops = [around(self_pair)]
        cross_hops = [around(pair_up(gate(cross_shard, self_pair), "pairB"))]
        for k in range(2):
            self_hops.append(around(self_hops[-1]))
            cross_hops.append(around(cross_hops[-1]))
        self_hops.append(last_hop(self_hops[-1], "takeA"))
        cross_hops.append(last_hop(cross_hops[-1], "takeB"))
        self_swaps = [core_swap(hop) for hop in self_hops[:3]]
        self_pieces = collect(self_shard, self_hops, self_swaps)
        cross_pieces = collect(cross_shard, cross_hops)
        ffn_pair = pair_up(gate(ffn_shard, self_hops[0]), "pairF")
        ffn_hops = [around(gate(ffn_pair, cross_hops[1]))]
        ffn_hops.append(around(ffn_hops[0]))
        text_in = gate(text, ffn_hops[0], cross_hops[2])
    else:
        gather = lambda shard: [lax.all_gather(shard, "dp", axis=0, tiled=True)]
        self_pieces = gather(
            jnp.concatenate([self_qkv[0], self_qkv[1], self_qkv[2], self_out.T], 1)
        )
        cross_pieces = gather(
            jnp.concatenate([cross_query, cross_keyval[0], cross_keyval[1], cross_out.T], 1)
        )
        text_in = text
        ffn_pieces = gather(jnp.concatenate([mlp_up, mlp_down.T], 1))

    square = ((model, width), BF)
    narrow = ((rows, width), BF)
    wide = ((rows, model), BF)
    halves = [((half, model), BF)] * 2
    half_f32 = ((half, model), F32)
    half_low = ((half, model), BF)
    heads = width // HEAD_DIM
    full = pltpu.VMEM((rows, model), F32)

    vmem = pl.BlockSpec(memory_space=pltpu.VMEM)
    smem = pl.BlockSpec(memory_space=pltpu.SMEM)
    hbm = pl.BlockSpec(memory_space=pltpu.HBM)
    w_self, saved, send, keep = pl.pallas_call(
        functools.partial(self_forward_kernel, len(self_pieces), seqs),
        out_shape=[
            jax.ShapeDtypeStruct((model, 4 * width), BF),
            jax.ShapeDtypeStruct((rows, 4 * width), BF),
            jax.ShapeDtypeStruct((half, model), BF),
            jax.ShapeDtypeStruct((half, model), BF),
        ],
        in_specs=[smem] + [vmem] * (3 + len(self_pieces)),
        out_specs=[hbm, hbm, vmem, vmem],
        scratch_shapes=[
            pltpu.VMEM((model, 4 * width), BF),
            pltpu.VMEM((rows, 4 * width), BF),
            full,
            pltpu.SemaphoreType.DMA((2,)),
        ],
        compiler_params=pltpu.CompilerParams(vmem_limit_bytes=VMEM_LIMIT),
        cost_estimate=COST,
        name="self_forward",
    )(text_lengths, text_in, norm_gain, norm_bias, *self_pieces)
    chip, other = mp_sum(send, keep)

    whole = lambda shape: pl.BlockSpec(shape, lambda b: (0,) * len(shape))
    per_seq = lambda b: (b, 0)
    cq, ck, cv, co, keys, values = pl.pallas_call(
        functools.partial(keyval_kernel, len(cross_pieces)),
        grid=(seqs,),
        out_shape=[jax.ShapeDtypeStruct((model, width), BF)] * 4
        + [jax.ShapeDtypeStruct((image_rows, width), BF)] * 2,
        in_specs=[pl.BlockSpec((patches, model), per_seq)]
        + [whole(piece.shape) for piece in cross_pieces],
        out_specs=[whole((model, width))] * 4 + [pl.BlockSpec((patches, width), per_seq)] * 2,
        compiler_params=pltpu.CompilerParams(vmem_limit_bytes=VMEM_LIMIT),
        cost_estimate=COST,
        name="keyval",
    )(image, *cross_pieces)

    hidden_one, normed_half = call(
        functools.partial(norm_kernel, 0, True),
        "norm_mid",
        [half_f32, half_low],
        (),
        (gate(chip, keys, ffn_hops[1]) if quick else chip, other, text, out_bias, norm_gain, norm_bias),
    )
    if quick:
        ffn_hops.append(around(gate(ffn_hops[1], normed_half)))
    normed_mid, xq, cross_prob, cross_ctx, send, keep = call(
        functools.partial(cross_forward_kernel, seqs),
        "cross_forward",
        [wide, narrow, ((seqs, heads * positions, patches), F32), narrow] + halves,
        (patch_counts,),
        (normed_half, core_swap(normed_half), cq, co, keys, values),
        [full],
        flops=2 * rows * model * width * 2,
    )
    chip, other = mp_sum(send, keep)
    if quick:
        ffn_hops.append(last_hop(gate(ffn_hops[2], chip), "takeF"))
        ffn_pieces = collect(ffn_shard, ffn_hops)
    w_up, w_down, grad_act = call(
        functools.partial(ffn_ready_kernel, len(ffn_pieces)),
        "ffn_ready",
        [((model, hidden), BF)] * 2 + [((rows, hidden), F32)],
        (),
        (grad, *ffn_pieces),
        flops=2 * rows * model * hidden,
    )
    hidden_two, normed_half = call(
        functools.partial(norm_kernel, 1, False),
        "norm_ffn",
        [half_f32, half_low],
        (),
        (chip, other, hidden_one, out_bias, norm_gain, norm_bias),
    )
    (normed_ffn, act, grad_low, up_sum, send, keep, out_send, out_keep) = call(
        ffn_kernel,
        "ffn",
        [wide, ((rows, hidden), BF), ((rows, hidden), BF), ((1, hidden), F32)] + halves + halves,
        (),
        (
            normed_half,
            core_swap(normed_half),
            w_up,
            w_down,
            grad_act,
            up_bias.reshape(1, hidden),
        ),
        [full],
        flops=2 * rows * model * hidden * 3,
    )
    chip, other = mp_sum(send, keep)

    ffn_blocks = call(
        functools.partial(ffn_weight_kernel, parts),
        "ffn_weights",
        [(blocks + (hidden,), BF)] * (2 * parts),
        (),
        (normed_ffn, grad_low, grad, act),
        [pltpu.VMEM((model, hidden), F32)],
        flops=2 * rows * model * hidden * 2,
    )
    up_sums = send_blocks(ffn_blocks[:parts], 2)
    down_sums = send_blocks(ffn_blocks[parts:], 1)
    vec_shape = ((8, model), F32)
    grad_two, low_half, vec_two = call(
        functools.partial(norm_back_kernel, 2, True),
        "norm_back_ffn",
        [half_f32, half_low, vec_shape],
        (),
        (gate(chip, *ffn_blocks), other, hidden_two, grad, norm_gain),
    )
    turned = ((width, image_rows), BF)
    grad_two_low, dq, dkt, dvt, send, keep = call(
        functools.partial(cross_back_kernel, seqs),
        "cross_back",
        [wide, narrow, turned, turned] + halves,
        (),
        (low_half, core_swap(low_half), cq, co, keys, values, xq, cross_prob),
        [full],
        flops=2 * rows * model * width * 2,
    )
    chip, other = mp_sum(send, keep)
    up_sums = fold(up_sums, 4, "fold_up", chip)
    down_sums = fold(down_sums, 2, "fold_down", up_sums[0])
    send_away, send_own, keep_away, keep_own = call(
        image_part_kernel,
        "image_part",
        [turned] * 4,
        (),
        (gate(dkt, chip), dvt, ck, cv),
    )

    cross_blocks = call(
        functools.partial(cross_weight_kernel, parts),
        "cross_weights",
        [(blocks + (4 * width,), BF)] * parts,
        (),
        (image, gate(dkt, down_sums[0]), dvt, normed_mid, dq, grad_two_low, cross_ctx),
        [pltpu.VMEM((model, width), F32)],
        flops=2 * image_rows * model * width * 2,
    )
    cross_sums = send_blocks(cross_blocks, 1)
    grad_one, low_half, vec_one = call(
        functools.partial(norm_back_kernel, 1, False),
        "norm_back_mid",
        [half_f32, half_low, vec_shape],
        (),
        (gate(chip, *cross_blocks), other, hidden_one, grad_two, norm_gain),
    )
    tall = ((rows + 16, model), BF)
    self_back = call(
        functools.partial(self_back_kernel, seqs, parts),
        "self_back",
        [(blocks + (4 * width,), BF)] * parts + [tall] * 2,
        (text_lengths,),
        (
            low_half,
            core_swap(low_half),
            text,
            norm_gain,
            norm_bias,
            w_self,
            saved,
            out_send,
            out_keep,
            vec_one,
            vec_two,
            up_sum,
        ),
        [
            pltpu.VMEM((rows, model), BF),
            pltpu.VMEM((3, rows, width), BF),
            full,
            pltpu.VMEM((model, width), F32),
            pltpu.VMEM((16, model), F32),
        ],
    )
    self_blocks, (send, keep) = self_back[:parts], self_back[parts:]
    self_sums = send_blocks(self_blocks, 1)
    chip_own, chip_away = call(
        image_chip_kernel,
        "image_chip",
        [((width, image_rows), F32), turned],
        (),
        (gate(keep_own, keep), core_swap(send_own), keep_away, core_swap(send_away)),
    )
    chip, other = mp_sum(send, gate(keep, chip_away))
    up_sums = fold(up_sums, 1, "fold_up", chip)
    cross_sums = fold(cross_sums, 2, "fold_cross", up_sums[0])
    down_sums = fold(down_sums, 4, "fold_down", cross_sums[0])
    text_half, out_half, vec = call(
        finish_kernel,
        "finish",
        [half_f32, half_low, ((16, model), BF)],
        (),
        (gate(chip, down_sums[0]), other, text, grad_one, norm_gain, hidden_two, out_bias),
    )
    image_away = level_swap(gate(chip_away, vec))
    if quick:
        low_rows = lambda count: ((count, 4 * width), BF)
        near, send, vec = call(
            fold_self_one_kernel,
            "fold_self",
            [low_rows(2 * height), low_rows(2 * height + 16), low_rows(16)],
            (),
            (*self_sums, vec, swap(vec, "dp", 8, 1)),
        )
        self_sums = near, swap(send, "dp", 8, 2)
        cross_sums = fold(cross_sums, 4, "fold_cross", near)
    text_grad, layer_out = call(
        join_both_kernel,
        "join",
        [((rows, model), F32), wide],
        (),
        (gate(text_half, cross_sums[0]), core_swap(text_half), out_half, core_swap(out_half)),
    )
    if quick:
        close = lambda sums, first, name: call(
            close_ffn_kernel, name, [((height, hidden), F32)], (), (gate(sums[0], first), sums[1])
        )[0]
        up_grad = close(up_sums, text_grad, "close_up")
        down_turned = close(down_sums, up_grad, "close_down")
        down_grad = down_turned.T
        near, send, vec = call(
            fold_self_two_kernel,
            "fold_self",
            [((height, 4 * width), F32), low_rows(height + 16), low_rows(16)],
            (),
            (gate(self_sums[0], down_turned), self_sums[1], vec),
        )
        self_sums = near, swap(send, "dp", 8, 4)
        query_grad, keyval_grad, cross_out_grad = call(
            close_cross_kernel,
            "close_cross",
            [((height, width), F32), ((2, height, width), F32), ((width, height), F32)],
            (),
            (gate(cross_sums[0], near), cross_sums[1]),
        )
    (image_grad,) = call(
        image_sum_kernel,
        "image_sum",
        [((seqs, width, patches), F32)],
        (),
        (gate(chip_own, cross_sums[0]), image_away),
    )
    vec_outs = [((3, model), F32)] * 3 + [((hidden,), F32)]
    if quick:
        qkv_grad, self_out_grad, gains, shifts, biases, ups = call(
            close_self_kernel,
            "close_self",
            [((3, height, width), F32), ((width, height), F32)] + vec_outs,
            (),
            (gate(self_sums[0], image_grad), self_sums[1], vec),
        )
    else:
        gains, shifts, biases, ups = call(
            vector_kernel, "close_vector", vec_outs, (), (lax.psum(vec.astype(F32), "dp"),)
        )
        total = whole_sum(self_sums)
        qkv_grad = jnp.stack([total[:, j * width : (j + 1) * width] for j in range(3)])
        self_out_grad = total[:, 3 * width :].T
        total = whole_sum(cross_sums)
        query_grad = total[:, :width]
        keyval_grad = jnp.stack([total[:, j * width : (j + 1) * width] for j in (1, 2)])
        cross_out_grad = total[:, 3 * width :].T
        up_grad, down_grad = whole_sum(up_sums), whole_sum(down_sums).T
    return (
        layer_out.reshape(seqs, positions, model),
        text_grad.reshape(seqs, positions, model),
        image_grad.transpose(0, 2, 1),
        qkv_grad,
        self_out_grad,
        query_grad,
        keyval_grad,
        cross_out_grad,
        up_grad,
        down_grad,
        gains,
        shifts,
        biases,
        ups.reshape(hidden),
    )


def solution(mesh):
    placed = (
        P("dp", None, None),
        P("dp", None, None),
        P("dp"),
        P("dp"),
        P(None, "dp", "mp"),
        P("mp", "dp"),
        P("dp", "mp"),
        P(None, "dp", "mp"),
        P("mp", "dp"),
        P("dp", "mp"),
        P("mp", "dp"),
        P(),
        P(),
        P(),
        P("mp"),
        P("dp", None, None),
    )
    return jax.shard_map(
        functools.partial(per_device, mesh.shape["dp"], mesh.shape["mp"]),
        mesh=mesh,
        in_specs=placed,
        out_specs=(
            P("dp", None, None),
            P("dp", None, None),
            P("dp", None, "mp"),
            P(None, "dp", "mp"),
            P("mp", "dp"),
            P("dp", "mp"),
            P(None, "dp", "mp"),
            P("mp", "dp"),
            P("dp", "mp"),
            P("mp", "dp"),
            P(),
            P(),
            P(),
            P("mp"),
        ),
        check_vma=False,
    )
```

```python
import functools
import math

import jax
import jax.numpy as jnp
from jax import lax
from jax.experimental import pallas as pl
from jax.experimental.pallas import tpu as pltpu
from jax.sharding import PartitionSpec as P

BF = jnp.bfloat16
F32 = jnp.float32
HEAD_DIM = 64
SCALE = HEAD_DIM ** (-0.5)
NORM_EPS = 1e-05
NEG_FILL = -1e30
INV_ROOT_TWO = 1.0 / math.sqrt(2.0)
INV_ROOT_TAU = 1.0 / math.sqrt(2.0 * math.pi)
VMEM_LIMIT = 24 * 1024 * 1024
COST_PER_BYTE = 1
COST = pl.CostEstimate(flops=1, bytes_accessed=10**7, transcendentals=0)


def nn(a, b):
    return lax.dot_general(a, b, (((1,), (0,)), ((), ())), preferred_element_type=F32)


def nt(a, b):
    return lax.dot_general(a, b, (((1,), (1,)), ((), ())), preferred_element_type=F32)


def tn(a, b):
    return lax.dot_general(a, b, (((0,), (0,)), ((), ())), preferred_element_type=F32)


def norm_parts(values):
    centered = values - jnp.mean(values, axis=-1, keepdims=True)
    inv_std = lax.rsqrt(jnp.mean(centered * centered, axis=-1, keepdims=True) + NORM_EPS)
    return centered * inv_std, inv_std


def norm_back(grad, normed, inv_std, gain_row):
    scaled = grad * gain_row
    first = jnp.mean(scaled, axis=-1, keepdims=True)
    second = jnp.mean(scaled * normed, axis=-1, keepdims=True)
    return inv_std * (scaled - first - normed * second)


def head_masks(width, kind):
    column = lax.broadcasted_iota(jnp.int32, (1, width), 1) // HEAD_DIM
    return [(column == h).astype(F32).astype(kind) for h in range(width // HEAD_DIM)]


def stack_heads(rows, masks):
    return jnp.concatenate([rows * m for m in masks], axis=0)


def unstack_heads(stacked, masks):
    count = stacked.shape[0] // len(masks)
    total = stacked[:count] * masks[0]
    for h in range(1, len(masks)):
        total = total + stacked[h * count : (h + 1) * count] * masks[h]
    return total


def call(body, name, outs, scalars, arrays, scratch=(), flops=0):
    nbytes = sum(a.size * a.dtype.itemsize for a in arrays)
    nbytes += sum(math.prod(s) * jnp.dtype(d).itemsize for s, d in outs)
    return pl.pallas_call(
        body,
        out_shape=[jax.ShapeDtypeStruct(s, d) for s, d in outs],
        in_specs=[pl.BlockSpec(memory_space=pltpu.SMEM)] * len(scalars)
        + [pl.BlockSpec(memory_space=pltpu.VMEM)] * len(arrays),
        out_specs=[pl.BlockSpec(memory_space=pltpu.VMEM)] * len(outs),
        scratch_shapes=list(scratch),
        compiler_params=pltpu.CompilerParams(vmem_limit_bytes=VMEM_LIMIT),
        cost_estimate=pl.CostEstimate(
            flops=1, bytes_accessed=int(nbytes * COST_PER_BYTE) + 1, transcendentals=0
        ),
        name=name,
    )(*scalars, *arrays)


def turns_of(one, two, three):
    return [a ^ b ^ c for a in (0, one) for c in (0, three) for b in (0, two)]


X_FIRST = (1, 2, 4)
Z_FIRST = (2, 4, 1)


def block_rows(turn, height):
    at = (lax.axis_index("dp") ^ turn) * height
    return pl.ds(pl.multiple_of(at, 32), height)


def half_rows(height, away=False):
    core = lax.axis_index("mp") & 1
    at = (1 - core if away else core) * height
    return pl.ds(pl.multiple_of(at, 128), height)


def ring_rows(hops, height):
    index = lax.axis_index("dp")
    spot = jnp.where((index & 1) == 0, index >> 1, 7 - (index >> 1))
    spot = (spot + hops + 8) & 7
    at = jnp.where(spot < 4, 2 * spot, 15 - 2 * spot) * height
    return pl.ds(pl.multiple_of(at, 32), height)


def place_pieces(pieces, targets):
    if len(pieces) == 1:
        blocks = [(slice(None), pieces[0])]
    else:
        height = pieces[0].shape[0]
        side = 2 * (lax.axis_index("mp") & 1) - 1
        blocks = [(ring_rows(0, height), pieces[0]), (ring_rows(4, height), pieces[7])]
        for k in (1, 2, 3):
            blocks.append((ring_rows(side * k, height), pieces[k].at[0]))
            blocks.append((ring_rows(-side * k, height), pieces[3 + k].at[1]))
    for rows, piece in blocks:
        start = 0
        for target in targets:
            width = target.shape[1]
            target[rows, :] = piece[:, start : start + width]
            start += width


def join_halves(own, other, target):
    half = own.shape[0]
    target[half_rows(half), :] = own[...]
    target[half_rows(half, True), :] = other[...]


def split_halves(full, send, keep):
    half = full.shape[0] // 2
    keep[:half] = full[half_rows(half), :].astype(keep.dtype)
    send[:half] = full[half_rows(half, True), :].astype(send.dtype)


def pack_self_kernel(qkv, out, packed):
    width = qkv.shape[2]
    for j in range(3):
        packed[:, j * width : (j + 1) * width] = qkv[j]
    packed[:, 3 * width :] = out[...].astype(F32).T.astype(BF)


def pack_cross_kernel(query, keyval, out, cross):
    width = query.shape[1]
    cross[:, :width] = query[...]
    cross[:, width : 2 * width] = keyval[0]
    cross[:, 2 * width : 3 * width] = keyval[1]
    cross[:, 3 * width :] = out[...].astype(F32).T.astype(BF)


def pack_ffn_kernel(up, down, ffn):
    hidden = up.shape[1]
    ffn[:, :hidden] = up[...]
    ffn[:, hidden:] = down[...]


def pair_kernel(own, other, out):
    out[0] = own[...]
    out[1] = other[...]


def take_kernel(pair, out):
    out[...] = pair[0]


def self_forward_kernel(
    count, seqs, lens, text, gain, bias, *refs
):
    pieces, (weights, saved, send, keep, w, qkv, full, sems) = refs[:count], refs[count:]
    place_pieces(pieces, (w,))
    save_w = pltpu.make_async_copy(w, weights, sems.at[0])
    save_w.start()
    n, _ = norm_parts(text[...].astype(F32))
    low = (n * gain[0:1] + bias[0:1]).astype(BF)
    width = w.shape[1] // 4
    qkv[:, : 3 * width] = nn(low, w[:, : 3 * width]).astype(BF)
    low_masks, masks = head_masks(width, BF), head_masks(width, F32)
    rows = text.shape[0] // seqs
    for b in range(seqs):
        at = slice(b * rows, (b + 1) * rows)
        q_stack = stack_heads(qkv[at, :width], low_masks)
        p = self_softmax(q_stack, qkv[at, width : 2 * width], lens[b], rows)
        qkv[at, 3 * width :] = unstack_heads(
            nn(p.astype(BF), qkv[at, 2 * width : 3 * width]), masks
        ).astype(BF)
    save_q = pltpu.make_async_copy(qkv, saved, sems.at[1])
    save_q.start()
    full[...] = nt(qkv[:, 3 * width :], w[:, 3 * width :])
    split_halves(full, send, keep)
    save_w.wait()
    save_q.wait()


def self_softmax(q_stack, keys, length, rows):
    shape = (q_stack.shape[0], rows)
    query_at = lax.broadcasted_iota(jnp.int32, shape, 0) % rows
    key_at = lax.broadcasted_iota(jnp.int32, shape, 1)
    allowed = (key_at <= query_at) & (key_at < length)
    scores = jnp.where(allowed, nt(q_stack, keys) * SCALE, NEG_FILL)
    raised = jnp.exp(scores - jnp.max(scores, axis=-1, keepdims=True))
    return raised / jnp.sum(raised, axis=-1, keepdims=True)


def keyval_kernel(count, image, *refs):
    pieces, (wq, wk, wv, wo, keys, values) = refs[:count], refs[count:]

    @pl.when(pl.program_id(0) == 0)
    def _():
        place_pieces(pieces, (wq, wk, wv, wo))

    keys[...] = nn(image[...], wk[...]).astype(BF)
    values[...] = nn(image[...], wv[...]).astype(BF)


def norm_kernel(index, sliced, chip, other, resid, out_bias, gain, bias, hidden, normed):
    half = chip.shape[0]
    if sliced:
        base = resid[half_rows(half), :].astype(F32)
    else:
        base = resid[...]
    value = (
        base
        + (chip[...].astype(F32) + other[...].astype(F32))
        + out_bias[index : index + 1]
    )
    hidden[...] = value
    n, _ = norm_parts(value)
    normed[...] = (n * gain[index + 1 : index + 2] + bias[index + 1 : index + 2]).astype(BF)


def cross_forward_kernel(
    seqs, counts, own, other, wq, wo, keys, values, normed, q, prob, ctx, send, keep, full
):
    join_halves(own, other, normed)
    q[...] = nn(normed[...], wq[...]).astype(BF)
    width = q.shape[1]
    low_masks, masks = head_masks(width, BF), head_masks(width, F32)
    rows = normed.shape[0] // seqs
    patches = keys.shape[0] // seqs
    patch_at = lax.broadcasted_iota(jnp.int32, (rows * len(masks), patches), 1)
    for b in range(seqs):
        at = slice(b * rows, (b + 1) * rows)
        ks = slice(b * patches, (b + 1) * patches)
        scores = nt(stack_heads(q[at], low_masks), keys[ks]) * SCALE
        scores = jnp.where(patch_at < counts[b], scores, NEG_FILL)
        raised = jnp.exp(scores - jnp.max(scores, axis=-1, keepdims=True))
        p = raised / jnp.sum(raised, axis=-1, keepdims=True)
        prob[b] = p
        ctx[at] = unstack_heads(nn(p.astype(BF), values[ks]), masks).astype(BF)
    full[...] = nt(ctx[...], wo[...])
    split_halves(full, send, keep)


def ffn_ready_kernel(count, grad, *refs):
    pieces, (up, down, grad_act) = refs[:count], refs[count:]
    place_pieces(pieces, (up, down))
    grad_act[...] = nn(grad[...], down[...])


def ffn_kernel(
    own, other, up, down, grad_act, up_bias,
    normed, act, grad_low, bias_sum, send, keep, out_send, out_keep, full,
):
    join_halves(own, other, normed)
    pre = nn(normed[...], up[...]) + up_bias[...]
    cdf = 0.5 * (1.0 + lax.erf(pre * INV_ROOT_TWO))
    density = jnp.exp(-0.5 * pre * pre) * INV_ROOT_TAU
    grad_pre = grad_act[...] * (cdf + pre * density)
    grad_low[...] = grad_pre.astype(BF)
    act[...] = (pre * cdf).astype(BF)
    bias_sum[...] = jnp.sum(grad_pre, axis=0, keepdims=True)
    full[...] = nt(grad_low[...], up[...])
    split_halves(full, send, keep)
    full[...] = nt(act[...], down[...])
    split_halves(full, out_send, out_keep)


def scatter_blocks(matrix, column, outs, order=X_FIRST):
    blocks = sum(o.shape[0] for o in outs)
    height = outs[0].shape[1]
    width = matrix.shape[1]
    turns = turns_of(*order)
    for k in range(blocks):
        rows = block_rows(turns[k], height) if blocks > 1 else slice(None)
        target = outs[k // outs[0].shape[0]]
        target[k % outs[0].shape[0], :, column : column + width] = matrix[rows, :].astype(BF)


def ffn_weight_kernel(parts, normed, grad_low, grad, act, *refs):
    ups, downs, full = refs[:parts], refs[parts : 2 * parts], refs[2 * parts]
    full[...] = tn(normed[...], grad_low[...])
    scatter_blocks(full, 0, ups, Z_FIRST)
    full[...] = tn(grad[...], act[...])
    scatter_blocks(full, 0, downs)


def norm_back_kernel(index, sliced, chip, other, hidden, resid, gain, total, low, vec):
    half = chip.shape[0]
    if sliced:
        base = resid[half_rows(half), :].astype(F32)
    else:
        base = resid[...]
    grad = chip[...].astype(F32) + other[...].astype(F32)
    n, inv_std = norm_parts(hidden[...])
    value = base + norm_back(grad, n, inv_std, gain[index : index + 1])
    total[...] = value
    low[...] = value.astype(BF)
    vec[...] = jnp.zeros_like(vec)
    vec[0:1] = 0.5 * jnp.sum(grad * n, axis=0, keepdims=True)
    vec[1:2] = 0.5 * jnp.sum(grad, axis=0, keepdims=True)
    vec[2:3] = 0.5 * jnp.sum(value, axis=0, keepdims=True)
    if sliced:
        vec[3:4] = 0.5 * jnp.sum(base, axis=0, keepdims=True)


def score_grad(p, values, grad_stack):
    grad_p = nt(grad_stack, values)
    inner = jnp.sum(p * grad_p, axis=-1, keepdims=True)
    return (p * (grad_p - inner)).astype(BF)


def cross_back_kernel(
    seqs, own, other, wq, wo, keys, values, q, prob, grad_two, dq, dkt, dvt, send, keep, full
):
    join_halves(own, other, grad_two)
    grad_ctx = nn(grad_two[...], wo[...]).astype(BF)
    width = q.shape[1]
    low_masks, masks = head_masks(width, BF), head_masks(width, F32)
    rows = q.shape[0] // seqs
    patches = keys.shape[0] // seqs
    for b in range(seqs):
        at = slice(b * rows, (b + 1) * rows)
        ks = slice(b * patches, (b + 1) * patches)
        p = prob[b]
        q_stack = stack_heads(q[at], low_masks)
        grad_stack = stack_heads(grad_ctx[at], low_masks)
        ds = score_grad(p, values[ks], grad_stack)
        dq[at] = unstack_heads(nn(ds, keys[ks]) * SCALE, masks).astype(BF)
        dkt[:, ks] = (tn(q_stack, ds) * SCALE).astype(BF)
        dvt[:, ks] = tn(grad_stack, p.astype(BF)).astype(BF)
    full[...] = nt(dq[...], wq[...])
    split_halves(full, send, keep)


def cross_weight_kernel(parts, image, dkt, dvt, normed, dq, grad_two, ctx, *refs):
    outs, turned = refs[:parts], refs[parts]
    width = dq.shape[1]
    turned[...] = tn(normed[...], dq[...])
    scatter_blocks(turned, 0, outs)
    turned[...] = nn(dkt[...], image[...]).T
    scatter_blocks(turned, width, outs)
    turned[...] = nn(dvt[...], image[...]).T
    scatter_blocks(turned, 2 * width, outs)
    turned[...] = tn(grad_two[...], ctx[...])
    scatter_blocks(turned, 3 * width, outs)


def image_part_kernel(dkt, dvt, wk, wv, away_one, away_two, own_one, own_two, keep_away, keep_own):
    width = wk.shape[1]
    core, level = lax.axis_index("mp") & 1, lax.axis_index("mp") >> 1
    half = own_one.shape[1]
    for k, targets in enumerate(
        ((keep_own,), (keep_away,), (own_one, own_two), (away_one, away_two))
    ):
        at = (2 * (level ^ (k & 1)) + (core ^ (k >> 1))) * width
        rows = pl.ds(pl.multiple_of(at, 64), width)
        part = (nn(wk[rows, :], dkt[...]) + nn(wv[rows, :], dvt[...])).astype(BF)
        if len(targets) == 1:
            targets[0][...] = part
        else:
            targets[0][...] = part[:, :half]
            targets[1][...] = part[:, half:]


def add_pair_kernel(one, two, out):
    out[...] = (one[...].astype(F32) + two[...].astype(F32)).astype(BF)


def add_halves_kernel(keep, one, two, out):
    half = one.shape[1]
    out[:, :half] = (keep[:, :half].astype(F32) + one[...].astype(F32)).astype(BF)
    out[:, half:] = (keep[:, half:].astype(F32) + two[...].astype(F32)).astype(BF)


def image_sum_kernel(keep, one, two, away, out):
    patches = out.shape[2]
    per = one.shape[1] // patches
    for b in range(out.shape[0]):
        ks = slice(b * patches, (b + 1) * patches)
        part = one if b < per else two
        ps = slice((b % per) * patches, (b % per + 1) * patches)
        out[b] = keep[:, ks].astype(F32) + part[:, ps].astype(F32) + away[:, ks].astype(F32)


def self_back_kernel(
    seqs, parts, lens, own, other, text, gain, bias, w, qkv,
    one, two, ups, *refs
):
    outs = refs[:parts]
    send, keep, low, dqkv, full, narrow, vec = refs[parts:]
    join_halves(own, other, low)
    width = w.shape[1] // 4
    grad_ctx = nn(low[...], w[:, 3 * width :]).astype(BF)
    low_masks, masks = head_masks(width, BF), head_masks(width, F32)
    rows = text.shape[0] // seqs
    for b in range(seqs):
        at = slice(b * rows, (b + 1) * rows)
        q_stack = stack_heads(qkv[at, :width], low_masks)
        keys = qkv[at, width : 2 * width]
        p = self_softmax(q_stack, keys, lens[b], rows)
        grad_stack = stack_heads(grad_ctx[at], low_masks)
        ds = score_grad(p, qkv[at, 2 * width : 3 * width], grad_stack)
        dqkv[0, at] = unstack_heads(nn(ds, keys) * SCALE, masks).astype(BF)
        dqkv[1, at] = (tn(ds, q_stack) * SCALE).astype(BF)
        dqkv[2, at] = tn(p.astype(BF), grad_stack).astype(BF)
    n, _ = norm_parts(text[...].astype(F32))
    normed = (n * gain[0:1] + bias[0:1]).astype(BF)
    for j in range(3):
        narrow[...] = tn(normed, dqkv[j])
        scatter_blocks(narrow, j * width, outs)
    narrow[...] = tn(low[...], qkv[:, 3 * width :])
    scatter_blocks(narrow, 3 * width, outs)
    part = nt(dqkv[0], w[:, :width])
    for j in (1, 2):
        part = part + nt(dqkv[j], w[:, j * width : (j + 1) * width])
    full[...] = part
    split_halves(full, send, keep)
    half = own.shape[0]
    vec[...] = jnp.zeros_like(vec)
    vec[0:1] = jnp.sum(part * n, axis=0, keepdims=True)
    vec[1:2], vec[2:3] = one[0:1], two[0:1]
    vec[3:4] = jnp.sum(part, axis=0, keepdims=True)
    vec[4:5], vec[5:6] = one[1:2], two[1:2]
    vec[6:7], vec[7:8], vec[8:9] = one[2:3], two[2:3], two[3:4]
    vec[pl.ds(9 + lax.axis_index("mp"), 1), :] = ups[...]
    send[half:] = vec[...].astype(BF)
    keep[half:] = vec[...].astype(BF)


def finish_kernel(chip, other, text, resid, gain, grad_out, vec):
    half = resid.shape[0]
    grad = chip[:half].astype(F32) + other[:half].astype(F32)
    base = text[half_rows(half), :].astype(F32)
    n, inv_std = norm_parts(base)
    grad_out[...] = resid[...] + norm_back(grad, n, inv_std, gain[0:1])
    vec[...] = (chip[half:].astype(F32) + other[half:].astype(F32)).astype(BF)


def layer_out_kernel(chip, other, hidden, out_bias, out):
    out[...] = (
        hidden[...] + (chip[...].astype(F32) + other[...].astype(F32)) + out_bias[2:3]
    ).astype(BF)


def join_both_kernel(own, other, own_low, other_low, out, out_low):
    join_halves(own, other, out)
    join_halves(own_low, other_low, out_low)


def fold_kernel(keep, other, stay, send):
    for k in range(keep.shape[0]):
        target = send if k % 2 else stay
        value = (keep[k].astype(F32) + other[k].astype(F32)).astype(target.dtype)
        if len(target.shape) == 3:
            target[k // 2] = value
        else:
            target[...] = value


def fold_self_one_kernel(keep, other, vec, vec_other, stay, send, vec_sum):
    height = keep.shape[1]
    for k in range(4):
        value = (keep[k].astype(F32) + other[k].astype(F32)).astype(BF)
        at = (k // 2) * height
        (send if k % 2 else stay)[at : at + height] = value
    total = (vec[...].astype(F32) + vec_other[...].astype(F32)).astype(BF)
    vec_sum[...] = total
    send[2 * height :] = total


def fold_self_two_kernel(keep, other, vec, stay, send, vec_sum):
    height = stay.shape[0]
    stay[...] = keep[:height].astype(F32) + other[:height].astype(F32)
    rest = slice(height, 2 * height)
    send[:height] = (keep[rest].astype(F32) + other[rest].astype(F32)).astype(BF)
    total = (vec[...].astype(F32) + other[2 * height :].astype(F32)).astype(BF)
    vec_sum[...] = total
    send[height:] = total


def vector_parts(total, gains, shifts, biases, ups):
    gains[...] = total[0:3]
    shifts[...] = total[3:6]
    biases[...] = total[6:9]
    full = total[9]
    for k in range(1, 4):
        full = jnp.where(lax.axis_index("mp") == k, total[9 + k], full)
    ups[...] = full


def vector_kernel(vec, gains, shifts, biases, ups):
    vector_parts(vec[...], gains, shifts, biases, ups)


def close_cross_kernel(*refs):
    own, other, query, keyval, out = refs
    total = own[...] + other[...].astype(F32)
    width = out.shape[0]
    query[...] = total[:, :width]
    keyval[0] = total[:, width : 2 * width]
    keyval[1] = total[:, 2 * width : 3 * width]
    out[...] = total[:, 3 * width :].T


def close_ffn_kernel(own, other, out):
    out[...] = own[...] + other[...].astype(F32)


def close_self_kernel(own, other, vec, qkv, out, gains, shifts, biases, ups):
    height = own.shape[0]
    total = own[...] + other[:height].astype(F32)
    width = out.shape[0]
    for j in range(3):
        qkv[j] = total[:, j * width : (j + 1) * width]
    out[...] = total[:, 3 * width :].T
    vector_parts(vec[...].astype(F32) + other[height:].astype(F32), gains, shifts, biases, ups)


def swap(value, axis, size, bits):
    return lax.ppermute(value, axis, [(i, i ^ bits) for i in range(size)])


def gate_all(values, *first):
    return list(lax.optimization_barrier((*values, *first)))[: len(values)]


def gate(value, *first):
    return lax.optimization_barrier((value, *first))[0]


def per_device(
    dp_size,
    mp_size,
    text_tokens,
    image_tokens,
    text_lengths,
    patch_counts,
    self_qkv,
    self_out,
    cross_query,
    cross_keyval,
    cross_out,
    mlp_up,
    mlp_down,
    norm_gain,
    norm_bias,
    out_bias,
    up_bias,
    out_grad,
):
    seqs, positions, model = text_tokens.shape
    patches = image_tokens.shape[1]
    rows = seqs * positions
    half = rows // 2
    width = cross_query.shape[1]
    hidden = mlp_up.shape[1]
    image_rows = seqs * patches
    quick = dp_size == 8
    height = model // dp_size
    parts, blocks = (2, (4, height)) if quick else (1, (1, model))

    spots = [0, 2, 4, 6, 7, 5, 3, 1]
    turns = [
        (spots[p] * mp_size + m, spots[(p + (1 if m % 2 == 0 else -1)) % 8] * mp_size + m)
        for p in range(8)
        for m in range(mp_size)
    ]

    def around(value):
        return lax.ppermute(value, ("dp", "mp"), turns)

    def pair_up(shard, name):
        return call(
            pair_kernel, name, [((2,) + shard.shape, BF)], (), (shard, core_swap(shard))
        )[0]

    def last_hop(pair, name):
        (own,) = call(take_kernel, name, [(pair.shape[1:], BF)], (), (pair,))
        return around(own)

    def collect(shard, hops, swaps=None):
        swaps = swaps or [core_swap(hop) for hop in hops[:3]]
        return [shard] + hops[:3] + swaps + [hops[3]]

    def send_blocks(outs, bits):
        return (outs[0], swap(outs[1], "dp", 8, bits)) if quick else outs

    def fold(halves, bits, name, *first):
        if not quick:
            return halves
        keep, other = halves
        count, shape = keep.shape[0] // 2, keep.shape[1:]
        kinds = [((2,) + shape, BF)] * 2 if count == 2 else [(shape, F32), (shape, BF)]
        stay, send = call(fold_kernel, name, kinds, (), (gate(keep, *first), other))
        return stay, swap(send, "dp", 8, bits)

    def whole_sum(halves):
        return lax.psum_scatter(halves[0][0], "dp", scatter_dimension=0, tiled=True).astype(F32)

    def core_swap(value):
        return swap(value, "mp", mp_size, 1)

    def level_swap(value):
        return swap(value, "mp", mp_size, 2)

    def add_pair(one, two):
        return call(add_pair_kernel, "add_pair", [(one.shape, BF)], (), (one, two))[0]

    def mp_sum(send, keep):
        chip = add_pair(keep, core_swap(send))
        return chip, level_swap(chip)

    text = text_tokens.reshape(rows, model)
    image = image_tokens.reshape(image_rows, model)
    grad = out_grad.reshape(rows, model)

    if quick:
        (self_shard,) = call(
            pack_self_kernel, "pack_self", [((height, 4 * width), BF)], (), (self_qkv, self_out)
        )
        (cross_shard,) = call(
            pack_cross_kernel,
            "pack_cross",
            [((height, 4 * width), BF)],
            (),
            (cross_query, cross_keyval, cross_out),
        )
        (ffn_shard,) = call(
            pack_ffn_kernel, "pack_ffn", [((height, 2 * hidden), BF)], (), (mlp_up, mlp_down.T)
        )
        self_pair = pair_up(self_shard, "pairA")
        self_hops = [around(self_pair)]
        cross_hops = [around(pair_up(gate(cross_shard, self_pair), "pairB"))]
        for k in range(2):
            self_hops.append(around(self_hops[-1]))
            cross_hops.append(around(cross_hops[-1]))
        self_hops.append(last_hop(self_hops[-1], "takeA"))
        cross_hops.append(last_hop(cross_hops[-1], "takeB"))
        self_swaps = [core_swap(hop) for hop in self_hops[:3]]
        self_pieces = collect(self_shard, self_hops, self_swaps)
        cross_pieces = collect(cross_shard, cross_hops)
        ffn_pair = pair_up(gate(ffn_shard, self_hops[0]), "pairF")
        ffn_hops = [around(gate(ffn_pair, cross_hops[1]))]
        ffn_hops.append(around(ffn_hops[0]))
        text_in = gate(text, ffn_hops[0], cross_hops[2])
    else:
        gather = lambda shard: [lax.all_gather(shard, "dp", axis=0, tiled=True)]
        self_pieces = gather(
            jnp.concatenate([self_qkv[0], self_qkv[1], self_qkv[2], self_out.T], 1)
        )
        cross_pieces = gather(
            jnp.concatenate([cross_query, cross_keyval[0], cross_keyval[1], cross_out.T], 1)
        )
        text_in = text
        ffn_pieces = gather(jnp.concatenate([mlp_up, mlp_down.T], 1))

    square = ((model, width), BF)
    narrow = ((rows, width), BF)
    wide = ((rows, model), BF)
    halves = [((half, model), BF)] * 2
    half_f32 = ((half, model), F32)
    half_low = ((half, model), BF)
    heads = width // HEAD_DIM
    full = pltpu.VMEM((rows, model), F32)

    vmem = pl.BlockSpec(memory_space=pltpu.VMEM)
    smem = pl.BlockSpec(memory_space=pltpu.SMEM)
    hbm = pl.BlockSpec(memory_space=pltpu.HBM)
    w_self, saved, send, keep = pl.pallas_call(
        functools.partial(self_forward_kernel, len(self_pieces), seqs),
        out_shape=[
            jax.ShapeDtypeStruct((model, 4 * width), BF),
            jax.ShapeDtypeStruct((rows, 4 * width), BF),
            jax.ShapeDtypeStruct((half, model), BF),
            jax.ShapeDtypeStruct((half, model), BF),
        ],
        in_specs=[smem] + [vmem] * (3 + len(self_pieces)),
        out_specs=[hbm, hbm, vmem, vmem],
        scratch_shapes=[
            pltpu.VMEM((model, 4 * width), BF),
            pltpu.VMEM((rows, 4 * width), BF),
            full,
            pltpu.SemaphoreType.DMA((2,)),
        ],
        compiler_params=pltpu.CompilerParams(vmem_limit_bytes=VMEM_LIMIT),
        cost_estimate=COST,
        name="self_forward",
    )(text_lengths, text_in, norm_gain, norm_bias, *self_pieces)
    chip, other = mp_sum(send, keep)

    whole = lambda shape: pl.BlockSpec(shape, lambda b: (0,) * len(shape))
    per_seq = lambda b: (b, 0)
    cq, ck, cv, co, keys, values = pl.pallas_call(
        functools.partial(keyval_kernel, len(cross_pieces)),
        grid=(seqs,),
        out_shape=[jax.ShapeDtypeStruct((model, width), BF)] * 4
        + [jax.ShapeDtypeStruct((image_rows, width), BF)] * 2,
        in_specs=[pl.BlockSpec((patches, model), per_seq)]
        + [whole(piece.shape) for piece in cross_pieces],
        out_specs=[whole((model, width))] * 4 + [pl.BlockSpec((patches, width), per_seq)] * 2,
        compiler_params=pltpu.CompilerParams(vmem_limit_bytes=VMEM_LIMIT),
        cost_estimate=COST,
        name="keyval",
    )(image, *cross_pieces)

    hidden_one, normed_half = call(
        functools.partial(norm_kernel, 0, True),
        "norm_mid",
        [half_f32, half_low],
        (),
        (gate(chip, keys, ffn_hops[1]) if quick else chip, other, text, out_bias, norm_gain, norm_bias),
    )
    if quick:
        ffn_hops.append(around(gate(ffn_hops[1], normed_half)))
    normed_mid, xq, cross_prob, cross_ctx, send, keep = call(
        functools.partial(cross_forward_kernel, seqs),
        "cross_forward",
        [wide, narrow, ((seqs, heads * positions, patches), F32), narrow] + halves,
        (patch_counts,),
        (normed_half, core_swap(normed_half), cq, co, keys, values),
        [full],
        flops=2 * rows * model * width * 2,
    )
    chip, other = mp_sum(send, keep)
    if quick:
        ffn_hops.append(last_hop(gate(ffn_hops[2], chip), "takeF"))
        ffn_pieces = collect(ffn_shard, ffn_hops)
    w_up, w_down, grad_act = call(
        functools.partial(ffn_ready_kernel, len(ffn_pieces)),
        "ffn_ready",
        [((model, hidden), BF)] * 2 + [((rows, hidden), F32)],
        (),
        (grad, *ffn_pieces),
        flops=2 * rows * model * hidden,
    )
    hidden_two, normed_half = call(
        functools.partial(norm_kernel, 1, False),
        "norm_ffn",
        [half_f32, half_low],
        (),
        (chip, other, hidden_one, out_bias, norm_gain, norm_bias),
    )
    (normed_ffn, act, grad_low, up_sum, send, keep, out_send, out_keep) = call(
        ffn_kernel,
        "ffn",
        [wide, ((rows, hidden), BF), ((rows, hidden), BF), ((1, hidden), F32)] + halves + halves,
        (),
        (
            normed_half,
            core_swap(normed_half),
            w_up,
            w_down,
            grad_act,
            up_bias.reshape(1, hidden),
        ),
        [full],
        flops=2 * rows * model * hidden * 3,
    )
    chip, other = mp_sum(send, keep)

    ffn_blocks = call(
        functools.partial(ffn_weight_kernel, parts),
        "ffn_weights",
        [(blocks + (hidden,), BF)] * (2 * parts),
        (),
        (normed_ffn, grad_low, grad, act),
        [pltpu.VMEM((model, hidden), F32)],
        flops=2 * rows * model * hidden * 2,
    )
    up_sums = send_blocks(ffn_blocks[:parts], 2)
    down_sums = send_blocks(ffn_blocks[parts:], 1)
    vec_shape = ((8, model), F32)
    grad_two, low_half, vec_two = call(
        functools.partial(norm_back_kernel, 2, True),
        "norm_back_ffn",
        [half_f32, half_low, vec_shape],
        (),
        (gate(chip, *ffn_blocks), other, hidden_two, grad, norm_gain),
    )
    turned = ((width, image_rows), BF)
    grad_two_low, dq, dkt, dvt, send, keep = call(
        functools.partial(cross_back_kernel, seqs),
        "cross_back",
        [wide, narrow, turned, turned] + halves,
        (),
        (low_half, core_swap(low_half), cq, co, keys, values, xq, cross_prob),
        [full],
        flops=2 * rows * model * width * 2,
    )
    turned_half = ((width, image_rows // 2), BF)
    away_one, away_two, own_one, own_two, keep_away, keep_own = call(
        image_part_kernel,
        "image_part",
        [turned_half] * 4 + [turned] * 2,
        (),
        (dkt, dvt, ck, cv),
    )
    chip, other = mp_sum(send, gate(keep, keep_own))
    up_sums = fold(up_sums, 4, "fold_up", chip)
    down_sums = fold(down_sums, 2, "fold_down", up_sums[0])
    cross_blocks = call(
        functools.partial(cross_weight_kernel, parts),
        "cross_weights",
        [(blocks + (4 * width,), BF)] * parts,
        (),
        (image, gate(dkt, down_sums[0]), dvt, normed_mid, dq, grad_two_low, cross_ctx),
        [pltpu.VMEM((model, width), F32)],
        flops=2 * image_rows * model * width * 2,
    )
    cross_sums = send_blocks(cross_blocks, 1)
    grad_one, low_half, vec_one = call(
        functools.partial(norm_back_kernel, 1, False),
        "norm_back_mid",
        [half_f32, half_low, vec_shape],
        (),
        (gate(chip, *cross_blocks), other, hidden_one, grad_two, norm_gain),
    )
    (chip_away,) = call(
        add_halves_kernel,
        "image_chip",
        [turned],
        (),
        (gate(keep_away, low_half), core_swap(away_one), core_swap(away_two)),
    )
    tall = ((half + 16, model), BF)
    self_back = call(
        functools.partial(self_back_kernel, seqs, parts),
        "self_back",
        [(blocks + (4 * width,), BF)] * parts + [tall] * 2,
        (text_lengths,),
        (
            low_half,
            core_swap(low_half),
            gate(text, chip_away),
            norm_gain,
            norm_bias,
            w_self,
            saved,
            vec_one,
            vec_two,
            up_sum,
        ),
        [
            pltpu.VMEM((rows, model), BF),
            pltpu.VMEM((3, rows, width), BF),
            full,
            pltpu.VMEM((model, width), F32),
            pltpu.VMEM((16, model), F32),
        ],
    )
    self_blocks, (send, keep) = self_back[:parts], self_back[parts:]
    self_sums = send_blocks(self_blocks, 1)
    chip, other = mp_sum(send, keep)
    text_half, vec = call(
        finish_kernel,
        "finish",
        [half_f32, ((16, model), BF)],
        (),
        (chip, other, text, grad_one, norm_gain),
    )
    image_away = level_swap(gate(chip_away, vec))
    cross_sums = fold(cross_sums, 2, "fold_cross", vec)
    down_sums = fold(down_sums, 4, "fold_down", cross_sums[0])
    up_sums = fold(up_sums, 1, "fold_up", down_sums[0])
    out_chip = add_pair(gate(out_keep, up_sums[0]), core_swap(out_send))
    out_other = level_swap(out_chip)
    if quick:
        low_rows = lambda count: ((count, 4 * width), BF)
        near, send, vec = call(
            fold_self_one_kernel,
            "fold_self",
            [low_rows(2 * height), low_rows(2 * height + 16), low_rows(16)],
            (),
            (gate(self_sums[0], out_chip), self_sums[1], vec, swap(vec, "dp", 8, 1)),
        )
        self_sums = near, swap(send, "dp", 8, 2)
        cross_sums = gate(cross_sums[0], near), cross_sums[1]
    cross_sums = fold(cross_sums, 4, "fold_cross", *self_sums[:1])
    if quick:
        close = lambda sums, first, name: call(
            close_ffn_kernel, name, [((height, hidden), F32)], (), (gate(sums[0], first), sums[1])
        )[0]
        down_turned = close(down_sums, cross_sums[0], "close_down")
        up_grad = close(up_sums, down_turned, "close_up")
        down_grad = down_turned.T
        join_first = gate(text_half, up_grad)
    else:
        join_first = text_half
    (out_half,) = call(
        layer_out_kernel,
        "layer_out",
        [half_low],
        (),
        (gate(out_chip, join_first), out_other, hidden_two, out_bias),
    )
    text_grad, layer_out = call(
        join_both_kernel,
        "join",
        [((rows, model), F32), wide],
        (),
        (join_first, core_swap(text_half), out_half, core_swap(out_half)),
    )
    if quick:
        near, send, vec = call(
            fold_self_two_kernel,
            "fold_self",
            [((height, 4 * width), F32), low_rows(height + 16), low_rows(16)],
            (),
            (gate(self_sums[0], text_grad), self_sums[1], vec),
        )
        self_sums = near, swap(send, "dp", 8, 4)
        query_grad, keyval_grad, cross_out_grad = call(
            close_cross_kernel,
            "close_cross",
            [((height, width), F32), ((2, height, width), F32), ((width, height), F32)],
            (),
            (gate(cross_sums[0], near), cross_sums[1]),
        )
    (image_grad,) = call(
        image_sum_kernel,
        "image_sum",
        [((seqs, width, patches), F32)],
        (),
        (gate(keep_own, query_grad) if quick else keep_own, core_swap(own_one), core_swap(own_two), image_away),
    )
    vec_outs = [((3, model), F32)] * 3 + [((hidden,), F32)]
    if quick:
        qkv_grad, self_out_grad, gains, shifts, biases, ups = call(
            close_self_kernel,
            "close_self",
            [((3, height, width), F32), ((width, height), F32)] + vec_outs,
            (),
            (gate(self_sums[0], image_grad), self_sums[1], vec),
        )
    else:
        gains, shifts, biases, ups = call(
            vector_kernel, "close_vector", vec_outs, (), (lax.psum(vec.astype(F32), "dp"),)
        )
        total = whole_sum(self_sums)
        qkv_grad = jnp.stack([total[:, j * width : (j + 1) * width] for j in range(3)])
        self_out_grad = total[:, 3 * width :].T
        total = whole_sum(cross_sums)
        query_grad = total[:, :width]
        keyval_grad = jnp.stack([total[:, j * width : (j + 1) * width] for j in (1, 2)])
        cross_out_grad = total[:, 3 * width :].T
        up_grad, down_grad = whole_sum(up_sums), whole_sum(down_sums).T
    return (
        layer_out.reshape(seqs, positions, model),
        text_grad.reshape(seqs, positions, model),
        image_grad.transpose(0, 2, 1),
        qkv_grad,
        self_out_grad,
        query_grad,
        keyval_grad,
        cross_out_grad,
        up_grad,
        down_grad,
        gains,
        shifts,
        biases,
        ups.reshape(hidden),
    )


def solution(mesh):
    placed = (
        P("dp", None, None),
        P("dp", None, None),
        P("dp"),
        P("dp"),
        P(None, "dp", "mp"),
        P("mp", "dp"),
        P("dp", "mp"),
        P(None, "dp", "mp"),
        P("mp", "dp"),
        P("dp", "mp"),
        P("mp", "dp"),
        P(),
        P(),
        P(),
        P("mp"),
        P("dp", None, None),
    )
    return jax.shard_map(
        functools.partial(per_device, mesh.shape["dp"], mesh.shape["mp"]),
        mesh=mesh,
        in_specs=placed,
        out_specs=(
            P("dp", None, None),
            P("dp", None, None),
            P("dp", None, "mp"),
            P(None, "dp", "mp"),
            P("mp", "dp"),
            P("dp", "mp"),
            P(None, "dp", "mp"),
            P("mp", "dp"),
            P("dp", "mp"),
            P("mp", "dp"),
            P(),
            P(),
            P(),
            P("mp"),
        ),
        check_vma=False,
    )
```

```python
import functools
import math

import jax
import jax.numpy as jnp
from jax import lax
from jax.experimental import pallas as pl
from jax.experimental.pallas import tpu as pltpu
from jax.sharding import PartitionSpec as P

BF = jnp.bfloat16
F32 = jnp.float32
HEAD_DIM = 64
SCALE = HEAD_DIM ** (-0.5)
NORM_EPS = 1e-05
NEG_FILL = -1e30
INV_ROOT_TWO = 1.0 / math.sqrt(2.0)
INV_ROOT_TAU = 1.0 / math.sqrt(2.0 * math.pi)
VMEM_LIMIT = 24 * 1024 * 1024
COST_PER_BYTE = 1
COST = pl.CostEstimate(flops=1, bytes_accessed=10**7, transcendentals=0)


def nn(a, b):
    return lax.dot_general(a, b, (((1,), (0,)), ((), ())), preferred_element_type=F32)


def nt(a, b):
    return lax.dot_general(a, b, (((1,), (1,)), ((), ())), preferred_element_type=F32)


def tn(a, b):
    return lax.dot_general(a, b, (((0,), (0,)), ((), ())), preferred_element_type=F32)


def norm_parts(values):
    centered = values - jnp.mean(values, axis=-1, keepdims=True)
    inv_std = lax.rsqrt(jnp.mean(centered * centered, axis=-1, keepdims=True) + NORM_EPS)
    return centered * inv_std, inv_std


def norm_back(grad, normed, inv_std, gain_row):
    scaled = grad * gain_row
    first = jnp.mean(scaled, axis=-1, keepdims=True)
    second = jnp.mean(scaled * normed, axis=-1, keepdims=True)
    return inv_std * (scaled - first - normed * second)


def head_masks(width, kind):
    column = lax.broadcasted_iota(jnp.int32, (1, width), 1) // HEAD_DIM
    return [(column == h).astype(F32).astype(kind) for h in range(width // HEAD_DIM)]


def stack_heads(rows, masks):
    return jnp.concatenate([rows * m for m in masks], axis=0)


def unstack_heads(stacked, masks):
    count = stacked.shape[0] // len(masks)
    total = stacked[:count] * masks[0]
    for h in range(1, len(masks)):
        total = total + stacked[h * count : (h + 1) * count] * masks[h]
    return total


def call(body, name, outs, scalars, arrays, scratch=(), flops=0):
    nbytes = sum(a.size * a.dtype.itemsize for a in arrays)
    nbytes += sum(math.prod(s) * jnp.dtype(d).itemsize for s, d in outs)
    return pl.pallas_call(
        body,
        out_shape=[jax.ShapeDtypeStruct(s, d) for s, d in outs],
        in_specs=[pl.BlockSpec(memory_space=pltpu.SMEM)] * len(scalars)
        + [pl.BlockSpec(memory_space=pltpu.VMEM)] * len(arrays),
        out_specs=[pl.BlockSpec(memory_space=pltpu.VMEM)] * len(outs),
        scratch_shapes=list(scratch),
        compiler_params=pltpu.CompilerParams(vmem_limit_bytes=VMEM_LIMIT),
        cost_estimate=pl.CostEstimate(
            flops=1, bytes_accessed=int(nbytes * COST_PER_BYTE) + 1, transcendentals=0
        ),
        name=name,
    )(*scalars, *arrays)


def turns_of(one, two, three):
    return [a ^ b ^ c for a in (0, one) for c in (0, three) for b in (0, two)]


X_FIRST = (1, 2, 4)
Z_FIRST = (2, 4, 1)
X_THEN_FAR = (1, 4, 2)


def block_rows(turn, height):
    at = (lax.axis_index("dp") ^ turn) * height
    return pl.ds(pl.multiple_of(at, 32), height)


def half_rows(height, away=False):
    core = lax.axis_index("mp") & 1
    at = (1 - core if away else core) * height
    return pl.ds(pl.multiple_of(at, 128), height)


def ring_rows(hops, height):
    index = lax.axis_index("dp")
    spot = jnp.where((index & 1) == 0, index >> 1, 7 - (index >> 1))
    spot = (spot + hops + 8) & 7
    at = jnp.where(spot < 4, 2 * spot, 15 - 2 * spot) * height
    return pl.ds(pl.multiple_of(at, 32), height)


def place_pieces(pieces, targets):
    if len(pieces) == 1:
        blocks = [(slice(None), pieces[0])]
    else:
        height = pieces[0].shape[0]
        side = 2 * (lax.axis_index("mp") & 1) - 1
        blocks = [(ring_rows(0, height), pieces[0]), (ring_rows(4, height), pieces[7])]
        for k in (1, 2, 3):
            blocks.append((ring_rows(side * k, height), pieces[k].at[0]))
            blocks.append((ring_rows(-side * k, height), pieces[3 + k].at[1]))
    for rows, piece in blocks:
        start = 0
        for target in targets:
            width = target.shape[1]
            target[rows, :] = piece[:, start : start + width]
            start += width


def join_halves(own, other, target):
    half = own.shape[0]
    target[half_rows(half), :] = own[...]
    target[half_rows(half, True), :] = other[...]


def split_halves(full, send, keep):
    half = full.shape[0] // 2
    keep[:half] = full[half_rows(half), :].astype(keep.dtype)
    send[:half] = full[half_rows(half, True), :].astype(send.dtype)


def pack_self_kernel(qkv, out, packed):
    width = qkv.shape[2]
    for j in range(3):
        packed[:, j * width : (j + 1) * width] = qkv[j]
    packed[:, 3 * width :] = out[...].astype(F32).T.astype(BF)


def pack_cross_kernel(query, keyval, out, cross):
    width = query.shape[1]
    cross[:, :width] = query[...]
    cross[:, width : 2 * width] = keyval[0]
    cross[:, 2 * width : 3 * width] = keyval[1]
    cross[:, 3 * width :] = out[...].astype(F32).T.astype(BF)


def pack_ffn_kernel(up, down, ffn):
    hidden = up.shape[1]
    ffn[:, :hidden] = up[...]
    ffn[:, hidden:] = down[...]


def pair_kernel(own, other, out):
    out[0] = own[...]
    out[1] = other[...]


def take_kernel(pair, out):
    out[...] = pair[0]


def self_forward_kernel(
    count, seqs, lens, text, gain, bias, *refs
):
    pieces, (weights, saved, send, keep, w, qkv, full, sems) = refs[:count], refs[count:]
    place_pieces(pieces, (w,))
    save_w = pltpu.make_async_copy(w, weights, sems.at[0])
    save_w.start()
    n, _ = norm_parts(text[...].astype(F32))
    low = (n * gain[0:1] + bias[0:1]).astype(BF)
    width = w.shape[1] // 4
    qkv[:, : 3 * width] = nn(low, w[:, : 3 * width]).astype(BF)
    low_masks, masks = head_masks(width, BF), head_masks(width, F32)
    rows = text.shape[0] // seqs
    for b in range(seqs):
        at = slice(b * rows, (b + 1) * rows)
        q_stack = stack_heads(qkv[at, :width], low_masks)
        p = self_softmax(q_stack, qkv[at, width : 2 * width], lens[b], rows)
        qkv[at, 3 * width :] = unstack_heads(
            nn(p.astype(BF), qkv[at, 2 * width : 3 * width]), masks
        ).astype(BF)
    save_q = pltpu.make_async_copy(qkv, saved, sems.at[1])
    save_q.start()
    full[...] = nt(qkv[:, 3 * width :], w[:, 3 * width :])
    split_halves(full, send, keep)
    save_w.wait()
    save_q.wait()


def self_softmax(q_stack, keys, length, rows):
    shape = (q_stack.shape[0], rows)
    query_at = lax.broadcasted_iota(jnp.int32, shape, 0) % rows
    key_at = lax.broadcasted_iota(jnp.int32, shape, 1)
    allowed = (key_at <= query_at) & (key_at < length)
    scores = jnp.where(allowed, nt(q_stack, keys) * SCALE, NEG_FILL)
    raised = jnp.exp(scores - jnp.max(scores, axis=-1, keepdims=True))
    return raised / jnp.sum(raised, axis=-1, keepdims=True)


def keyval_kernel(count, image, *refs):
    pieces, (wq, wk, wv, wo, keys, values) = refs[:count], refs[count:]

    @pl.when(pl.program_id(0) == 0)
    def _():
        place_pieces(pieces, (wq, wk, wv, wo))

    keys[...] = nn(image[...], wk[...]).astype(BF)
    values[...] = nn(image[...], wv[...]).astype(BF)


def norm_kernel(index, sliced, chip, other, resid, out_bias, gain, bias, hidden, normed):
    half = chip.shape[0]
    if sliced:
        base = resid[half_rows(half), :].astype(F32)
    else:
        base = resid[...]
    value = (
        base
        + (chip[...].astype(F32) + other[...].astype(F32))
        + out_bias[index : index + 1]
    )
    hidden[...] = value
    n, _ = norm_parts(value)
    normed[...] = (n * gain[index + 1 : index + 2] + bias[index + 1 : index + 2]).astype(BF)


def cross_forward_kernel(
    seqs, counts, own, other, wq, wo, keys, values, normed, q, prob, ctx, send, keep, full
):
    join_halves(own, other, normed)
    q[...] = nn(normed[...], wq[...]).astype(BF)
    width = q.shape[1]
    low_masks, masks = head_masks(width, BF), head_masks(width, F32)
    rows = normed.shape[0] // seqs
    patches = keys.shape[0] // seqs
    patch_at = lax.broadcasted_iota(jnp.int32, (rows * len(masks), patches), 1)
    for b in range(seqs):
        at = slice(b * rows, (b + 1) * rows)
        ks = slice(b * patches, (b + 1) * patches)
        scores = nt(stack_heads(q[at], low_masks), keys[ks]) * SCALE
        scores = jnp.where(patch_at < counts[b], scores, NEG_FILL)
        raised = jnp.exp(scores - jnp.max(scores, axis=-1, keepdims=True))
        p = raised / jnp.sum(raised, axis=-1, keepdims=True)
        prob[b] = p
        ctx[at] = unstack_heads(nn(p.astype(BF), values[ks]), masks).astype(BF)
    full[...] = nt(ctx[...], wo[...])
    split_halves(full, send, keep)


def ffn_ready_kernel(count, grad, *refs):
    pieces, (up, down, grad_act) = refs[:count], refs[count:]
    place_pieces(pieces, (up, down))
    grad_act[...] = nn(grad[...], down[...])


def ffn_kernel(
    own, other, up, down, grad_act, up_bias,
    normed, act, grad_low, bias_sum, send, keep, out_send, out_keep, full,
):
    join_halves(own, other, normed)
    pre = nn(normed[...], up[...]) + up_bias[...]
    cdf = 0.5 * (1.0 + lax.erf(pre * INV_ROOT_TWO))
    density = jnp.exp(-0.5 * pre * pre) * INV_ROOT_TAU
    grad_pre = grad_act[...] * (cdf + pre * density)
    grad_low[...] = grad_pre.astype(BF)
    act[...] = (pre * cdf).astype(BF)
    bias_sum[...] = jnp.sum(grad_pre, axis=0, keepdims=True)
    full[...] = nt(grad_low[...], up[...])
    split_halves(full, send, keep)
    full[...] = nt(act[...], down[...])
    split_halves(full, out_send, out_keep)


def scatter_blocks(matrix, column, outs, order=X_FIRST):
    blocks = sum(o.shape[0] for o in outs)
    height = outs[0].shape[1]
    width = matrix.shape[1]
    turns = turns_of(*order)
    for k in range(blocks):
        rows = block_rows(turns[k], height) if blocks > 1 else slice(None)
        target = outs[k // outs[0].shape[0]]
        target[k % outs[0].shape[0], :, column : column + width] = matrix[rows, :].astype(BF)


def ffn_weight_kernel(parts, normed, grad_low, grad, act, *refs):
    ups, downs, full = refs[:parts], refs[parts : 2 * parts], refs[2 * parts]
    full[...] = tn(normed[...], grad_low[...])
    scatter_blocks(full, 0, ups, Z_FIRST)
    full[...] = tn(grad[...], act[...])
    scatter_blocks(full, 0, downs)


def norm_back_kernel(index, sliced, chip, other, hidden, resid, gain, total, low, vec):
    half = chip.shape[0]
    if sliced:
        base = resid[half_rows(half), :].astype(F32)
    else:
        base = resid[...]
    grad = chip[...].astype(F32) + other[...].astype(F32)
    n, inv_std = norm_parts(hidden[...])
    value = base + norm_back(grad, n, inv_std, gain[index : index + 1])
    total[...] = value
    low[...] = value.astype(BF)
    vec[...] = jnp.zeros_like(vec)
    vec[0:1] = 0.5 * jnp.sum(grad * n, axis=0, keepdims=True)
    vec[1:2] = 0.5 * jnp.sum(grad, axis=0, keepdims=True)
    vec[2:3] = 0.5 * jnp.sum(value, axis=0, keepdims=True)
    if sliced:
        vec[3:4] = 0.5 * jnp.sum(base, axis=0, keepdims=True)


def score_grad(p, values, grad_stack):
    grad_p = nt(grad_stack, values)
    inner = jnp.sum(p * grad_p, axis=-1, keepdims=True)
    return (p * (grad_p - inner)).astype(BF)


def cross_back_kernel(
    seqs, own, other, wq, wo, keys, values, q, prob, grad_two, dq, dkt, dvt, send, keep, full
):
    join_halves(own, other, grad_two)
    grad_ctx = nn(grad_two[...], wo[...]).astype(BF)
    width = q.shape[1]
    low_masks, masks = head_masks(width, BF), head_masks(width, F32)
    rows = q.shape[0] // seqs
    patches = keys.shape[0] // seqs
    for b in range(seqs):
        at = slice(b * rows, (b + 1) * rows)
        ks = slice(b * patches, (b + 1) * patches)
        p = prob[b]
        q_stack = stack_heads(q[at], low_masks)
        grad_stack = stack_heads(grad_ctx[at], low_masks)
        ds = score_grad(p, values[ks], grad_stack)
        dq[at] = unstack_heads(nn(ds, keys[ks]) * SCALE, masks).astype(BF)
        dkt[:, ks] = (tn(q_stack, ds) * SCALE).astype(BF)
        dvt[:, ks] = tn(grad_stack, p.astype(BF)).astype(BF)
    full[...] = nt(dq[...], wq[...])
    split_halves(full, send, keep)


def cross_weight_kernel(parts, image, dkt, dvt, normed, dq, grad_two, ctx, *refs):
    outs, turned = refs[:parts], refs[parts]
    width = dq.shape[1]
    turned[...] = tn(normed[...], dq[...])
    scatter_blocks(turned, 0, outs, X_THEN_FAR)
    turned[...] = nn(dkt[...], image[...]).T
    scatter_blocks(turned, width, outs, X_THEN_FAR)
    turned[...] = nn(dvt[...], image[...]).T
    scatter_blocks(turned, 2 * width, outs, X_THEN_FAR)
    turned[...] = tn(grad_two[...], ctx[...])
    scatter_blocks(turned, 3 * width, outs, X_THEN_FAR)


def image_part_kernel(dkt, dvt, wk, wv, away_one, away_two, own_one, own_two, keep_away, keep_own):
    width = wk.shape[1]
    core, level = lax.axis_index("mp") & 1, lax.axis_index("mp") >> 1
    half = own_one.shape[1]
    for k, targets in enumerate(
        ((keep_own,), (keep_away,), (own_one, own_two), (away_one, away_two))
    ):
        at = (2 * (level ^ (k & 1)) + (core ^ (k >> 1))) * width
        rows = pl.ds(pl.multiple_of(at, 64), width)
        part = (nn(wk[rows, :], dkt[...]) + nn(wv[rows, :], dvt[...])).astype(BF)
        if len(targets) == 1:
            targets[0][...] = part
        else:
            targets[0][...] = part[:, :half]
            targets[1][...] = part[:, half:]


def add_pair_kernel(one, two, out):
    out[...] = (one[...].astype(F32) + two[...].astype(F32)).astype(BF)


def add_halves_kernel(keep, one, two, out):
    half = one.shape[1]
    out[:, :half] = (keep[:, :half].astype(F32) + one[...].astype(F32)).astype(BF)
    out[:, half:] = (keep[:, half:].astype(F32) + two[...].astype(F32)).astype(BF)


def image_sum_kernel(keep, one, two, away, out):
    patches = out.shape[2]
    per = one.shape[1] // patches
    for b in range(out.shape[0]):
        ks = slice(b * patches, (b + 1) * patches)
        part = one if b < per else two
        ps = slice((b % per) * patches, (b % per + 1) * patches)
        out[b] = keep[:, ks].astype(F32) + part[:, ps].astype(F32) + away[:, ks].astype(F32)


def self_back_kernel(
    seqs, parts, lens, own, other, text, gain, bias, w, qkv,
    one, two, ups, *refs
):
    outs = refs[:parts]
    send, keep, low, dqkv, full, narrow, vec = refs[parts:]
    join_halves(own, other, low)
    width = w.shape[1] // 4
    grad_ctx = nn(low[...], w[:, 3 * width :]).astype(BF)
    low_masks, masks = head_masks(width, BF), head_masks(width, F32)
    rows = text.shape[0] // seqs
    for b in range(seqs):
        at = slice(b * rows, (b + 1) * rows)
        q_stack = stack_heads(qkv[at, :width], low_masks)
        keys = qkv[at, width : 2 * width]
        p = self_softmax(q_stack, keys, lens[b], rows)
        grad_stack = stack_heads(grad_ctx[at], low_masks)
        ds = score_grad(p, qkv[at, 2 * width : 3 * width], grad_stack)
        dqkv[0, at] = unstack_heads(nn(ds, keys) * SCALE, masks).astype(BF)
        dqkv[1, at] = (tn(ds, q_stack) * SCALE).astype(BF)
        dqkv[2, at] = tn(p.astype(BF), grad_stack).astype(BF)
    n, _ = norm_parts(text[...].astype(F32))
    normed = (n * gain[0:1] + bias[0:1]).astype(BF)
    for j in range(3):
        narrow[...] = tn(normed, dqkv[j])
        scatter_blocks(narrow, j * width, outs)
    narrow[...] = tn(low[...], qkv[:, 3 * width :])
    scatter_blocks(narrow, 3 * width, outs)
    part = nt(dqkv[0], w[:, :width])
    for j in (1, 2):
        part = part + nt(dqkv[j], w[:, j * width : (j + 1) * width])
    full[...] = part
    split_halves(full, send, keep)
    half = own.shape[0]
    vec[...] = jnp.zeros_like(vec)
    vec[0:1] = jnp.sum(part * n, axis=0, keepdims=True)
    vec[1:2], vec[2:3] = one[0:1], two[0:1]
    vec[3:4] = jnp.sum(part, axis=0, keepdims=True)
    vec[4:5], vec[5:6] = one[1:2], two[1:2]
    vec[6:7], vec[7:8], vec[8:9] = one[2:3], two[2:3], two[3:4]
    vec[pl.ds(9 + lax.axis_index("mp"), 1), :] = ups[...]
    send[half:] = vec[...].astype(BF)
    keep[half:] = vec[...].astype(BF)


def finish_kernel(chip, other, text, resid, gain, grad_out, vec):
    half = resid.shape[0]
    grad = chip[:half].astype(F32) + other[:half].astype(F32)
    base = text[half_rows(half), :].astype(F32)
    n, inv_std = norm_parts(base)
    grad_out[...] = resid[...] + norm_back(grad, n, inv_std, gain[0:1])
    vec[...] = (chip[half:].astype(F32) + other[half:].astype(F32)).astype(BF)


def layer_out_kernel(chip, other, hidden, out_bias, out):
    out[...] = (
        hidden[...] + (chip[...].astype(F32) + other[...].astype(F32)) + out_bias[2:3]
    ).astype(BF)


def join_both_kernel(own, other, own_low, other_low, out, out_low):
    join_halves(own, other, out)
    join_halves(own_low, other_low, out_low)


def fold_kernel(keep, other, stay, send):
    for k in range(keep.shape[0]):
        target = send if k % 2 else stay
        value = (keep[k].astype(F32) + other[k].astype(F32)).astype(target.dtype)
        if len(target.shape) == 3:
            target[k // 2] = value
        else:
            target[...] = value


def fold_self_one_kernel(keep, other, vec, vec_other, stay, send, vec_sum):
    height = keep.shape[1]
    for k in range(4):
        value = (keep[k].astype(F32) + other[k].astype(F32)).astype(BF)
        at = (k // 2) * height
        (send if k % 2 else stay)[at : at + height] = value
    total = (vec[...].astype(F32) + vec_other[...].astype(F32)).astype(BF)
    vec_sum[...] = total
    send[2 * height :] = total


def fold_self_two_kernel(keep, other, vec, stay, send, vec_sum):
    height = stay.shape[0]
    stay[...] = keep[:height].astype(F32) + other[:height].astype(F32)
    rest = slice(height, 2 * height)
    send[:height] = (keep[rest].astype(F32) + other[rest].astype(F32)).astype(BF)
    total = (vec[...].astype(F32) + other[2 * height :].astype(F32)).astype(BF)
    vec_sum[...] = total
    send[height:] = total


def vector_parts(total, gains, shifts, biases, ups):
    gains[...] = total[0:3]
    shifts[...] = total[3:6]
    biases[...] = total[6:9]
    full = total[9]
    for k in range(1, 4):
        full = jnp.where(lax.axis_index("mp") == k, total[9 + k], full)
    ups[...] = full


def vector_kernel(vec, gains, shifts, biases, ups):
    vector_parts(vec[...], gains, shifts, biases, ups)


def close_cross_kernel(*refs):
    own, other, query, keyval, out = refs
    total = own[...] + other[...].astype(F32)
    width = out.shape[0]
    query[...] = total[:, :width]
    keyval[0] = total[:, width : 2 * width]
    keyval[1] = total[:, 2 * width : 3 * width]
    out[...] = total[:, 3 * width :].T


def close_ffn_kernel(own, other, out):
    out[...] = own[...] + other[...].astype(F32)


def close_self_kernel(own, other, vec, qkv, out, gains, shifts, biases, ups):
    height = own.shape[0]
    total = own[...] + other[:height].astype(F32)
    width = out.shape[0]
    for j in range(3):
        qkv[j] = total[:, j * width : (j + 1) * width]
    out[...] = total[:, 3 * width :].T
    vector_parts(vec[...].astype(F32) + other[height:].astype(F32), gains, shifts, biases, ups)


def swap(value, axis, size, bits):
    return lax.ppermute(value, axis, [(i, i ^ bits) for i in range(size)])


def gate_all(values, *first):
    return list(lax.optimization_barrier((*values, *first)))[: len(values)]


def gate(value, *first):
    return lax.optimization_barrier((value, *first))[0]


def per_device(
    dp_size,
    mp_size,
    text_tokens,
    image_tokens,
    text_lengths,
    patch_counts,
    self_qkv,
    self_out,
    cross_query,
    cross_keyval,
    cross_out,
    mlp_up,
    mlp_down,
    norm_gain,
    norm_bias,
    out_bias,
    up_bias,
    out_grad,
):
    seqs, positions, model = text_tokens.shape
    patches = image_tokens.shape[1]
    rows = seqs * positions
    half = rows // 2
    width = cross_query.shape[1]
    hidden = mlp_up.shape[1]
    image_rows = seqs * patches
    quick = dp_size == 8
    height = model // dp_size
    parts, blocks = (2, (4, height)) if quick else (1, (1, model))

    spots = [0, 2, 4, 6, 7, 5, 3, 1]
    turns = [
        (spots[p] * mp_size + m, spots[(p + (1 if m % 2 == 0 else -1)) % 8] * mp_size + m)
        for p in range(8)
        for m in range(mp_size)
    ]

    def around(value):
        return lax.ppermute(value, ("dp", "mp"), turns)

    def pair_up(shard, name):
        return call(
            pair_kernel, name, [((2,) + shard.shape, BF)], (), (shard, core_swap(shard))
        )[0]

    def last_hop(pair, name):
        (own,) = call(take_kernel, name, [(pair.shape[1:], BF)], (), (pair,))
        return around(own)

    def collect(shard, hops, swaps=None):
        swaps = swaps or [core_swap(hop) for hop in hops[:3]]
        return [shard] + hops[:3] + swaps + [hops[3]]

    def send_blocks(outs, bits):
        return (outs[0], swap(outs[1], "dp", 8, bits)) if quick else outs

    def fold(halves, bits, name, *first):
        if not quick:
            return halves
        keep, other = halves
        count, shape = keep.shape[0] // 2, keep.shape[1:]
        kinds = [((2,) + shape, BF)] * 2 if count == 2 else [(shape, F32), (shape, BF)]
        stay, send = call(fold_kernel, name, kinds, (), (gate(keep, *first), other))
        return stay, swap(send, "dp", 8, bits)

    def whole_sum(halves):
        return lax.psum_scatter(halves[0][0], "dp", scatter_dimension=0, tiled=True).astype(F32)

    def core_swap(value):
        return swap(value, "mp", mp_size, 1)

    def level_swap(value):
        return swap(value, "mp", mp_size, 2)

    def add_pair(one, two):
        return call(add_pair_kernel, "add_pair", [(one.shape, BF)], (), (one, two))[0]

    def mp_sum(send, keep):
        chip = add_pair(keep, core_swap(send))
        return chip, level_swap(chip)

    text = text_tokens.reshape(rows, model)
    image = image_tokens.reshape(image_rows, model)
    grad = out_grad.reshape(rows, model)

    if quick:
        (self_shard,) = call(
            pack_self_kernel, "pack_self", [((height, 4 * width), BF)], (), (self_qkv, self_out)
        )
        (cross_shard,) = call(
            pack_cross_kernel,
            "pack_cross",
            [((height, 4 * width), BF)],
            (),
            (cross_query, cross_keyval, cross_out),
        )
        (ffn_shard,) = call(
            pack_ffn_kernel, "pack_ffn", [((height, 2 * hidden), BF)], (), (mlp_up, mlp_down.T)
        )
        self_pair = pair_up(self_shard, "pairA")
        self_hops = [around(self_pair)]
        cross_hops = [around(pair_up(gate(cross_shard, self_pair), "pairB"))]
        for k in range(2):
            self_hops.append(around(self_hops[-1]))
            cross_hops.append(around(cross_hops[-1]))
        self_hops.append(last_hop(self_hops[-1], "takeA"))
        cross_hops.append(last_hop(cross_hops[-1], "takeB"))
        self_swaps = [core_swap(hop) for hop in self_hops[:3]]
        self_pieces = collect(self_shard, self_hops, self_swaps)
        cross_pieces = collect(cross_shard, cross_hops)
        ffn_pair = pair_up(gate(ffn_shard, self_hops[0]), "pairF")
        ffn_hops = [around(gate(ffn_pair, cross_hops[1]))]
        ffn_hops.append(around(ffn_hops[0]))
        text_in = gate(text, ffn_hops[0], cross_hops[2])
    else:
        gather = lambda shard: [lax.all_gather(shard, "dp", axis=0, tiled=True)]
        self_pieces = gather(
            jnp.concatenate([self_qkv[0], self_qkv[1], self_qkv[2], self_out.T], 1)
        )
        cross_pieces = gather(
            jnp.concatenate([cross_query, cross_keyval[0], cross_keyval[1], cross_out.T], 1)
        )
        text_in = text
        ffn_pieces = gather(jnp.concatenate([mlp_up, mlp_down.T], 1))

    square = ((model, width), BF)
    narrow = ((rows, width), BF)
    wide = ((rows, model), BF)
    halves = [((half, model), BF)] * 2
    half_f32 = ((half, model), F32)
    half_low = ((half, model), BF)
    heads = width // HEAD_DIM
    full = pltpu.VMEM((rows, model), F32)

    vmem = pl.BlockSpec(memory_space=pltpu.VMEM)
    smem = pl.BlockSpec(memory_space=pltpu.SMEM)
    hbm = pl.BlockSpec(memory_space=pltpu.HBM)
    w_self, saved, send, keep = pl.pallas_call(
        functools.partial(self_forward_kernel, len(self_pieces), seqs),
        out_shape=[
            jax.ShapeDtypeStruct((model, 4 * width), BF),
            jax.ShapeDtypeStruct((rows, 4 * width), BF),
            jax.ShapeDtypeStruct((half, model), BF),
            jax.ShapeDtypeStruct((half, model), BF),
        ],
        in_specs=[smem] + [vmem] * (3 + len(self_pieces)),
        out_specs=[hbm, hbm, vmem, vmem],
        scratch_shapes=[
            pltpu.VMEM((model, 4 * width), BF),
            pltpu.VMEM((rows, 4 * width), BF),
            full,
            pltpu.SemaphoreType.DMA((2,)),
        ],
        compiler_params=pltpu.CompilerParams(vmem_limit_bytes=VMEM_LIMIT),
        cost_estimate=COST,
        name="self_forward",
    )(text_lengths, text_in, norm_gain, norm_bias, *self_pieces)
    chip, other = mp_sum(send, keep)

    whole = lambda shape: pl.BlockSpec(shape, lambda b: (0,) * len(shape))
    per_seq = lambda b: (b, 0)
    cq, ck, cv, co, keys, values = pl.pallas_call(
        functools.partial(keyval_kernel, len(cross_pieces)),
        grid=(seqs,),
        out_shape=[jax.ShapeDtypeStruct((model, width), BF)] * 4
        + [jax.ShapeDtypeStruct((image_rows, width), BF)] * 2,
        in_specs=[pl.BlockSpec((patches, model), per_seq)]
        + [whole(piece.shape) for piece in cross_pieces],
        out_specs=[whole((model, width))] * 4 + [pl.BlockSpec((patches, width), per_seq)] * 2,
        compiler_params=pltpu.CompilerParams(vmem_limit_bytes=VMEM_LIMIT),
        cost_estimate=COST,
        name="keyval",
    )(image, *cross_pieces)

    hidden_one, normed_half = call(
        functools.partial(norm_kernel, 0, True),
        "norm_mid",
        [half_f32, half_low],
        (),
        (gate(chip, keys, ffn_hops[1]) if quick else chip, other, text, out_bias, norm_gain, norm_bias),
    )
    if quick:
        ffn_hops.append(around(gate(ffn_hops[1], normed_half)))
    normed_mid, xq, cross_prob, cross_ctx, send, keep = call(
        functools.partial(cross_forward_kernel, seqs),
        "cross_forward",
        [wide, narrow, ((seqs, heads * positions, patches), F32), narrow] + halves,
        (patch_counts,),
        (normed_half, core_swap(normed_half), cq, co, keys, values),
        [full],
        flops=2 * rows * model * width * 2,
    )
    chip, other = mp_sum(send, keep)
    if quick:
        ffn_hops.append(last_hop(gate(ffn_hops[2], chip), "takeF"))
        ffn_pieces = collect(ffn_shard, ffn_hops)
    w_up, w_down, grad_act = call(
        functools.partial(ffn_ready_kernel, len(ffn_pieces)),
        "ffn_ready",
        [((model, hidden), BF)] * 2 + [((rows, hidden), F32)],
        (),
        (grad, *ffn_pieces),
        flops=2 * rows * model * hidden,
    )
    hidden_two, normed_half = call(
        functools.partial(norm_kernel, 1, False),
        "norm_ffn",
        [half_f32, half_low],
        (),
        (chip, other, hidden_one, out_bias, norm_gain, norm_bias),
    )
    (normed_ffn, act, grad_low, up_sum, send, keep, out_send, out_keep) = call(
        ffn_kernel,
        "ffn",
        [wide, ((rows, hidden), BF), ((rows, hidden), BF), ((1, hidden), F32)] + halves + halves,
        (),
        (
            normed_half,
            core_swap(normed_half),
            w_up,
            w_down,
            grad_act,
            up_bias.reshape(1, hidden),
        ),
        [full],
        flops=2 * rows * model * hidden * 3,
    )
    chip, other = mp_sum(send, keep)

    ffn_blocks = call(
        functools.partial(ffn_weight_kernel, parts),
        "ffn_weights",
        [(blocks + (hidden,), BF)] * (2 * parts),
        (),
        (normed_ffn, grad_low, grad, act),
        [pltpu.VMEM((model, hidden), F32)],
        flops=2 * rows * model * hidden * 2,
    )
    up_sums = send_blocks(ffn_blocks[:parts], 2)
    down_sums = send_blocks(ffn_blocks[parts:], 1)
    vec_shape = ((8, model), F32)
    grad_two, low_half, vec_two = call(
        functools.partial(norm_back_kernel, 2, True),
        "norm_back_ffn",
        [half_f32, half_low, vec_shape],
        (),
        (gate(chip, *ffn_blocks), other, hidden_two, grad, norm_gain),
    )
    turned = ((width, image_rows), BF)
    grad_two_low, dq, dkt, dvt, send, keep = call(
        functools.partial(cross_back_kernel, seqs),
        "cross_back",
        [wide, narrow, turned, turned] + halves,
        (),
        (low_half, core_swap(low_half), cq, co, keys, values, xq, cross_prob),
        [full],
        flops=2 * rows * model * width * 2,
    )
    turned_half = ((width, image_rows // 2), BF)
    away_one, away_two, own_one, own_two, keep_away, keep_own = call(
        image_part_kernel,
        "image_part",
        [turned_half] * 4 + [turned] * 2,
        (),
        (dkt, dvt, ck, cv),
    )
    chip, other = mp_sum(send, gate(keep, keep_own))
    up_sums = fold(up_sums, 4, "fold_up", chip)
    down_sums = fold(down_sums, 2, "fold_down", up_sums[0])
    cross_blocks = call(
        functools.partial(cross_weight_kernel, parts),
        "cross_weights",
        [(blocks + (4 * width,), BF)] * parts,
        (),
        (image, gate(dkt, down_sums[0]), dvt, normed_mid, dq, grad_two_low, cross_ctx),
        [pltpu.VMEM((model, width), F32)],
        flops=2 * image_rows * model * width * 2,
    )
    cross_sums = send_blocks(cross_blocks, 1)
    grad_one, low_half, vec_one = call(
        functools.partial(norm_back_kernel, 1, False),
        "norm_back_mid",
        [half_f32, half_low, vec_shape],
        (),
        (gate(chip, *cross_blocks), other, hidden_one, grad_two, norm_gain),
    )
    (chip_away,) = call(
        add_halves_kernel,
        "image_chip",
        [turned],
        (),
        (gate(keep_away, low_half), core_swap(away_one), core_swap(away_two)),
    )
    tall = ((half + 16, model), BF)
    self_back = call(
        functools.partial(self_back_kernel, seqs, parts),
        "self_back",
        [(blocks + (4 * width,), BF)] * parts + [tall] * 2,
        (text_lengths,),
        (
            low_half,
            core_swap(low_half),
            gate(text, chip_away),
            norm_gain,
            norm_bias,
            w_self,
            saved,
            vec_one,
            vec_two,
            up_sum,
        ),
        [
            pltpu.VMEM((rows, model), BF),
            pltpu.VMEM((3, rows, width), BF),
            full,
            pltpu.VMEM((model, width), F32),
            pltpu.VMEM((16, model), F32),
        ],
    )
    self_blocks, (send, keep) = self_back[:parts], self_back[parts:]
    self_sums = send_blocks(self_blocks, 1)
    chip, other = mp_sum(send, keep)
    text_half, vec = call(
        finish_kernel,
        "finish",
        [half_f32, ((16, model), BF)],
        (),
        (chip, other, text, grad_one, norm_gain),
    )
    image_away = level_swap(gate(chip_away, vec))
    cross_sums = fold(cross_sums, 4, "fold_cross", vec)
    down_sums = fold(down_sums, 4, "fold_down", cross_sums[0])
    up_sums = fold(up_sums, 1, "fold_up", down_sums[0])
    out_chip = add_pair(gate(out_keep, up_sums[0]), core_swap(out_send))
    out_other = level_swap(out_chip)
    if quick:
        low_rows = lambda count: ((count, 4 * width), BF)
        near, send, vec = call(
            fold_self_one_kernel,
            "fold_self",
            [low_rows(2 * height), low_rows(2 * height + 16), low_rows(16)],
            (),
            (gate(self_sums[0], out_chip), self_sums[1], vec, swap(vec, "dp", 8, 1)),
        )
        self_sums = near, swap(send, "dp", 8, 2)
        cross_sums = gate(cross_sums[0], near), cross_sums[1]
    cross_sums = fold(cross_sums, 2, "fold_cross", *self_sums[:1])
    if quick:
        close = lambda sums, first, name: call(
            close_ffn_kernel, name, [((height, hidden), F32)], (), (gate(sums[0], first), sums[1])
        )[0]
        down_turned = close(down_sums, cross_sums[0], "close_down")
        up_grad = close(up_sums, down_turned, "close_up")
        down_grad = down_turned.T
        join_first = gate(text_half, up_grad)
    else:
        join_first = text_half
    (out_half,) = call(
        layer_out_kernel,
        "layer_out",
        [half_low],
        (),
        (gate(out_chip, join_first), out_other, hidden_two, out_bias),
    )
    text_grad, layer_out = call(
        join_both_kernel,
        "join",
        [((rows, model), F32), wide],
        (),
        (join_first, core_swap(text_half), out_half, core_swap(out_half)),
    )
    if quick:
        near, send, vec = call(
            fold_self_two_kernel,
            "fold_self",
            [((height, 4 * width), F32), low_rows(height + 16), low_rows(16)],
            (),
            (gate(self_sums[0], text_grad), self_sums[1], vec),
        )
        self_sums = near, swap(send, "dp", 8, 4)
    (image_grad,) = call(
        image_sum_kernel,
        "image_sum",
        [((seqs, width, patches), F32)],
        (),
        (gate(keep_own, near if quick else text_grad), core_swap(own_one), core_swap(own_two), image_away),
    )
    if quick:
        query_grad, keyval_grad, cross_out_grad = call(
            close_cross_kernel,
            "close_cross",
            [((height, width), F32), ((2, height, width), F32), ((width, height), F32)],
            (),
            (gate(cross_sums[0], image_grad), cross_sums[1]),
        )
    vec_outs = [((3, model), F32)] * 3 + [((hidden,), F32)]
    if quick:
        qkv_grad, self_out_grad, gains, shifts, biases, ups = call(
            close_self_kernel,
            "close_self",
            [((3, height, width), F32), ((width, height), F32)] + vec_outs,
            (),
            (gate(self_sums[0], query_grad), self_sums[1], vec),
        )
    else:
        gains, shifts, biases, ups = call(
            vector_kernel, "close_vector", vec_outs, (), (lax.psum(vec.astype(F32), "dp"),)
        )
        total = whole_sum(self_sums)
        qkv_grad = jnp.stack([total[:, j * width : (j + 1) * width] for j in range(3)])
        self_out_grad = total[:, 3 * width :].T
        total = whole_sum(cross_sums)
        query_grad = total[:, :width]
        keyval_grad = jnp.stack([total[:, j * width : (j + 1) * width] for j in (1, 2)])
        cross_out_grad = total[:, 3 * width :].T
        up_grad, down_grad = whole_sum(up_sums), whole_sum(down_sums).T
    return (
        layer_out.reshape(seqs, positions, model),
        text_grad.reshape(seqs, positions, model),
        image_grad.transpose(0, 2, 1),
        qkv_grad,
        self_out_grad,
        query_grad,
        keyval_grad,
        cross_out_grad,
        up_grad,
        down_grad,
        gains,
        shifts,
        biases,
        ups.reshape(hidden),
    )


def solution(mesh):
    placed = (
        P("dp", None, None),
        P("dp", None, None),
        P("dp"),
        P("dp"),
        P(None, "dp", "mp"),
        P("mp", "dp"),
        P("dp", "mp"),
        P(None, "dp", "mp"),
        P("mp", "dp"),
        P("dp", "mp"),
        P("mp", "dp"),
        P(),
        P(),
        P(),
        P("mp"),
        P("dp", None, None),
    )
    return jax.shard_map(
        functools.partial(per_device, mesh.shape["dp"], mesh.shape["mp"]),
        mesh=mesh,
        in_specs=placed,
        out_specs=(
            P("dp", None, None),
            P("dp", None, None),
            P("dp", None, "mp"),
            P(None, "dp", "mp"),
            P("mp", "dp"),
            P("dp", "mp"),
            P(None, "dp", "mp"),
            P("mp", "dp"),
            P("dp", "mp"),
            P("mp", "dp"),
            P(),
            P(),
            P(),
            P("mp"),
        ),
        check_vma=False,
    )
```

```python
import functools
import math

import jax
import jax.numpy as jnp
from jax import lax
from jax.experimental import pallas as pl
from jax.experimental.pallas import tpu as pltpu
from jax.sharding import PartitionSpec as P

BF = jnp.bfloat16
F32 = jnp.float32
HEAD_DIM = 64
SCALE = HEAD_DIM ** (-0.5)
NORM_EPS = 1e-05
NEG_FILL = -1e30
INV_ROOT_TWO = 1.0 / math.sqrt(2.0)
INV_ROOT_TAU = 1.0 / math.sqrt(2.0 * math.pi)
VMEM_LIMIT = 24 * 1024 * 1024
COST_PER_BYTE = 1
COST = pl.CostEstimate(flops=1, bytes_accessed=10**7, transcendentals=0)


def nn(a, b):
    return lax.dot_general(a, b, (((1,), (0,)), ((), ())), preferred_element_type=F32)


def nt(a, b):
    return lax.dot_general(a, b, (((1,), (1,)), ((), ())), preferred_element_type=F32)


def tn(a, b):
    return lax.dot_general(a, b, (((0,), (0,)), ((), ())), preferred_element_type=F32)


def norm_parts(values):
    centered = values - jnp.mean(values, axis=-1, keepdims=True)
    inv_std = lax.rsqrt(jnp.mean(centered * centered, axis=-1, keepdims=True) + NORM_EPS)
    return centered * inv_std, inv_std


def norm_back(grad, normed, inv_std, gain_row):
    scaled = grad * gain_row
    first = jnp.mean(scaled, axis=-1, keepdims=True)
    second = jnp.mean(scaled * normed, axis=-1, keepdims=True)
    return inv_std * (scaled - first - normed * second)


def head_masks(width, kind):
    column = lax.broadcasted_iota(jnp.int32, (1, width), 1) // HEAD_DIM
    return [(column == h).astype(F32).astype(kind) for h in range(width // HEAD_DIM)]


def stack_heads(rows, masks):
    return jnp.concatenate([rows * m for m in masks], axis=0)


def unstack_heads(stacked, masks):
    count = stacked.shape[0] // len(masks)
    total = stacked[:count] * masks[0]
    for h in range(1, len(masks)):
        total = total + stacked[h * count : (h + 1) * count] * masks[h]
    return total


def call(body, name, outs, scalars, arrays, scratch=(), flops=0):
    nbytes = sum(a.size * a.dtype.itemsize for a in arrays)
    nbytes += sum(math.prod(s) * jnp.dtype(d).itemsize for s, d in outs)
    return pl.pallas_call(
        body,
        out_shape=[jax.ShapeDtypeStruct(s, d) for s, d in outs],
        in_specs=[pl.BlockSpec(memory_space=pltpu.SMEM)] * len(scalars)
        + [pl.BlockSpec(memory_space=pltpu.VMEM)] * len(arrays),
        out_specs=[pl.BlockSpec(memory_space=pltpu.VMEM)] * len(outs),
        scratch_shapes=list(scratch),
        compiler_params=pltpu.CompilerParams(vmem_limit_bytes=VMEM_LIMIT),
        cost_estimate=pl.CostEstimate(
            flops=1, bytes_accessed=int(nbytes * COST_PER_BYTE) + 1, transcendentals=0
        ),
        name=name,
    )(*scalars, *arrays)


def turns_of(one, two, three):
    return [a ^ b ^ c for a in (0, one) for c in (0, three) for b in (0, two)]


X_FIRST = (1, 2, 4)
Z_FIRST = (2, 4, 1)
X_THEN_FAR = (1, 4, 2)


def block_rows(turn, height):
    at = (lax.axis_index("dp") ^ turn) * height
    return pl.ds(pl.multiple_of(at, 32), height)


def half_rows(height, away=False):
    core = lax.axis_index("mp") & 1
    at = (1 - core if away else core) * height
    return pl.ds(pl.multiple_of(at, 128), height)


def ring_rows(hops, height):
    index = lax.axis_index("dp")
    spot = jnp.where((index & 1) == 0, index >> 1, 7 - (index >> 1))
    spot = (spot + hops + 8) & 7
    at = jnp.where(spot < 4, 2 * spot, 15 - 2 * spot) * height
    return pl.ds(pl.multiple_of(at, 32), height)


def place_pieces(pieces, targets):
    if len(pieces) == 1:
        blocks = [(slice(None), pieces[0])]
    else:
        height = pieces[0].shape[0]
        side = 2 * (lax.axis_index("mp") & 1) - 1
        blocks = [(ring_rows(0, height), pieces[0]), (ring_rows(4, height), pieces[7])]
        for k in (1, 2, 3):
            blocks.append((ring_rows(side * k, height), pieces[k].at[0]))
            blocks.append((ring_rows(-side * k, height), pieces[3 + k].at[1]))
    for rows, piece in blocks:
        start = 0
        for target in targets:
            width = target.shape[1]
            target[rows, :] = piece[:, start : start + width]
            start += width


def join_halves(own, other, target):
    half = own.shape[0]
    target[half_rows(half), :] = own[...]
    target[half_rows(half, True), :] = other[...]


def split_halves(full, send, keep):
    half = full.shape[0] // 2
    keep[:half] = full[half_rows(half), :].astype(keep.dtype)
    send[:half] = full[half_rows(half, True), :].astype(send.dtype)


def pack_self_kernel(qkv, out, packed):
    width = qkv.shape[2]
    for j in range(3):
        packed[:, j * width : (j + 1) * width] = qkv[j]
    packed[:, 3 * width :] = out[...].astype(F32).T.astype(BF)


def pack_cross_kernel(query, keyval, out, cross):
    width = query.shape[1]
    cross[:, :width] = query[...]
    cross[:, width : 2 * width] = keyval[0]
    cross[:, 2 * width : 3 * width] = keyval[1]
    cross[:, 3 * width :] = out[...].astype(F32).T.astype(BF)


def pack_ffn_kernel(up, down, ffn):
    hidden = up.shape[1]
    ffn[:, :hidden] = up[...]
    ffn[:, hidden:] = down[...]


def pair_kernel(own, other, out):
    out[0] = own[...]
    out[1] = other[...]


def take_kernel(pair, out):
    out[...] = pair[0]


def self_forward_kernel(
    count, seqs, lens, text, gain, bias, *refs
):
    pieces, (weights, saved, send, keep, w, qkv, full, sems) = refs[:count], refs[count:]
    place_pieces(pieces, (w,))
    save_w = pltpu.make_async_copy(w, weights, sems.at[0])
    save_w.start()
    n, _ = norm_parts(text[...].astype(F32))
    low = (n * gain[0:1] + bias[0:1]).astype(BF)
    width = w.shape[1] // 4
    qkv[:, : 3 * width] = nn(low, w[:, : 3 * width]).astype(BF)
    low_masks, masks = head_masks(width, BF), head_masks(width, F32)
    rows = text.shape[0] // seqs
    for b in range(seqs):
        at = slice(b * rows, (b + 1) * rows)
        q_stack = stack_heads(qkv[at, :width], low_masks)
        p = self_softmax(q_stack, qkv[at, width : 2 * width], lens[b], rows)
        qkv[at, 3 * width :] = unstack_heads(
            nn(p.astype(BF), qkv[at, 2 * width : 3 * width]), masks
        ).astype(BF)
    save_q = pltpu.make_async_copy(qkv, saved, sems.at[1])
    save_q.start()
    full[...] = nt(qkv[:, 3 * width :], w[:, 3 * width :])
    split_halves(full, send, keep)
    save_w.wait()
    save_q.wait()


def self_softmax(q_stack, keys, length, rows):
    shape = (q_stack.shape[0], rows)
    query_at = lax.broadcasted_iota(jnp.int32, shape, 0) % rows
    key_at = lax.broadcasted_iota(jnp.int32, shape, 1)
    allowed = (key_at <= query_at) & (key_at < length)
    scores = jnp.where(allowed, nt(q_stack, keys) * SCALE, NEG_FILL)
    raised = jnp.exp(scores - jnp.max(scores, axis=-1, keepdims=True))
    return raised / jnp.sum(raised, axis=-1, keepdims=True)


def keyval_kernel(count, image, *refs):
    pieces, (wq, wk, wv, wo, keys, values) = refs[:count], refs[count:]

    @pl.when(pl.program_id(0) == 0)
    def _():
        place_pieces(pieces, (wq, wk, wv, wo))

    keys[...] = nn(image[...], wk[...]).astype(BF)
    values[...] = nn(image[...], wv[...]).astype(BF)


def norm_kernel(index, sliced, chip, other, resid, out_bias, gain, bias, hidden, normed):
    half = chip.shape[0]
    if sliced:
        base = resid[half_rows(half), :].astype(F32)
    else:
        base = resid[...]
    value = (
        base
        + (chip[...].astype(F32) + other[...].astype(F32))
        + out_bias[index : index + 1]
    )
    hidden[...] = value
    n, _ = norm_parts(value)
    normed[...] = (n * gain[index + 1 : index + 2] + bias[index + 1 : index + 2]).astype(BF)


def cross_forward_kernel(
    seqs, counts, own, other, wq, wo, keys, values, normed, q, prob, ctx, send, keep, full
):
    join_halves(own, other, normed)
    q[...] = nn(normed[...], wq[...]).astype(BF)
    width = q.shape[1]
    low_masks, masks = head_masks(width, BF), head_masks(width, F32)
    rows = normed.shape[0] // seqs
    patches = keys.shape[0] // seqs
    patch_at = lax.broadcasted_iota(jnp.int32, (rows * len(masks), patches), 1)
    for b in range(seqs):
        at = slice(b * rows, (b + 1) * rows)
        ks = slice(b * patches, (b + 1) * patches)
        scores = nt(stack_heads(q[at], low_masks), keys[ks]) * SCALE
        scores = jnp.where(patch_at < counts[b], scores, NEG_FILL)
        raised = jnp.exp(scores - jnp.max(scores, axis=-1, keepdims=True))
        p = raised / jnp.sum(raised, axis=-1, keepdims=True)
        prob[b] = p
        ctx[at] = unstack_heads(nn(p.astype(BF), values[ks]), masks).astype(BF)
    full[...] = nt(ctx[...], wo[...])
    split_halves(full, send, keep)


def ffn_ready_kernel(count, grad, *refs):
    pieces, (up, down, grad_act) = refs[:count], refs[count:]
    place_pieces(pieces, (up, down))
    grad_act[...] = nn(grad[...], down[...])


def ffn_kernel(
    own, other, up, down, grad_act, up_bias,
    normed, act, grad_low, bias_sum, send, keep, out_send, out_keep, full,
):
    join_halves(own, other, normed)
    pre = nn(normed[...], up[...]) + up_bias[...]
    cdf = 0.5 * (1.0 + lax.erf(pre * INV_ROOT_TWO))
    density = jnp.exp(-0.5 * pre * pre) * INV_ROOT_TAU
    grad_pre = grad_act[...] * (cdf + pre * density)
    grad_low[...] = grad_pre.astype(BF)
    act[...] = (pre * cdf).astype(BF)
    bias_sum[...] = jnp.sum(grad_pre, axis=0, keepdims=True)
    full[...] = nt(grad_low[...], up[...])
    split_halves(full, send, keep)
    full[...] = nt(act[...], down[...])
    split_halves(full, out_send, out_keep)


def scatter_blocks(matrix, column, outs, order=X_FIRST):
    blocks = sum(o.shape[0] for o in outs)
    height = outs[0].shape[1]
    width = matrix.shape[1]
    turns = turns_of(*order)
    for k in range(blocks):
        rows = block_rows(turns[k], height) if blocks > 1 else slice(None)
        target = outs[k // outs[0].shape[0]]
        target[k % outs[0].shape[0], :, column : column + width] = matrix[rows, :].astype(BF)


def ffn_weight_kernel(parts, normed, grad_low, grad, act, *refs):
    ups, downs, full = refs[:parts], refs[parts : 2 * parts], refs[2 * parts]
    full[...] = tn(normed[...], grad_low[...])
    scatter_blocks(full, 0, ups, Z_FIRST)
    full[...] = tn(grad[...], act[...])
    scatter_blocks(full, 0, downs)


def norm_back_kernel(index, sliced, chip, other, hidden, resid, gain, total, low, vec):
    half = chip.shape[0]
    if sliced:
        base = resid[half_rows(half), :].astype(F32)
    else:
        base = resid[...]
    grad = chip[...].astype(F32) + other[...].astype(F32)
    n, inv_std = norm_parts(hidden[...])
    value = base + norm_back(grad, n, inv_std, gain[index : index + 1])
    total[...] = value
    low[...] = value.astype(BF)
    vec[...] = jnp.zeros_like(vec)
    vec[0:1] = 0.5 * jnp.sum(grad * n, axis=0, keepdims=True)
    vec[1:2] = 0.5 * jnp.sum(grad, axis=0, keepdims=True)
    vec[2:3] = 0.5 * jnp.sum(value, axis=0, keepdims=True)
    if sliced:
        vec[3:4] = 0.5 * jnp.sum(base, axis=0, keepdims=True)


def score_grad(p, values, grad_stack):
    grad_p = nt(grad_stack, values)
    inner = jnp.sum(p * grad_p, axis=-1, keepdims=True)
    return (p * (grad_p - inner)).astype(BF)


def cross_back_kernel(
    seqs, own, other, wq, wo, keys, values, q, prob, grad_two, dq, dkt, dvt, send, keep, full
):
    join_halves(own, other, grad_two)
    grad_ctx = nn(grad_two[...], wo[...]).astype(BF)
    width = q.shape[1]
    low_masks, masks = head_masks(width, BF), head_masks(width, F32)
    rows = q.shape[0] // seqs
    patches = keys.shape[0] // seqs
    for b in range(seqs):
        at = slice(b * rows, (b + 1) * rows)
        ks = slice(b * patches, (b + 1) * patches)
        p = prob[b]
        q_stack = stack_heads(q[at], low_masks)
        grad_stack = stack_heads(grad_ctx[at], low_masks)
        ds = score_grad(p, values[ks], grad_stack)
        dq[at] = unstack_heads(nn(ds, keys[ks]) * SCALE, masks).astype(BF)
        dkt[:, ks] = (tn(q_stack, ds) * SCALE).astype(BF)
        dvt[:, ks] = tn(grad_stack, p.astype(BF)).astype(BF)
    full[...] = nt(dq[...], wq[...])
    split_halves(full, send, keep)


def cross_weight_kernel(parts, image, dkt, dvt, normed, dq, grad_two, ctx, *refs):
    outs, turned = refs[:parts], refs[parts]
    width = dq.shape[1]
    turned[...] = tn(normed[...], dq[...])
    scatter_blocks(turned, 0, outs, X_THEN_FAR)
    turned[...] = nn(dkt[...], image[...]).T
    scatter_blocks(turned, width, outs, X_THEN_FAR)
    turned[...] = nn(dvt[...], image[...]).T
    scatter_blocks(turned, 2 * width, outs, X_THEN_FAR)
    turned[...] = tn(grad_two[...], ctx[...])
    scatter_blocks(turned, 3 * width, outs, X_THEN_FAR)


def image_part_kernel(dkt, dvt, wk, wv, away_one, away_two, own_one, own_two, keep_away, keep_own):
    width = wk.shape[1]
    core, level = lax.axis_index("mp") & 1, lax.axis_index("mp") >> 1
    half = own_one.shape[1]
    for k, targets in enumerate(
        ((keep_own,), (keep_away,), (own_one, own_two), (away_one, away_two))
    ):
        at = (2 * (level ^ (k & 1)) + (core ^ (k >> 1))) * width
        rows = pl.ds(pl.multiple_of(at, 64), width)
        part = (nn(wk[rows, :], dkt[...]) + nn(wv[rows, :], dvt[...])).astype(BF)
        if len(targets) == 1:
            targets[0][...] = part
        else:
            targets[0][...] = part[:, :half]
            targets[1][...] = part[:, half:]


def add_pair_kernel(one, two, out):
    out[...] = (one[...].astype(F32) + two[...].astype(F32)).astype(BF)


def add_halves_kernel(keep, one, two, out):
    half = one.shape[1]
    out[:, :half] = (keep[:, :half].astype(F32) + one[...].astype(F32)).astype(BF)
    out[:, half:] = (keep[:, half:].astype(F32) + two[...].astype(F32)).astype(BF)


def image_sum_kernel(keep, one, two, away, out):
    patches = out.shape[2]
    per = one.shape[1] // patches
    for b in range(out.shape[0]):
        ks = slice(b * patches, (b + 1) * patches)
        part = one if b < per else two
        ps = slice((b % per) * patches, (b % per + 1) * patches)
        out[b] = keep[:, ks].astype(F32) + part[:, ps].astype(F32) + away[:, ks].astype(F32)


def self_back_kernel(
    seqs, parts, lens, own, other, text, gain, bias, w, qkv,
    one, two, ups, *refs
):
    outs = refs[:parts]
    send, keep, low, dqkv, full, narrow, vec = refs[parts:]
    join_halves(own, other, low)
    width = w.shape[1] // 4
    grad_ctx = nn(low[...], w[:, 3 * width :]).astype(BF)
    low_masks, masks = head_masks(width, BF), head_masks(width, F32)
    rows = text.shape[0] // seqs
    for b in range(seqs):
        at = slice(b * rows, (b + 1) * rows)
        q_stack = stack_heads(qkv[at, :width], low_masks)
        keys = qkv[at, width : 2 * width]
        p = self_softmax(q_stack, keys, lens[b], rows)
        grad_stack = stack_heads(grad_ctx[at], low_masks)
        ds = score_grad(p, qkv[at, 2 * width : 3 * width], grad_stack)
        dqkv[0, at] = unstack_heads(nn(ds, keys) * SCALE, masks).astype(BF)
        dqkv[1, at] = (tn(ds, q_stack) * SCALE).astype(BF)
        dqkv[2, at] = tn(p.astype(BF), grad_stack).astype(BF)
    n, _ = norm_parts(text[...].astype(F32))
    normed = (n * gain[0:1] + bias[0:1]).astype(BF)
    for j in range(3):
        narrow[...] = tn(normed, dqkv[j])
        scatter_blocks(narrow, j * width, outs)
    narrow[...] = tn(low[...], qkv[:, 3 * width :])
    scatter_blocks(narrow, 3 * width, outs)
    part = nt(dqkv[0], w[:, :width])
    for j in (1, 2):
        part = part + nt(dqkv[j], w[:, j * width : (j + 1) * width])
    full[...] = part
    split_halves(full, send, keep)
    half = own.shape[0]
    vec[...] = jnp.zeros_like(vec)
    vec[0:1] = jnp.sum(part * n, axis=0, keepdims=True)
    vec[1:2], vec[2:3] = one[0:1], two[0:1]
    vec[3:4] = jnp.sum(part, axis=0, keepdims=True)
    vec[4:5], vec[5:6] = one[1:2], two[1:2]
    vec[6:7], vec[7:8], vec[8:9] = one[2:3], two[2:3], two[3:4]
    vec[pl.ds(9 + lax.axis_index("mp"), 1), :] = ups[...]
    send[half:] = vec[...].astype(BF)
    keep[half:] = vec[...].astype(BF)


def finish_kernel(chip, other, text, resid, gain, grad_out, vec):
    half = resid.shape[0]
    grad = chip[:half].astype(F32) + other[:half].astype(F32)
    base = text[half_rows(half), :].astype(F32)
    n, inv_std = norm_parts(base)
    grad_out[...] = resid[...] + norm_back(grad, n, inv_std, gain[0:1])
    vec[...] = (chip[half:].astype(F32) + other[half:].astype(F32)).astype(BF)


def layer_out_kernel(chip, other, hidden, out_bias, out):
    out[...] = (
        hidden[...] + (chip[...].astype(F32) + other[...].astype(F32)) + out_bias[2:3]
    ).astype(BF)


def join_both_kernel(own, other, own_low, other_low, out, out_low):
    join_halves(own, other, out)
    join_halves(own_low, other_low, out_low)


def fold_kernel(keep, other, stay, send):
    for k in range(keep.shape[0]):
        target = send if k % 2 else stay
        value = (keep[k].astype(F32) + other[k].astype(F32)).astype(target.dtype)
        if len(target.shape) == 3:
            target[k // 2] = value
        else:
            target[...] = value


def fold_self_one_kernel(keep, other, vec, vec_other, stay, send, vec_sum):
    height = keep.shape[1]
    for k in range(4):
        value = (keep[k].astype(F32) + other[k].astype(F32)).astype(BF)
        at = (k // 2) * height
        (send if k % 2 else stay)[at : at + height] = value
    total = (vec[...].astype(F32) + vec_other[...].astype(F32)).astype(BF)
    vec_sum[...] = total
    send[2 * height :] = total


def fold_self_two_kernel(keep, other, vec, stay, send, vec_sum):
    height = stay.shape[0]
    stay[...] = keep[:height].astype(F32) + other[:height].astype(F32)
    rest = slice(height, 2 * height)
    send[:height] = (keep[rest].astype(F32) + other[rest].astype(F32)).astype(BF)
    total = (vec[...].astype(F32) + other[2 * height :].astype(F32)).astype(BF)
    vec_sum[...] = total
    send[height:] = total


def vector_parts(total, gains, shifts, biases, ups):
    gains[...] = total[0:3]
    shifts[...] = total[3:6]
    biases[...] = total[6:9]
    full = total[9]
    for k in range(1, 4):
        full = jnp.where(lax.axis_index("mp") == k, total[9 + k], full)
    ups[...] = full


def vector_kernel(vec, gains, shifts, biases, ups):
    vector_parts(vec[...], gains, shifts, biases, ups)


def close_cross_kernel(*refs):
    own, other, query, keyval, out = refs
    total = own[...] + other[...].astype(F32)
    width = out.shape[0]
    query[...] = total[:, :width]
    keyval[0] = total[:, width : 2 * width]
    keyval[1] = total[:, 2 * width : 3 * width]
    out[...] = total[:, 3 * width :].T


def close_ffn_kernel(own, other, out):
    out[...] = own[...] + other[...].astype(F32)


def close_self_kernel(own, other, vec, qkv, out, gains, shifts, biases, ups):
    height = own.shape[0]
    total = own[...] + other[:height].astype(F32)
    width = out.shape[0]
    for j in range(3):
        qkv[j] = total[:, j * width : (j + 1) * width]
    out[...] = total[:, 3 * width :].T
    vector_parts(vec[...].astype(F32) + other[height:].astype(F32), gains, shifts, biases, ups)


def swap(value, axis, size, bits):
    return lax.ppermute(value, axis, [(i, i ^ bits) for i in range(size)])


def gate_all(values, *first):
    return list(lax.optimization_barrier((*values, *first)))[: len(values)]


def gate(value, *first):
    return lax.optimization_barrier((value, *first))[0]


def per_device(
    dp_size,
    mp_size,
    text_tokens,
    image_tokens,
    text_lengths,
    patch_counts,
    self_qkv,
    self_out,
    cross_query,
    cross_keyval,
    cross_out,
    mlp_up,
    mlp_down,
    norm_gain,
    norm_bias,
    out_bias,
    up_bias,
    out_grad,
):
    seqs, positions, model = text_tokens.shape
    patches = image_tokens.shape[1]
    rows = seqs * positions
    half = rows // 2
    width = cross_query.shape[1]
    hidden = mlp_up.shape[1]
    image_rows = seqs * patches
    quick = dp_size == 8
    height = model // dp_size
    parts, blocks = (2, (4, height)) if quick else (1, (1, model))

    spots = [0, 2, 4, 6, 7, 5, 3, 1]
    turns = [
        (spots[p] * mp_size + m, spots[(p + (1 if m % 2 == 0 else -1)) % 8] * mp_size + m)
        for p in range(8)
        for m in range(mp_size)
    ]

    def around(value):
        return lax.ppermute(value, ("dp", "mp"), turns)

    def pair_up(shard, name):
        return call(
            pair_kernel, name, [((2,) + shard.shape, BF)], (), (shard, core_swap(shard))
        )[0]

    def last_hop(pair, name):
        (own,) = call(take_kernel, name, [(pair.shape[1:], BF)], (), (pair,))
        return around(own)

    def collect(shard, hops, swaps=None):
        swaps = swaps or [core_swap(hop) for hop in hops[:3]]
        return [shard] + hops[:3] + swaps + [hops[3]]

    def send_blocks(outs, bits):
        return (outs[0], swap(outs[1], "dp", 8, bits)) if quick else outs

    def fold(halves, bits, name, *first):
        if not quick:
            return halves
        keep, other = halves
        count, shape = keep.shape[0] // 2, keep.shape[1:]
        kinds = [((2,) + shape, BF)] * 2 if count == 2 else [(shape, F32), (shape, BF)]
        stay, send = call(fold_kernel, name, kinds, (), (gate(keep, *first), other))
        return stay, swap(send, "dp", 8, bits)

    def whole_sum(halves):
        return lax.psum_scatter(halves[0][0], "dp", scatter_dimension=0, tiled=True).astype(F32)

    def core_swap(value):
        return swap(value, "mp", mp_size, 1)

    def level_swap(value):
        return swap(value, "mp", mp_size, 2)

    def add_pair(one, two):
        return call(add_pair_kernel, "add_pair", [(one.shape, BF)], (), (one, two))[0]

    def mp_sum(send, keep):
        chip = add_pair(keep, core_swap(send))
        return chip, level_swap(chip)

    text = text_tokens.reshape(rows, model)
    image = image_tokens.reshape(image_rows, model)
    grad = out_grad.reshape(rows, model)

    if quick:
        (self_shard,) = call(
            pack_self_kernel, "pack_self", [((height, 4 * width), BF)], (), (self_qkv, self_out)
        )
        (cross_shard,) = call(
            pack_cross_kernel,
            "pack_cross",
            [((height, 4 * width), BF)],
            (),
            (cross_query, cross_keyval, cross_out),
        )
        (ffn_shard,) = call(
            pack_ffn_kernel, "pack_ffn", [((height, 2 * hidden), BF)], (), (mlp_up, mlp_down.T)
        )
        self_pair = pair_up(self_shard, "pairA")
        self_hops = [around(self_pair)]
        cross_hops = [around(pair_up(gate(cross_shard, self_pair), "pairB"))]
        for k in range(2):
            self_hops.append(around(self_hops[-1]))
            cross_hops.append(around(cross_hops[-1]))
        self_hops.append(last_hop(self_hops[-1], "takeA"))
        cross_hops.append(last_hop(cross_hops[-1], "takeB"))
        self_swaps = [core_swap(hop) for hop in self_hops[:3]]
        self_pieces = collect(self_shard, self_hops, self_swaps)
        cross_pieces = collect(cross_shard, cross_hops)
        ffn_pair = pair_up(gate(ffn_shard, self_hops[0]), "pairF")
        ffn_hops = [around(gate(ffn_pair, self_hops[1]))]
        ffn_hops.append(around(ffn_hops[0]))
        text_in = gate(text, ffn_hops[0], cross_hops[3])
    else:
        gather = lambda shard: [lax.all_gather(shard, "dp", axis=0, tiled=True)]
        self_pieces = gather(
            jnp.concatenate([self_qkv[0], self_qkv[1], self_qkv[2], self_out.T], 1)
        )
        cross_pieces = gather(
            jnp.concatenate([cross_query, cross_keyval[0], cross_keyval[1], cross_out.T], 1)
        )
        text_in = text
        ffn_pieces = gather(jnp.concatenate([mlp_up, mlp_down.T], 1))

    square = ((model, width), BF)
    narrow = ((rows, width), BF)
    wide = ((rows, model), BF)
    halves = [((half, model), BF)] * 2
    half_f32 = ((half, model), F32)
    half_low = ((half, model), BF)
    heads = width // HEAD_DIM
    full = pltpu.VMEM((rows, model), F32)

    vmem = pl.BlockSpec(memory_space=pltpu.VMEM)
    smem = pl.BlockSpec(memory_space=pltpu.SMEM)
    hbm = pl.BlockSpec(memory_space=pltpu.HBM)
    w_self, saved, send, keep = pl.pallas_call(
        functools.partial(self_forward_kernel, len(self_pieces), seqs),
        out_shape=[
            jax.ShapeDtypeStruct((model, 4 * width), BF),
            jax.ShapeDtypeStruct((rows, 4 * width), BF),
            jax.ShapeDtypeStruct((half, model), BF),
            jax.ShapeDtypeStruct((half, model), BF),
        ],
        in_specs=[smem] + [vmem] * (3 + len(self_pieces)),
        out_specs=[hbm, hbm, vmem, vmem],
        scratch_shapes=[
            pltpu.VMEM((model, 4 * width), BF),
            pltpu.VMEM((rows, 4 * width), BF),
            full,
            pltpu.SemaphoreType.DMA((2,)),
        ],
        compiler_params=pltpu.CompilerParams(vmem_limit_bytes=VMEM_LIMIT),
        cost_estimate=COST,
        name="self_forward",
    )(text_lengths, text_in, norm_gain, norm_bias, *self_pieces)
    chip, other = mp_sum(send, keep)

    whole = lambda shape: pl.BlockSpec(shape, lambda b: (0,) * len(shape))
    per_seq = lambda b: (b, 0)
    cq, ck, cv, co, keys, values = pl.pallas_call(
        functools.partial(keyval_kernel, len(cross_pieces)),
        grid=(seqs,),
        out_shape=[jax.ShapeDtypeStruct((model, width), BF)] * 4
        + [jax.ShapeDtypeStruct((image_rows, width), BF)] * 2,
        in_specs=[pl.BlockSpec((patches, model), per_seq)]
        + [whole(piece.shape) for piece in cross_pieces],
        out_specs=[whole((model, width))] * 4 + [pl.BlockSpec((patches, width), per_seq)] * 2,
        compiler_params=pltpu.CompilerParams(vmem_limit_bytes=VMEM_LIMIT),
        cost_estimate=COST,
        name="keyval",
    )(image, *cross_pieces)

    hidden_one, normed_half = call(
        functools.partial(norm_kernel, 0, True),
        "norm_mid",
        [half_f32, half_low],
        (),
        (gate(chip, keys, ffn_hops[1]) if quick else chip, other, text, out_bias, norm_gain, norm_bias),
    )
    if quick:
        ffn_hops.append(around(gate(ffn_hops[1], normed_half)))
    normed_mid, xq, cross_prob, cross_ctx, send, keep = call(
        functools.partial(cross_forward_kernel, seqs),
        "cross_forward",
        [wide, narrow, ((seqs, heads * positions, patches), F32), narrow] + halves,
        (patch_counts,),
        (normed_half, core_swap(normed_half), cq, co, keys, values),
        [full],
        flops=2 * rows * model * width * 2,
    )
    chip, other = mp_sum(send, keep)
    if quick:
        ffn_hops.append(last_hop(gate(ffn_hops[2], chip), "takeF"))
        ffn_pieces = collect(ffn_shard, ffn_hops)
    w_up, w_down, grad_act = call(
        functools.partial(ffn_ready_kernel, len(ffn_pieces)),
        "ffn_ready",
        [((model, hidden), BF)] * 2 + [((rows, hidden), F32)],
        (),
        (grad, *ffn_pieces),
        flops=2 * rows * model * hidden,
    )
    hidden_two, normed_half = call(
        functools.partial(norm_kernel, 1, False),
        "norm_ffn",
        [half_f32, half_low],
        (),
        (chip, other, hidden_one, out_bias, norm_gain, norm_bias),
    )
    (normed_ffn, act, grad_low, up_sum, send, keep, out_send, out_keep) = call(
        ffn_kernel,
        "ffn",
        [wide, ((rows, hidden), BF), ((rows, hidden), BF), ((1, hidden), F32)] + halves + halves,
        (),
        (
            normed_half,
            core_swap(normed_half),
            w_up,
            w_down,
            grad_act,
            up_bias.reshape(1, hidden),
        ),
        [full],
        flops=2 * rows * model * hidden * 3,
    )
    chip, other = mp_sum(send, keep)

    ffn_blocks = call(
        functools.partial(ffn_weight_kernel, parts),
        "ffn_weights",
        [(blocks + (hidden,), BF)] * (2 * parts),
        (),
        (normed_ffn, grad_low, grad, act),
        [pltpu.VMEM((model, hidden), F32)],
        flops=2 * rows * model * hidden * 2,
    )
    up_sums = send_blocks(ffn_blocks[:parts], 2)
    down_sums = send_blocks(ffn_blocks[parts:], 1)
    vec_shape = ((8, model), F32)
    grad_two, low_half, vec_two = call(
        functools.partial(norm_back_kernel, 2, True),
        "norm_back_ffn",
        [half_f32, half_low, vec_shape],
        (),
        (gate(chip, *ffn_blocks), other, hidden_two, grad, norm_gain),
    )
    turned = ((width, image_rows), BF)
    grad_two_low, dq, dkt, dvt, send, keep = call(
        functools.partial(cross_back_kernel, seqs),
        "cross_back",
        [wide, narrow, turned, turned] + halves,
        (),
        (low_half, core_swap(low_half), cq, co, keys, values, xq, cross_prob),
        [full],
        flops=2 * rows * model * width * 2,
    )
    turned_half = ((width, image_rows // 2), BF)
    away_one, away_two, own_one, own_two, keep_away, keep_own = call(
        image_part_kernel,
        "image_part",
        [turned_half] * 4 + [turned] * 2,
        (),
        (dkt, dvt, ck, cv),
    )
    chip, other = mp_sum(send, gate(keep, keep_own))
    up_sums = fold(up_sums, 4, "fold_up", chip)
    down_sums = fold(down_sums, 2, "fold_down", up_sums[0])
    cross_blocks = call(
        functools.partial(cross_weight_kernel, parts),
        "cross_weights",
        [(blocks + (4 * width,), BF)] * parts,
        (),
        (image, gate(dkt, down_sums[0]), dvt, normed_mid, dq, grad_two_low, cross_ctx),
        [pltpu.VMEM((model, width), F32)],
        flops=2 * image_rows * model * width * 2,
    )
    cross_sums = send_blocks(cross_blocks, 1)
    grad_one, low_half, vec_one = call(
        functools.partial(norm_back_kernel, 1, False),
        "norm_back_mid",
        [half_f32, half_low, vec_shape],
        (),
        (gate(chip, *cross_blocks), other, hidden_one, grad_two, norm_gain),
    )
    (chip_away,) = call(
        add_halves_kernel,
        "image_chip",
        [turned],
        (),
        (gate(keep_away, low_half), core_swap(away_one), core_swap(away_two)),
    )
    tall = ((half + 16, model), BF)
    self_back = call(
        functools.partial(self_back_kernel, seqs, parts),
        "self_back",
        [(blocks + (4 * width,), BF)] * parts + [tall] * 2,
        (text_lengths,),
        (
            low_half,
            core_swap(low_half),
            gate(text, chip_away),
            norm_gain,
            norm_bias,
            w_self,
            saved,
            vec_one,
            vec_two,
            up_sum,
        ),
        [
            pltpu.VMEM((rows, model), BF),
            pltpu.VMEM((3, rows, width), BF),
            full,
            pltpu.VMEM((model, width), F32),
            pltpu.VMEM((16, model), F32),
        ],
    )
    self_blocks, (send, keep) = self_back[:parts], self_back[parts:]
    self_sums = send_blocks(self_blocks, 1)
    chip, other = mp_sum(send, keep)
    text_half, vec = call(
        finish_kernel,
        "finish",
        [half_f32, ((16, model), BF)],
        (),
        (chip, other, text, grad_one, norm_gain),
    )
    image_away = level_swap(gate(chip_away, vec))
    cross_sums = fold(cross_sums, 4, "fold_cross", vec)
    down_sums = fold(down_sums, 4, "fold_down", cross_sums[0])
    up_sums = fold(up_sums, 1, "fold_up", down_sums[0])
    out_chip = add_pair(gate(out_keep, up_sums[0]), core_swap(out_send))
    out_other = level_swap(out_chip)
    if quick:
        low_rows = lambda count: ((count, 4 * width), BF)
        near, send, vec = call(
            fold_self_one_kernel,
            "fold_self",
            [low_rows(2 * height), low_rows(2 * height + 16), low_rows(16)],
            (),
            (gate(self_sums[0], out_chip), self_sums[1], vec, swap(vec, "dp", 8, 1)),
        )
        self_sums = near, swap(send, "dp", 8, 2)
        cross_sums = gate(cross_sums[0], near), cross_sums[1]
    cross_sums = fold(cross_sums, 2, "fold_cross", *self_sums[:1])
    if quick:
        close = lambda sums, first, name: call(
            close_ffn_kernel, name, [((height, hidden), F32)], (), (gate(sums[0], first), sums[1])
        )[0]
        down_turned = close(down_sums, cross_sums[0], "close_down")
        up_grad = close(up_sums, down_turned, "close_up")
        down_grad = down_turned.T
        join_first = gate(text_half, up_grad)
    else:
        join_first = text_half
    (out_half,) = call(
        layer_out_kernel,
        "layer_out",
        [half_low],
        (),
        (gate(out_chip, join_first), out_other, hidden_two, out_bias),
    )
    text_grad, layer_out = call(
        join_both_kernel,
        "join",
        [((rows, model), F32), wide],
        (),
        (join_first, core_swap(text_half), out_half, core_swap(out_half)),
    )
    if quick:
        near, send, vec = call(
            fold_self_two_kernel,
            "fold_self",
            [((height, 4 * width), F32), low_rows(height + 16), low_rows(16)],
            (),
            (gate(self_sums[0], text_grad), self_sums[1], vec),
        )
        self_sums = near, swap(send, "dp", 8, 4)
    (image_grad,) = call(
        image_sum_kernel,
        "image_sum",
        [((seqs, width, patches), F32)],
        (),
        (gate(keep_own, near if quick else text_grad), core_swap(own_one), core_swap(own_two), image_away),
    )
    if quick:
        query_grad, keyval_grad, cross_out_grad = call(
            close_cross_kernel,
            "close_cross",
            [((height, width), F32), ((2, height, width), F32), ((width, height), F32)],
            (),
            (gate(cross_sums[0], image_grad), cross_sums[1]),
        )
    vec_outs = [((3, model), F32)] * 3 + [((hidden,), F32)]
    if quick:
        qkv_grad, self_out_grad, gains, shifts, biases, ups = call(
            close_self_kernel,
            "close_self",
            [((3, height, width), F32), ((width, height), F32)] + vec_outs,
            (),
            (gate(self_sums[0], query_grad), self_sums[1], vec),
        )
    else:
        gains, shifts, biases, ups = call(
            vector_kernel, "close_vector", vec_outs, (), (lax.psum(vec.astype(F32), "dp"),)
        )
        total = whole_sum(self_sums)
        qkv_grad = jnp.stack([total[:, j * width : (j + 1) * width] for j in range(3)])
        self_out_grad = total[:, 3 * width :].T
        total = whole_sum(cross_sums)
        query_grad = total[:, :width]
        keyval_grad = jnp.stack([total[:, j * width : (j + 1) * width] for j in (1, 2)])
        cross_out_grad = total[:, 3 * width :].T
        up_grad, down_grad = whole_sum(up_sums), whole_sum(down_sums).T
    return (
        layer_out.reshape(seqs, positions, model),
        text_grad.reshape(seqs, positions, model),
        image_grad.transpose(0, 2, 1),
        qkv_grad,
        self_out_grad,
        query_grad,
        keyval_grad,
        cross_out_grad,
        up_grad,
        down_grad,
        gains,
        shifts,
        biases,
        ups.reshape(hidden),
    )


def solution(mesh):
    placed = (
        P("dp", None, None),
        P("dp", None, None),
        P("dp"),
        P("dp"),
        P(None, "dp", "mp"),
        P("mp", "dp"),
        P("dp", "mp"),
        P(None, "dp", "mp"),
        P("mp", "dp"),
        P("dp", "mp"),
        P("mp", "dp"),
        P(),
        P(),
        P(),
        P("mp"),
        P("dp", None, None),
    )
    return jax.shard_map(
        functools.partial(per_device, mesh.shape["dp"], mesh.shape["mp"]),
        mesh=mesh,
        in_specs=placed,
        out_specs=(
            P("dp", None, None),
            P("dp", None, None),
            P("dp", None, "mp"),
            P(None, "dp", "mp"),
            P("mp", "dp"),
            P("dp", "mp"),
            P(None, "dp", "mp"),
            P("mp", "dp"),
            P("dp", "mp"),
            P("mp", "dp"),
            P(),
            P(),
            P(),
            P("mp"),
        ),
        check_vma=False,
    )
```

```python
import functools
import math

import jax
import jax.numpy as jnp
from jax import lax
from jax.experimental import pallas as pl
from jax.experimental.pallas import tpu as pltpu
from jax.sharding import PartitionSpec as P

BF = jnp.bfloat16
F32 = jnp.float32
HEAD_DIM = 64
SCALE = HEAD_DIM ** (-0.5)
NORM_EPS = 1e-05
NEG_FILL = -1e30
INV_ROOT_TWO = 1.0 / math.sqrt(2.0)
INV_ROOT_TAU = 1.0 / math.sqrt(2.0 * math.pi)
VMEM_LIMIT = 24 * 1024 * 1024
COST_PER_BYTE = 1
COST = pl.CostEstimate(flops=1, bytes_accessed=10**7, transcendentals=0)


def nn(a, b):
    return lax.dot_general(a, b, (((1,), (0,)), ((), ())), preferred_element_type=F32)


def nt(a, b):
    return lax.dot_general(a, b, (((1,), (1,)), ((), ())), preferred_element_type=F32)


def tn(a, b):
    return lax.dot_general(a, b, (((0,), (0,)), ((), ())), preferred_element_type=F32)


def norm_parts(values):
    centered = values - jnp.mean(values, axis=-1, keepdims=True)
    inv_std = lax.rsqrt(jnp.mean(centered * centered, axis=-1, keepdims=True) + NORM_EPS)
    return centered * inv_std, inv_std


def norm_back(grad, normed, inv_std, gain_row):
    scaled = grad * gain_row
    first = jnp.mean(scaled, axis=-1, keepdims=True)
    second = jnp.mean(scaled * normed, axis=-1, keepdims=True)
    return inv_std * (scaled - first - normed * second)


def head_masks(width, kind):
    column = lax.broadcasted_iota(jnp.int32, (1, width), 1) // HEAD_DIM
    return [(column == h).astype(F32).astype(kind) for h in range(width // HEAD_DIM)]


def stack_heads(rows, masks):
    return jnp.concatenate([rows * m for m in masks], axis=0)


def unstack_heads(stacked, masks):
    count = stacked.shape[0] // len(masks)
    total = stacked[:count] * masks[0]
    for h in range(1, len(masks)):
        total = total + stacked[h * count : (h + 1) * count] * masks[h]
    return total


def call(body, name, outs, scalars, arrays, scratch=(), flops=0):
    nbytes = sum(a.size * a.dtype.itemsize for a in arrays)
    nbytes += sum(math.prod(s) * jnp.dtype(d).itemsize for s, d in outs)
    return pl.pallas_call(
        body,
        out_shape=[jax.ShapeDtypeStruct(s, d) for s, d in outs],
        in_specs=[pl.BlockSpec(memory_space=pltpu.SMEM)] * len(scalars)
        + [pl.BlockSpec(memory_space=pltpu.VMEM)] * len(arrays),
        out_specs=[pl.BlockSpec(memory_space=pltpu.VMEM)] * len(outs),
        scratch_shapes=list(scratch),
        compiler_params=pltpu.CompilerParams(vmem_limit_bytes=VMEM_LIMIT),
        cost_estimate=pl.CostEstimate(
            flops=1, bytes_accessed=int(nbytes * COST_PER_BYTE) + 1, transcendentals=0
        ),
        name=name,
    )(*scalars, *arrays)


def turns_of(one, two, three):
    return [a ^ b ^ c for a in (0, one) for c in (0, three) for b in (0, two)]


X_FIRST = (1, 2, 4)
Z_FIRST = (2, 4, 1)
X_THEN_FAR = (1, 4, 2)


def block_rows(turn, height):
    at = (lax.axis_index("dp") ^ turn) * height
    return pl.ds(pl.multiple_of(at, 32), height)


def half_rows(height, away=False):
    core = lax.axis_index("mp") & 1
    at = (1 - core if away else core) * height
    return pl.ds(pl.multiple_of(at, 128), height)


def ring_rows(hops, height):
    index = lax.axis_index("dp")
    spot = jnp.where((index & 1) == 0, index >> 1, 7 - (index >> 1))
    spot = (spot + hops + 8) & 7
    at = jnp.where(spot < 4, 2 * spot, 15 - 2 * spot) * height
    return pl.ds(pl.multiple_of(at, 32), height)


def place_pieces(pieces, targets):
    if len(pieces) == 1:
        blocks = [(slice(None), pieces[0])]
    else:
        height = pieces[0].shape[0]
        side = 2 * (lax.axis_index("mp") & 1) - 1
        blocks = [(ring_rows(0, height), pieces[0]), (ring_rows(4, height), pieces[7])]
        for k in (1, 2, 3):
            blocks.append((ring_rows(side * k, height), pieces[k].at[0]))
            blocks.append((ring_rows(-side * k, height), pieces[3 + k].at[1]))
    for rows, piece in blocks:
        start = 0
        for target in targets:
            width = target.shape[1]
            target[rows, :] = piece[:, start : start + width]
            start += width


def join_halves(own, other, target):
    half = own.shape[0]
    target[half_rows(half), :] = own[...]
    target[half_rows(half, True), :] = other[...]


def split_halves(full, send, keep):
    half = full.shape[0] // 2
    keep[:half] = full[half_rows(half), :].astype(keep.dtype)
    send[:half] = full[half_rows(half, True), :].astype(send.dtype)


def pack_self_kernel(qkv, out, packed):
    width = qkv.shape[2]
    for j in range(3):
        packed[:, j * width : (j + 1) * width] = qkv[j]
    packed[:, 3 * width :] = out[...].astype(F32).T.astype(BF)


def pack_cross_kernel(query, keyval, out, cross):
    width = query.shape[1]
    cross[:, :width] = query[...]
    cross[:, width : 2 * width] = keyval[0]
    cross[:, 2 * width : 3 * width] = keyval[1]
    cross[:, 3 * width :] = out[...].astype(F32).T.astype(BF)


def pack_ffn_kernel(up, down, ffn):
    hidden = up.shape[1]
    ffn[:, :hidden] = up[...]
    ffn[:, hidden:] = down[...]


def pair_kernel(own, other, out):
    out[0] = own[...]
    out[1] = other[...]


def take_kernel(pair, out):
    out[...] = pair[0]


def self_forward_kernel(
    count, seqs, lens, text, gain, bias, *refs
):
    pieces, (weights, saved, send, keep, w, qkv, full, sems) = refs[:count], refs[count:]
    place_pieces(pieces, (w,))
    save_w = pltpu.make_async_copy(w, weights, sems.at[0])
    save_w.start()
    n, _ = norm_parts(text[...].astype(F32))
    low = (n * gain[0:1] + bias[0:1]).astype(BF)
    width = w.shape[1] // 4
    qkv[:, : 3 * width] = nn(low, w[:, : 3 * width]).astype(BF)
    low_masks, masks = head_masks(width, BF), head_masks(width, F32)
    rows = text.shape[0] // seqs
    for b in range(seqs):
        at = slice(b * rows, (b + 1) * rows)
        q_stack = stack_heads(qkv[at, :width], low_masks)
        p = self_softmax(q_stack, qkv[at, width : 2 * width], lens[b], rows)
        qkv[at, 3 * width :] = unstack_heads(
            nn(p.astype(BF), qkv[at, 2 * width : 3 * width]), masks
        ).astype(BF)
    save_q = pltpu.make_async_copy(qkv, saved, sems.at[1])
    save_q.start()
    full[...] = nt(qkv[:, 3 * width :], w[:, 3 * width :])
    split_halves(full, send, keep)
    save_w.wait()
    save_q.wait()


def self_softmax(q_stack, keys, length, rows):
    shape = (q_stack.shape[0], rows)
    query_at = lax.broadcasted_iota(jnp.int32, shape, 0) % rows
    key_at = lax.broadcasted_iota(jnp.int32, shape, 1)
    allowed = (key_at <= query_at) & (key_at < length)
    scores = jnp.where(allowed, nt(q_stack, keys) * SCALE, NEG_FILL)
    raised = jnp.exp(scores - jnp.max(scores, axis=-1, keepdims=True))
    return raised / jnp.sum(raised, axis=-1, keepdims=True)


def keyval_kernel(count, image, *refs):
    pieces, (wq, wk, wv, wo, keys, values) = refs[:count], refs[count:]

    @pl.when(pl.program_id(0) == 0)
    def _():
        place_pieces(pieces, (wq, wk, wv, wo))

    keys[...] = nn(image[...], wk[...]).astype(BF)
    values[...] = nn(image[...], wv[...]).astype(BF)


def norm_kernel(index, sliced, chip, other, resid, out_bias, gain, bias, hidden, normed):
    half = chip.shape[0]
    if sliced:
        base = resid[half_rows(half), :].astype(F32)
    else:
        base = resid[...]
    value = (
        base
        + (chip[...].astype(F32) + other[...].astype(F32))
        + out_bias[index : index + 1]
    )
    hidden[...] = value
    n, _ = norm_parts(value)
    normed[...] = (n * gain[index + 1 : index + 2] + bias[index + 1 : index + 2]).astype(BF)


def cross_forward_kernel(
    seqs, counts, own, other, wq, wo, keys, values, normed, q, prob, ctx, send, keep, full
):
    join_halves(own, other, normed)
    q[...] = nn(normed[...], wq[...]).astype(BF)
    width = q.shape[1]
    low_masks, masks = head_masks(width, BF), head_masks(width, F32)
    rows = normed.shape[0] // seqs
    patches = keys.shape[0] // seqs
    patch_at = lax.broadcasted_iota(jnp.int32, (rows * len(masks), patches), 1)
    for b in range(seqs):
        at = slice(b * rows, (b + 1) * rows)
        ks = slice(b * patches, (b + 1) * patches)
        scores = nt(stack_heads(q[at], low_masks), keys[ks]) * SCALE
        scores = jnp.where(patch_at < counts[b], scores, NEG_FILL)
        raised = jnp.exp(scores - jnp.max(scores, axis=-1, keepdims=True))
        p = raised / jnp.sum(raised, axis=-1, keepdims=True)
        prob[b] = p
        ctx[at] = unstack_heads(nn(p.astype(BF), values[ks]), masks).astype(BF)
    full[...] = nt(ctx[...], wo[...])
    split_halves(full, send, keep)


def ffn_ready_kernel(count, grad, *refs):
    pieces, (up, down, grad_act) = refs[:count], refs[count:]
    place_pieces(pieces, (up, down))
    grad_act[...] = nn(grad[...], down[...])


def ffn_kernel(
    own, other, up, down, grad_act, up_bias,
    normed, act, grad_low, bias_sum, send, keep, out_send, out_keep, full,
):
    join_halves(own, other, normed)
    pre = nn(normed[...], up[...]) + up_bias[...]
    cdf = 0.5 * (1.0 + lax.erf(pre * INV_ROOT_TWO))
    density = jnp.exp(-0.5 * pre * pre) * INV_ROOT_TAU
    grad_pre = grad_act[...] * (cdf + pre * density)
    grad_low[...] = grad_pre.astype(BF)
    act[...] = (pre * cdf).astype(BF)
    bias_sum[...] = jnp.sum(grad_pre, axis=0, keepdims=True)
    full[...] = nt(grad_low[...], up[...])
    split_halves(full, send, keep)
    full[...] = nt(act[...], down[...])
    split_halves(full, out_send, out_keep)


def scatter_blocks(matrix, column, outs, order=X_FIRST):
    blocks = sum(o.shape[0] for o in outs)
    height = outs[0].shape[1]
    width = matrix.shape[1]
    turns = turns_of(*order)
    for k in range(blocks):
        rows = block_rows(turns[k], height) if blocks > 1 else slice(None)
        target = outs[k // outs[0].shape[0]]
        target[k % outs[0].shape[0], :, column : column + width] = matrix[rows, :].astype(BF)


def ffn_weight_kernel(parts, normed, grad_low, grad, act, *refs):
    ups, downs, full = refs[:parts], refs[parts : 2 * parts], refs[2 * parts]
    full[...] = tn(normed[...], grad_low[...])
    scatter_blocks(full, 0, ups, Z_FIRST)
    full[...] = tn(grad[...], act[...])
    scatter_blocks(full, 0, downs)


def norm_back_kernel(index, sliced, chip, other, hidden, resid, gain, total, low, vec):
    half = chip.shape[0]
    if sliced:
        base = resid[half_rows(half), :].astype(F32)
    else:
        base = resid[...]
    grad = chip[...].astype(F32) + other[...].astype(F32)
    n, inv_std = norm_parts(hidden[...])
    value = base + norm_back(grad, n, inv_std, gain[index : index + 1])
    total[...] = value
    low[...] = value.astype(BF)
    vec[...] = jnp.zeros_like(vec)
    vec[0:1] = 0.5 * jnp.sum(grad * n, axis=0, keepdims=True)
    vec[1:2] = 0.5 * jnp.sum(grad, axis=0, keepdims=True)
    vec[2:3] = 0.5 * jnp.sum(value, axis=0, keepdims=True)
    if sliced:
        vec[3:4] = 0.5 * jnp.sum(base, axis=0, keepdims=True)


def score_grad(p, values, grad_stack):
    grad_p = nt(grad_stack, values)
    inner = jnp.sum(p * grad_p, axis=-1, keepdims=True)
    return (p * (grad_p - inner)).astype(BF)


def cross_back_kernel(
    seqs, own, other, wq, wo, keys, values, q, prob, grad_two, dq, dkt, dvt, send, keep, full
):
    join_halves(own, other, grad_two)
    grad_ctx = nn(grad_two[...], wo[...]).astype(BF)
    width = q.shape[1]
    low_masks, masks = head_masks(width, BF), head_masks(width, F32)
    rows = q.shape[0] // seqs
    patches = keys.shape[0] // seqs
    for b in range(seqs):
        at = slice(b * rows, (b + 1) * rows)
        ks = slice(b * patches, (b + 1) * patches)
        p = prob[b]
        q_stack = stack_heads(q[at], low_masks)
        grad_stack = stack_heads(grad_ctx[at], low_masks)
        ds = score_grad(p, values[ks], grad_stack)
        dq[at] = unstack_heads(nn(ds, keys[ks]) * SCALE, masks).astype(BF)
        dkt[:, ks] = (tn(q_stack, ds) * SCALE).astype(BF)
        dvt[:, ks] = tn(grad_stack, p.astype(BF)).astype(BF)
    full[...] = nt(dq[...], wq[...])
    split_halves(full, send, keep)


def cross_weight_kernel(parts, image, dkt, dvt, normed, dq, grad_two, ctx, *refs):
    outs, turned = refs[:parts], refs[parts]
    width = dq.shape[1]
    turned[...] = tn(normed[...], dq[...])
    scatter_blocks(turned, 0, outs, X_THEN_FAR)
    turned[...] = nn(dkt[...], image[...]).T
    scatter_blocks(turned, width, outs, X_THEN_FAR)
    turned[...] = nn(dvt[...], image[...]).T
    scatter_blocks(turned, 2 * width, outs, X_THEN_FAR)
    turned[...] = tn(grad_two[...], ctx[...])
    scatter_blocks(turned, 3 * width, outs, X_THEN_FAR)


def image_part_kernel(dkt, dvt, wk, wv, away_one, away_two, own_one, own_two, keep_away, keep_own):
    width = wk.shape[1]
    core, level = lax.axis_index("mp") & 1, lax.axis_index("mp") >> 1
    half = own_one.shape[1]
    for k, targets in enumerate(
        ((keep_own,), (keep_away,), (own_one, own_two), (away_one, away_two))
    ):
        at = (2 * (level ^ (k & 1)) + (core ^ (k >> 1))) * width
        rows = pl.ds(pl.multiple_of(at, 64), width)
        part = (nn(wk[rows, :], dkt[...]) + nn(wv[rows, :], dvt[...])).astype(BF)
        if len(targets) == 1:
            targets[0][...] = part
        else:
            targets[0][...] = part[:, :half]
            targets[1][...] = part[:, half:]


def add_pair_kernel(one, two, out):
    out[...] = (one[...].astype(F32) + two[...].astype(F32)).astype(BF)


def add_halves_kernel(keep, one, two, out):
    half = one.shape[1]
    out[:, :half] = (keep[:, :half].astype(F32) + one[...].astype(F32)).astype(BF)
    out[:, half:] = (keep[:, half:].astype(F32) + two[...].astype(F32)).astype(BF)


def image_sum_kernel(keep, one, two, away, out):
    patches = out.shape[2]
    per = one.shape[1] // patches
    for b in range(out.shape[0]):
        ks = slice(b * patches, (b + 1) * patches)
        part = one if b < per else two
        ps = slice((b % per) * patches, (b % per + 1) * patches)
        out[b] = keep[:, ks].astype(F32) + part[:, ps].astype(F32) + away[:, ks].astype(F32)


def self_back_kernel(
    seqs, parts, lens, own, other, text, gain, bias, w, qkv,
    one, two, ups, *refs
):
    outs = refs[:parts]
    send, keep, low, dqkv, full, narrow, vec = refs[parts:]
    join_halves(own, other, low)
    width = w.shape[1] // 4
    grad_ctx = nn(low[...], w[:, 3 * width :]).astype(BF)
    low_masks, masks = head_masks(width, BF), head_masks(width, F32)
    rows = text.shape[0] // seqs
    for b in range(seqs):
        at = slice(b * rows, (b + 1) * rows)
        q_stack = stack_heads(qkv[at, :width], low_masks)
        keys = qkv[at, width : 2 * width]
        p = self_softmax(q_stack, keys, lens[b], rows)
        grad_stack = stack_heads(grad_ctx[at], low_masks)
        ds = score_grad(p, qkv[at, 2 * width : 3 * width], grad_stack)
        dqkv[0, at] = unstack_heads(nn(ds, keys) * SCALE, masks).astype(BF)
        dqkv[1, at] = (tn(ds, q_stack) * SCALE).astype(BF)
        dqkv[2, at] = tn(p.astype(BF), grad_stack).astype(BF)
    n, _ = norm_parts(text[...].astype(F32))
    normed = (n * gain[0:1] + bias[0:1]).astype(BF)
    for j in range(3):
        narrow[...] = tn(normed, dqkv[j])
        scatter_blocks(narrow, j * width, outs)
    narrow[...] = tn(low[...], qkv[:, 3 * width :])
    scatter_blocks(narrow, 3 * width, outs)
    part = nt(dqkv[0], w[:, :width])
    for j in (1, 2):
        part = part + nt(dqkv[j], w[:, j * width : (j + 1) * width])
    full[...] = part
    split_halves(full, send, keep)
    half = own.shape[0]
    vec[...] = jnp.zeros_like(vec)
    vec[0:1] = jnp.sum(part * n, axis=0, keepdims=True)
    vec[1:2], vec[2:3] = one[0:1], two[0:1]
    vec[3:4] = jnp.sum(part, axis=0, keepdims=True)
    vec[4:5], vec[5:6] = one[1:2], two[1:2]
    vec[6:7], vec[7:8], vec[8:9] = one[2:3], two[2:3], two[3:4]
    vec[pl.ds(9 + lax.axis_index("mp"), 1), :] = ups[...]
    send[half:] = vec[...].astype(BF)
    keep[half:] = vec[...].astype(BF)


def finish_kernel(chip, other, text, resid, gain, grad_out, vec):
    half = resid.shape[0]
    grad = chip[:half].astype(F32) + other[:half].astype(F32)
    base = text[half_rows(half), :].astype(F32)
    n, inv_std = norm_parts(base)
    grad_out[...] = resid[...] + norm_back(grad, n, inv_std, gain[0:1])
    vec[...] = (chip[half:].astype(F32) + other[half:].astype(F32)).astype(BF)


def layer_out_kernel(chip, other, hidden, out_bias, out):
    out[...] = (
        hidden[...] + (chip[...].astype(F32) + other[...].astype(F32)) + out_bias[2:3]
    ).astype(BF)


def join_both_kernel(own, other, own_low, other_low, out, out_low):
    join_halves(own, other, out)
    join_halves(own_low, other_low, out_low)


def fold_kernel(keep, other, stay, send):
    for k in range(keep.shape[0]):
        target = send if k % 2 else stay
        value = (keep[k].astype(F32) + other[k].astype(F32)).astype(target.dtype)
        if len(target.shape) == 3:
            target[k // 2] = value
        else:
            target[...] = value


def fold_self_one_kernel(keep, other, vec, vec_other, stay, send, vec_sum):
    height = keep.shape[1]
    for k in range(4):
        value = (keep[k].astype(F32) + other[k].astype(F32)).astype(BF)
        at = (k // 2) * height
        (send if k % 2 else stay)[at : at + height] = value
    total = (vec[...].astype(F32) + vec_other[...].astype(F32)).astype(BF)
    vec_sum[...] = total
    send[2 * height :] = total


def fold_self_two_kernel(keep, other, vec, stay, send, vec_sum):
    height = stay.shape[0]
    stay[...] = keep[:height].astype(F32) + other[:height].astype(F32)
    rest = slice(height, 2 * height)
    send[:height] = (keep[rest].astype(F32) + other[rest].astype(F32)).astype(BF)
    total = (vec[...].astype(F32) + other[2 * height :].astype(F32)).astype(BF)
    vec_sum[...] = total
    send[height:] = total


def vector_parts(total, gains, shifts, biases, ups):
    gains[...] = total[0:3]
    shifts[...] = total[3:6]
    biases[...] = total[6:9]
    full = total[9]
    for k in range(1, 4):
        full = jnp.where(lax.axis_index("mp") == k, total[9 + k], full)
    ups[...] = full


def vector_kernel(vec, gains, shifts, biases, ups):
    vector_parts(vec[...], gains, shifts, biases, ups)


def close_cross_kernel(*refs):
    own, other, query, keyval, out = refs
    total = own[...] + other[...].astype(F32)
    width = out.shape[0]
    query[...] = total[:, :width]
    keyval[0] = total[:, width : 2 * width]
    keyval[1] = total[:, 2 * width : 3 * width]
    out[...] = total[:, 3 * width :].T


def close_ffn_kernel(own, other, out):
    out[...] = own[...] + other[...].astype(F32)


def close_self_kernel(own, other, vec, qkv, out, gains, shifts, biases, ups):
    height = own.shape[0]
    total = own[...] + other[:height].astype(F32)
    width = out.shape[0]
    for j in range(3):
        qkv[j] = total[:, j * width : (j + 1) * width]
    out[...] = total[:, 3 * width :].T
    vector_parts(vec[...].astype(F32) + other[height:].astype(F32), gains, shifts, biases, ups)


def swap(value, axis, size, bits):
    return lax.ppermute(value, axis, [(i, i ^ bits) for i in range(size)])


def gate_all(values, *first):
    return list(lax.optimization_barrier((*values, *first)))[: len(values)]


def gate(value, *first):
    return lax.optimization_barrier((value, *first))[0]


def per_device(
    dp_size,
    mp_size,
    text_tokens,
    image_tokens,
    text_lengths,
    patch_counts,
    self_qkv,
    self_out,
    cross_query,
    cross_keyval,
    cross_out,
    mlp_up,
    mlp_down,
    norm_gain,
    norm_bias,
    out_bias,
    up_bias,
    out_grad,
):
    seqs, positions, model = text_tokens.shape
    patches = image_tokens.shape[1]
    rows = seqs * positions
    half = rows // 2
    width = cross_query.shape[1]
    hidden = mlp_up.shape[1]
    image_rows = seqs * patches
    quick = dp_size == 8
    height = model // dp_size
    parts, blocks = (2, (4, height)) if quick else (1, (1, model))

    spots = [0, 2, 4, 6, 7, 5, 3, 1]
    turns = [
        (spots[p] * mp_size + m, spots[(p + (1 if m % 2 == 0 else -1)) % 8] * mp_size + m)
        for p in range(8)
        for m in range(mp_size)
    ]

    def around(value):
        return lax.ppermute(value, ("dp", "mp"), turns)

    def pair_up(shard, name):
        return call(
            pair_kernel, name, [((2,) + shard.shape, BF)], (), (shard, core_swap(shard))
        )[0]

    def last_hop(pair, name):
        (own,) = call(take_kernel, name, [(pair.shape[1:], BF)], (), (pair,))
        return around(own)

    def collect(shard, hops, swaps=None):
        swaps = swaps or [core_swap(hop) for hop in hops[:3]]
        return [shard] + hops[:3] + swaps + [hops[3]]

    def send_blocks(outs, bits):
        return (outs[0], swap(outs[1], "dp", 8, bits)) if quick else outs

    def fold(halves, bits, name, *first):
        if not quick:
            return halves
        keep, other = halves
        count, shape = keep.shape[0] // 2, keep.shape[1:]
        kinds = [((2,) + shape, BF)] * 2 if count == 2 else [(shape, F32), (shape, BF)]
        stay, send = call(fold_kernel, name, kinds, (), (gate(keep, *first), other))
        return stay, swap(send, "dp", 8, bits)

    def whole_sum(halves):
        return lax.psum_scatter(halves[0][0], "dp", scatter_dimension=0, tiled=True).astype(F32)

    def core_swap(value):
        return swap(value, "mp", mp_size, 1)

    def level_swap(value):
        return swap(value, "mp", mp_size, 2)

    def add_pair(one, two):
        return call(add_pair_kernel, "add_pair", [(one.shape, BF)], (), (one, two))[0]

    def mp_sum(send, keep):
        chip = add_pair(keep, core_swap(send))
        return chip, level_swap(chip)

    text = text_tokens.reshape(rows, model)
    image = image_tokens.reshape(image_rows, model)
    grad = out_grad.reshape(rows, model)

    if quick:
        (self_shard,) = call(
            pack_self_kernel, "pack_self", [((height, 4 * width), BF)], (), (self_qkv, self_out)
        )
        (ffn_shard,) = call(
            pack_ffn_kernel, "pack_ffn", [((height, 2 * hidden), BF)], (), (mlp_up, mlp_down.T)
        )
        self_pair = pair_up(self_shard, "pairA")
        (cross_shard,) = call(
            pack_cross_kernel,
            "pack_cross",
            [((height, 4 * width), BF)],
            (),
            (gate(cross_query, self_pair), cross_keyval, cross_out),
        )
        self_hops = [around(self_pair)]
        cross_hops = [around(pair_up(gate(cross_shard, self_pair), "pairB"))]
        for k in range(2):
            self_hops.append(around(self_hops[-1]))
            cross_hops.append(around(cross_hops[-1]))
        self_hops.append(last_hop(self_hops[-1], "takeA"))
        cross_hops.append(last_hop(cross_hops[-1], "takeB"))
        self_swaps = [core_swap(hop) for hop in self_hops[:3]]
        self_pieces = collect(self_shard, self_hops, self_swaps)
        cross_pieces = collect(cross_shard, cross_hops)
        ffn_pair = pair_up(gate(ffn_shard, self_hops[0]), "pairF")
        ffn_hops = [around(gate(ffn_pair, self_hops[1]))]
        ffn_hops.append(around(ffn_hops[0]))
        text_in = gate(text, ffn_hops[0], cross_hops[3])
    else:
        gather = lambda shard: [lax.all_gather(shard, "dp", axis=0, tiled=True)]
        self_pieces = gather(
            jnp.concatenate([self_qkv[0], self_qkv[1], self_qkv[2], self_out.T], 1)
        )
        cross_pieces = gather(
            jnp.concatenate([cross_query, cross_keyval[0], cross_keyval[1], cross_out.T], 1)
        )
        text_in = text
        ffn_pieces = gather(jnp.concatenate([mlp_up, mlp_down.T], 1))

    square = ((model, width), BF)
    narrow = ((rows, width), BF)
    wide = ((rows, model), BF)
    halves = [((half, model), BF)] * 2
    half_f32 = ((half, model), F32)
    half_low = ((half, model), BF)
    heads = width // HEAD_DIM
    full = pltpu.VMEM((rows, model), F32)

    vmem = pl.BlockSpec(memory_space=pltpu.VMEM)
    smem = pl.BlockSpec(memory_space=pltpu.SMEM)
    hbm = pl.BlockSpec(memory_space=pltpu.HBM)
    w_self, saved, send, keep = pl.pallas_call(
        functools.partial(self_forward_kernel, len(self_pieces), seqs),
        out_shape=[
            jax.ShapeDtypeStruct((model, 4 * width), BF),
            jax.ShapeDtypeStruct((rows, 4 * width), BF),
            jax.ShapeDtypeStruct((half, model), BF),
            jax.ShapeDtypeStruct((half, model), BF),
        ],
        in_specs=[smem] + [vmem] * (3 + len(self_pieces)),
        out_specs=[hbm, hbm, vmem, vmem],
        scratch_shapes=[
            pltpu.VMEM((model, 4 * width), BF),
            pltpu.VMEM((rows, 4 * width), BF),
            full,
            pltpu.SemaphoreType.DMA((2,)),
        ],
        compiler_params=pltpu.CompilerParams(vmem_limit_bytes=VMEM_LIMIT),
        cost_estimate=COST,
        name="self_forward",
    )(text_lengths, text_in, norm_gain, norm_bias, *self_pieces)
    chip, other = mp_sum(send, keep)

    whole = lambda shape: pl.BlockSpec(shape, lambda b: (0,) * len(shape))
    per_seq = lambda b: (b, 0)
    cq, ck, cv, co, keys, values = pl.pallas_call(
        functools.partial(keyval_kernel, len(cross_pieces)),
        grid=(seqs,),
        out_shape=[jax.ShapeDtypeStruct((model, width), BF)] * 4
        + [jax.ShapeDtypeStruct((image_rows, width), BF)] * 2,
        in_specs=[pl.BlockSpec((patches, model), per_seq)]
        + [whole(piece.shape) for piece in cross_pieces],
        out_specs=[whole((model, width))] * 4 + [pl.BlockSpec((patches, width), per_seq)] * 2,
        compiler_params=pltpu.CompilerParams(vmem_limit_bytes=VMEM_LIMIT),
        cost_estimate=COST,
        name="keyval",
    )(image, *cross_pieces)

    hidden_one, normed_half = call(
        functools.partial(norm_kernel, 0, True),
        "norm_mid",
        [half_f32, half_low],
        (),
        (gate(chip, keys, ffn_hops[1]) if quick else chip, other, text, out_bias, norm_gain, norm_bias),
    )
    if quick:
        ffn_hops.append(around(gate(ffn_hops[1], normed_half)))
    normed_mid, xq, cross_prob, cross_ctx, send, keep = call(
        functools.partial(cross_forward_kernel, seqs),
        "cross_forward",
        [wide, narrow, ((seqs, heads * positions, patches), F32), narrow] + halves,
        (patch_counts,),
        (normed_half, core_swap(normed_half), cq, co, keys, values),
        [full],
        flops=2 * rows * model * width * 2,
    )
    chip, other = mp_sum(send, keep)
    if quick:
        ffn_hops.append(last_hop(gate(ffn_hops[2], chip), "takeF"))
        ffn_pieces = collect(ffn_shard, ffn_hops)
    w_up, w_down, grad_act = call(
        functools.partial(ffn_ready_kernel, len(ffn_pieces)),
        "ffn_ready",
        [((model, hidden), BF)] * 2 + [((rows, hidden), F32)],
        (),
        (grad, *ffn_pieces),
        flops=2 * rows * model * hidden,
    )
    hidden_two, normed_half = call(
        functools.partial(norm_kernel, 1, False),
        "norm_ffn",
        [half_f32, half_low],
        (),
        (chip, other, hidden_one, out_bias, norm_gain, norm_bias),
    )
    (normed_ffn, act, grad_low, up_sum, send, keep, out_send, out_keep) = call(
        ffn_kernel,
        "ffn",
        [wide, ((rows, hidden), BF), ((rows, hidden), BF), ((1, hidden), F32)] + halves + halves,
        (),
        (
            normed_half,
            core_swap(normed_half),
            w_up,
            w_down,
            grad_act,
            up_bias.reshape(1, hidden),
        ),
        [full],
        flops=2 * rows * model * hidden * 3,
    )
    chip, other = mp_sum(send, keep)

    ffn_blocks = call(
        functools.partial(ffn_weight_kernel, parts),
        "ffn_weights",
        [(blocks + (hidden,), BF)] * (2 * parts),
        (),
        (normed_ffn, grad_low, grad, act),
        [pltpu.VMEM((model, hidden), F32)],
        flops=2 * rows * model * hidden * 2,
    )
    up_sums = send_blocks(ffn_blocks[:parts], 2)
    down_sums = send_blocks(ffn_blocks[parts:], 1)
    vec_shape = ((8, model), F32)
    grad_two, low_half, vec_two = call(
        functools.partial(norm_back_kernel, 2, True),
        "norm_back_ffn",
        [half_f32, half_low, vec_shape],
        (),
        (gate(chip, *ffn_blocks), other, hidden_two, grad, norm_gain),
    )
    turned = ((width, image_rows), BF)
    grad_two_low, dq, dkt, dvt, send, keep = call(
        functools.partial(cross_back_kernel, seqs),
        "cross_back",
        [wide, narrow, turned, turned] + halves,
        (),
        (low_half, core_swap(low_half), cq, co, keys, values, xq, cross_prob),
        [full],
        flops=2 * rows * model * width * 2,
    )
    turned_half = ((width, image_rows // 2), BF)
    away_one, away_two, own_one, own_two, keep_away, keep_own = call(
        image_part_kernel,
        "image_part",
        [turned_half] * 4 + [turned] * 2,
        (),
        (dkt, dvt, ck, cv),
    )
    chip, other = mp_sum(send, gate(keep, keep_own))
    up_sums = fold(up_sums, 4, "fold_up", chip)
    down_sums = fold(down_sums, 2, "fold_down", up_sums[0])
    cross_blocks = call(
        functools.partial(cross_weight_kernel, parts),
        "cross_weights",
        [(blocks + (4 * width,), BF)] * parts,
        (),
        (image, gate(dkt, down_sums[0]), dvt, normed_mid, dq, grad_two_low, cross_ctx),
        [pltpu.VMEM((model, width), F32)],
        flops=2 * image_rows * model * width * 2,
    )
    cross_sums = send_blocks(cross_blocks, 1)
    grad_one, low_half, vec_one = call(
        functools.partial(norm_back_kernel, 1, False),
        "norm_back_mid",
        [half_f32, half_low, vec_shape],
        (),
        (gate(chip, *cross_blocks), other, hidden_one, grad_two, norm_gain),
    )
    (chip_away,) = call(
        add_halves_kernel,
        "image_chip",
        [turned],
        (),
        (gate(keep_away, low_half), core_swap(away_one), core_swap(away_two)),
    )
    tall = ((half + 16, model), BF)
    self_back = call(
        functools.partial(self_back_kernel, seqs, parts),
        "self_back",
        [(blocks + (4 * width,), BF)] * parts + [tall] * 2,
        (text_lengths,),
        (
            low_half,
            core_swap(low_half),
            gate(text, chip_away),
            norm_gain,
            norm_bias,
            w_self,
            saved,
            vec_one,
            vec_two,
            up_sum,
        ),
        [
            pltpu.VMEM((rows, model), BF),
            pltpu.VMEM((3, rows, width), BF),
            full,
            pltpu.VMEM((model, width), F32),
            pltpu.VMEM((16, model), F32),
        ],
    )
    self_blocks, (send, keep) = self_back[:parts], self_back[parts:]
    self_sums = send_blocks(self_blocks, 1)
    chip, other = mp_sum(send, keep)
    text_half, vec = call(
        finish_kernel,
        "finish",
        [half_f32, ((16, model), BF)],
        (),
        (chip, other, text, grad_one, norm_gain),
    )
    image_away = level_swap(gate(chip_away, vec))
    cross_sums = fold(cross_sums, 4, "fold_cross", vec)
    down_sums = fold(down_sums, 4, "fold_down", cross_sums[0])
    up_sums = fold(up_sums, 1, "fold_up", down_sums[0])
    out_chip = add_pair(gate(out_keep, up_sums[0]), core_swap(out_send))
    out_other = level_swap(out_chip)
    if quick:
        low_rows = lambda count: ((count, 4 * width), BF)
        near, send, vec = call(
            fold_self_one_kernel,
            "fold_self",
            [low_rows(2 * height), low_rows(2 * height + 16), low_rows(16)],
            (),
            (gate(self_sums[0], out_chip), self_sums[1], vec, swap(vec, "dp", 8, 1)),
        )
        self_sums = near, swap(send, "dp", 8, 2)
        cross_sums = gate(cross_sums[0], near), cross_sums[1]
    cross_sums = fold(cross_sums, 2, "fold_cross", *self_sums[:1])
    if quick:
        close = lambda sums, first, name: call(
            close_ffn_kernel, name, [((height, hidden), F32)], (), (gate(sums[0], first), sums[1])
        )[0]
        down_turned = close(down_sums, cross_sums[0], "close_down")
        up_grad = close(up_sums, down_turned, "close_up")
        down_grad = down_turned.T
        join_first = gate(text_half, up_grad)
    else:
        join_first = text_half
    (out_half,) = call(
        layer_out_kernel,
        "layer_out",
        [half_low],
        (),
        (gate(out_chip, join_first), out_other, hidden_two, out_bias),
    )
    text_grad, layer_out = call(
        join_both_kernel,
        "join",
        [((rows, model), F32), wide],
        (),
        (join_first, core_swap(text_half), out_half, core_swap(out_half)),
    )
    if quick:
        near, send, vec = call(
            fold_self_two_kernel,
            "fold_self",
            [((height, 4 * width), F32), low_rows(height + 16), low_rows(16)],
            (),
            (gate(self_sums[0], text_grad), self_sums[1], vec),
        )
        self_sums = near, swap(send, "dp", 8, 4)
    (image_grad,) = call(
        image_sum_kernel,
        "image_sum",
        [((seqs, width, patches), F32)],
        (),
        (gate(keep_own, near if quick else text_grad), core_swap(own_one), core_swap(own_two), image_away),
    )
    if quick:
        query_grad, keyval_grad, cross_out_grad = call(
            close_cross_kernel,
            "close_cross",
            [((height, width), F32), ((2, height, width), F32), ((width, height), F32)],
            (),
            (gate(cross_sums[0], image_grad), cross_sums[1]),
        )
    vec_outs = [((3, model), F32)] * 3 + [((hidden,), F32)]
    if quick:
        qkv_grad, self_out_grad, gains, shifts, biases, ups = call(
            close_self_kernel,
            "close_self",
            [((3, height, width), F32), ((width, height), F32)] + vec_outs,
            (),
            (gate(self_sums[0], query_grad), self_sums[1], vec),
        )
    else:
        gains, shifts, biases, ups = call(
            vector_kernel, "close_vector", vec_outs, (), (lax.psum(vec.astype(F32), "dp"),)
        )
        total = whole_sum(self_sums)
        qkv_grad = jnp.stack([total[:, j * width : (j + 1) * width] for j in range(3)])
        self_out_grad = total[:, 3 * width :].T
        total = whole_sum(cross_sums)
        query_grad = total[:, :width]
        keyval_grad = jnp.stack([total[:, j * width : (j + 1) * width] for j in (1, 2)])
        cross_out_grad = total[:, 3 * width :].T
        up_grad, down_grad = whole_sum(up_sums), whole_sum(down_sums).T
    return (
        layer_out.reshape(seqs, positions, model),
        text_grad.reshape(seqs, positions, model),
        image_grad.transpose(0, 2, 1),
        qkv_grad,
        self_out_grad,
        query_grad,
        keyval_grad,
        cross_out_grad,
        up_grad,
        down_grad,
        gains,
        shifts,
        biases,
        ups.reshape(hidden),
    )


def solution(mesh):
    placed = (
        P("dp", None, None),
        P("dp", None, None),
        P("dp"),
        P("dp"),
        P(None, "dp", "mp"),
        P("mp", "dp"),
        P("dp", "mp"),
        P(None, "dp", "mp"),
        P("mp", "dp"),
        P("dp", "mp"),
        P("mp", "dp"),
        P(),
        P(),
        P(),
        P("mp"),
        P("dp", None, None),
    )
    return jax.shard_map(
        functools.partial(per_device, mesh.shape["dp"], mesh.shape["mp"]),
        mesh=mesh,
        in_specs=placed,
        out_specs=(
            P("dp", None, None),
            P("dp", None, None),
            P("dp", None, "mp"),
            P(None, "dp", "mp"),
            P("mp", "dp"),
            P("dp", "mp"),
            P(None, "dp", "mp"),
            P("mp", "dp"),
            P("dp", "mp"),
            P("mp", "dp"),
            P(),
            P(),
            P(),
            P("mp"),
        ),
        check_vma=False,
    )
```
